512 devices in a mesh: tg: 8 (over x, core), pw: 64 (over y, z).
Axes of the slice: x: 4, y: 8, z: 8, core: 2. Of those that a mesh axis runs over, the one named last changes fastest.
Arguments:
- orbital_coefficients: float32 [8, 2, 4096, 192], P(None, None, ('tg', 'pw')), may hold values from -6 to 6
- potential: float32 [192, 36864], P('pw'), may hold values from -2 to 2
- line_lateral_place: int32 [36864], replicated, may hold values from 0 to 36863, as said below
- stick_count: int32 [512], replicated, may hold values from 1 to 8, 2560 in all
- proj_atom: int32 [2048], replicated, may hold values from 0 to 511
- atom_pos: float32 [3, 512], replicated, may hold values from 0 to 1
- proj_radius: float32 [2048], replicated, may hold values from 2 to 40
- proj_diag: float32 [2048], replicated, may hold values from 1 to 10
- ionic_pseudo_dij: float32 [2048], replicated, may hold values from -1 to 1
Outputs:
- hpsi: float32 [8, 2, 4096, 192], P(None, None, ('tg', 'pw'))
The draws below stay inside these ranges and needn't reach their ends.
Inputs may be any that keep to these rules, and one draw needn't show every extreme that they name: line_lateral_place holds 36864 distinct column positions; the first 4096 belong to the stick slots in order and are columns with gx^2 + gy^2 <= 48^2 in random order, or, where that disc holds fewer than 4096 columns, all of them followed by the nearest columns outside it. stick_count[k] counts the live slots among the 8 slots k * 8 and on; the live ones come first; some block is full.
All inputs are finite; a program needn't handle non-finite values.
Results may differ from the reference program's by a relative error of at most 0.0003.
Values sent between devices are 32-bit elements; how exact they have to be, the bound alone decides.
No kernel may reach another device: no remote copies, remote signals or barrier semaphores. Data moves between devices by JAX's collectives and lax.ppermute only.
A program may use at most 128 MiB of HBM per device.

```python
import math
import jax
import jax.numpy as jnp
import numpy as np
from jax import lax

GRID_EDGE = 192
NPROJ = 2048
NATOM = 512
DEVICE_LINES = 8
ORBITAL_COUNT = 8
LINE_CAPACITY = 4096
DEVICES = 512


def draw_line_lateral_place(key, part):
    key = jax.random.fold_in(key, 11)
    total = GRID_EDGE * GRID_EDGE
    cells = jnp.arange(total, dtype=jnp.int32)
    half = GRID_EDGE // 2
    gx = jnp.where(cells // GRID_EDGE < half, cells // GRID_EDGE, cells // GRID_EDGE - GRID_EDGE)
    gy = jnp.where(cells % GRID_EDGE < half, cells % GRID_EDGE, cells % GRID_EDGE - GRID_EDGE)
    radius_sq = gx * gx + gy * gy
    limit = GRID_EDGE // 4 * (GRID_EDGE // 4)
    order_key = jnp.where(radius_sq <= limit, 0, radius_sq).astype(jnp.int32)
    shuffled = jax.random.permutation(key, cells)
    ranked = jnp.argsort(order_key[shuffled], stable=True)
    return shuffled[ranked].astype(jnp.int32)


def set_ends(drawn, rng, low, top_value):
    shape = drawn.shape
    place = [jax.random.randint(jax.random.fold_in(rng, axis), (), 0, shape[axis]) for axis in range(len(shape))]
    drawn = drawn.at[tuple(place)].set(low)
    longest = shape.index(max(shape))
    place[longest] = (place[longest] + 1) % shape[longest]
    return drawn.at[tuple(place)].set(top_value)


def block_scale(stream_key, shape, shards, smallest, largest):
    loudness, own = 1.0, jax.random.fold_in(stream_key, 6)
    for position, parts in shards:
        draws = jnp.exp(jax.random.uniform(jax.random.fold_in(own, position), (parts,), jnp.float32, smallest / len(shards), largest / len(shards)))
        loudness = loudness * jnp.repeat(draws, shape[position] // parts).reshape([-1 if axis == position else 1 for axis in range(len(shape))])
    return loudness


def length_profile(number_of, total, reach, skew):
    portions = [(1 << 20) // math.isqrt(standing ** skew) + 1 for standing in range(2, number_of + 1)]
    spare, counts = total - reach - (number_of - 1), [1] * (number_of - 1)
    while spare > 0:
        movable = [i for i in range(number_of - 1) if counts[i] < reach]
        mass, left = sum([portions[i] for i in movable]), spare
        for i in movable:
            addition = min(reach - counts[i], max(1, left * portions[i] // mass), spare)
            counts[i] = counts[i] + addition
            spare = spare - addition
    return np.array([reach] + counts)


def uneven_parts(stream_key, amount, total, reach, slope):
    if amount == 2:
        one = jax.random.randint(stream_key, (), max(1, total - reach), min(reach, total - 1) + 1)
        return jnp.stack([one, total - one])
    sizes = jnp.asarray(length_profile(amount, total, reach, slope), jnp.int32)
    twos = (amount - 1) // 2
    giver, receiver = sizes[1:1 + 2 * twos:2], sizes[2:2 + 2 * twos:2]
    margin = jnp.minimum(giver - 1, reach - receiver)
    moved = jax.random.randint(jax.random.fold_in(stream_key, 1), (twos,), 0, 1 << 20) % (margin + 1)
    sizes = sizes.at[1:1 + 2 * twos:2].set(giver - moved).at[2:2 + 2 * twos:2].set(receiver + moved)
    return sizes[jax.random.permutation(jax.random.fold_in(stream_key, 2), amount)]


def noise(rng, shape, scale, most, split=(), kind=jnp.bfloat16):
    entries = jax.random.normal(rng, shape, jnp.float32) * scale
    if len(split) > 0:
        entries = block_scale(rng, shape, split, -0.22, 0.18) * entries
    return jnp.clip(entries, min=-most, max=most).astype(kind)


def setup_inputs(seed: int = 0) -> dict:
    keys = jax.random.split(jax.random.key(seed), 10)
    orbital_coefficients = noise(keys[0], (ORBITAL_COUNT, 2, LINE_CAPACITY, GRID_EDGE), 1.0, 6.0, ((2, 512),), jnp.float32)
    potential = jnp.clip(jax.random.uniform(keys[1], (GRID_EDGE, GRID_EDGE * GRID_EDGE), jnp.float32, -2.0, 2.0) * block_scale(keys[1], (GRID_EDGE, GRID_EDGE * GRID_EDGE), ((0, 64),), -0.4, 0.0), -2.0, 2.0)
    line_lateral_place = draw_line_lateral_place(jax.random.fold_in(keys[9], 71), 0)
    stick_count = uneven_parts(keys[3], DEVICES, DEVICES * DEVICE_LINES * 5 // 8, DEVICE_LINES, 2).astype(jnp.int32)
    proj_atom = set_ends(jax.random.randint(keys[4], (NPROJ,), 0, NATOM), jax.random.fold_in(keys[4], 1), 0, NATOM - 1).astype(jnp.int32)
    atom_pos = jnp.clip(jax.random.uniform(keys[5], (3, NATOM), jnp.float32, 0.0, 1.0), 0.0, 1.0)
    proj_radius = jnp.clip(jnp.exp(jax.random.uniform(keys[6], (NPROJ,), jnp.float32, math.log(2.0), math.log(40.0))), 2.0, 40.0)
    proj_diag = jnp.clip(jnp.exp(jax.random.uniform(keys[7], (NPROJ,), jnp.float32, math.log(1.0), math.log(10.0))), 1.0, 10.0)
    ionic_pseudo_dij = jnp.clip(jax.random.uniform(keys[8], (NPROJ,), jnp.float32, -1.0, 1.0), -1.0, 1.0)
    return dict(orbital_coefficients=orbital_coefficients, potential=potential, line_lateral_place=line_lateral_place, stick_count=stick_count, proj_atom=proj_atom, atom_pos=atom_pos, proj_radius=proj_radius, proj_diag=proj_diag, ionic_pseudo_dij=ionic_pseudo_dij)


HIGHEST_STATE = lax.Precision.HIGHEST
kinetic_scale = 2.0

def signed_index(index, count):
    return jnp.where(index < count // 2, index, index - count)

def projector_factors(vertical_lines, atom_pos, proj_atom, proj_radius, grid_edge_length):
    natom = atom_pos.shape[1]
    membership_mask = (proj_atom[:, None] == jnp.arange(natom, dtype=jnp.int32)[None, :]).astype(atom_pos.dtype)
    places = jnp.dot(membership_mask, atom_pos.T, precision=HIGHEST_STATE)
    wavenumber_first_cartesian = signed_index(vertical_lines // grid_edge_length, grid_edge_length).astype(atom_pos.dtype)
    freq_y = signed_index(vertical_lines % grid_edge_length, grid_edge_length).astype(atom_pos.dtype)
    freq_z = signed_index(jnp.arange(grid_edge_length, dtype=jnp.int32), grid_edge_length).astype(atom_pos.dtype)
    spread = proj_radius[:, None] / (grid_edge_length * grid_edge_length)
    turns_xy = wavenumber_first_cartesian[None, :] * places[:, 0:1] + freq_y[None, :] * places[:, 1:2]
    turns_xy = turns_xy - jnp.floor(turns_xy)
    amp_xy = jnp.exp(-spread * (wavenumber_first_cartesian * wavenumber_first_cartesian + freq_y * freq_y)[None, :])
    turns_z = freq_z[None, :] * places[:, 2:3]
    turns_z = turns_z - jnp.floor(turns_z)
    amp_z = jnp.exp(-spread * (freq_z * freq_z)[None, :])
    angle_xy = 2.0 * math.pi * turns_xy
    angle_z = 2.0 * math.pi * turns_z
    return ((amp_xy * jnp.cos(angle_xy), -amp_xy * jnp.sin(angle_xy)), (amp_z * jnp.cos(angle_z), -amp_z * jnp.sin(angle_z)), membership_mask)

def project(coeff, a_re, a_im, b_re, b_im):
    with_re = jnp.einsum('pz,bcsz->pbcs', b_re, coeff, precision=HIGHEST_STATE)
    with_im = jnp.einsum('pz,bcsz->pbcs', b_im, coeff, precision=HIGHEST_STATE)
    y_re = with_re[:, :, 0] + with_im[:, :, 1]
    y_im = with_re[:, :, 1] - with_im[:, :, 0]
    part_re = lax.optimization_barrier(jnp.sum(a_re[:, None, :] * y_re + a_im[:, None, :] * y_im, axis=2))
    part_im = lax.optimization_barrier(jnp.sum(a_re[:, None, :] * y_im - a_im[:, None, :] * y_re, axis=2))
    return jnp.stack([part_re, part_im])

def couple(beta_coefficient_product, membership_mask, proj_diag, ionic_pseudo_dij):
    multiplied_result = beta_coefficient_product * ionic_pseudo_dij[None, :, None]
    per_ion_loop = jnp.einsum('zm,yzs->yms', membership_mask, multiplied_result, precision=HIGHEST_STATE)
    common_between = jnp.einsum('hl,slz->shz', membership_mask, per_ion_loop, precision=HIGHEST_STATE)
    return beta_coefficient_product * proj_diag[None, :, None] + ionic_pseudo_dij[None, :, None] * common_between

def expand(quadrature_multipliers, a_re, a_im, b_re, b_im):
    z_re = a_re[:, None, :] * quadrature_multipliers[0][:, :, None] - a_im[:, None, :] * quadrature_multipliers[1][:, :, None]
    z_im = a_re[:, None, :] * quadrature_multipliers[1][:, :, None] + a_im[:, None, :] * quadrature_multipliers[0][:, :, None]
    out_re = jnp.einsum('pz,pbs->bsz', b_re, z_re, precision=HIGHEST_STATE) - jnp.einsum('pz,pbs->bsz', b_im, z_im, precision=HIGHEST_STATE)
    out_im = jnp.einsum('pz,pbs->bsz', b_re, z_im, precision=HIGHEST_STATE) + jnp.einsum('pz,pbs->bsz', b_im, z_re, precision=HIGHEST_STATE)
    return jnp.stack([out_re, out_im], axis=1)

def local_band(coeff, field_pot, vertical_lines, grid_edge_length):
    values = lax.complex(coeff[0], coeff[1])
    boxed = jnp.zeros((grid_edge_length * grid_edge_length, grid_edge_length), values.dtype).at[vertical_lines].set(values).reshape(grid_edge_length, grid_edge_length, grid_edge_length)
    field = jnp.fft.ifftn(boxed)
    applied = jnp.fft.fftn(field * field_pot)
    picked = applied.reshape(grid_edge_length * grid_edge_length, grid_edge_length)[vertical_lines]
    return jnp.stack([jnp.real(picked), jnp.imag(picked)])

def reference(orbital_coefficients, potential, line_lateral_place, stick_count, proj_atom, atom_pos, proj_radius, proj_diag, ionic_pseudo_dij):
    grid_edge_length = GRID_EDGE
    vertical_lines = line_lateral_place[:LINE_CAPACITY]
    inside_range = jnp.arange(LINE_CAPACITY, dtype=jnp.int32) % DEVICE_LINES
    live = (inside_range < jnp.repeat(stick_count, DEVICE_LINES)).astype(orbital_coefficients.dtype)
    coeff = orbital_coefficients * live[None, None, :, None]
    cube = potential.reshape(grid_edge_length, grid_edge_length, grid_edge_length)
    field_pot = jnp.transpose(cube, (1, 2, 0))
    local = lax.map(lambda band: local_band(band, field_pot, vertical_lines, grid_edge_length), coeff)
    (a_re, a_im), (b_re, b_im), membership_mask = projector_factors(vertical_lines, atom_pos, proj_atom, proj_radius, grid_edge_length)
    running_accumulations = lax.map(lambda band: project(band[None], a_re, a_im, b_re, b_im)[:, :, 0], coeff)
    beta_coefficient_product = jnp.transpose(running_accumulations, (1, 2, 0)) / math.sqrt(LINE_CAPACITY * GRID_EDGE)
    quadrature_multipliers = couple(beta_coefficient_product, membership_mask, proj_diag, ionic_pseudo_dij)
    vnl = lax.map(lambda wband: expand(wband[:, :, None], a_re, a_im, b_re, b_im)[0], jnp.transpose(quadrature_multipliers, (2, 0, 1)))
    vnl = vnl / math.sqrt(NPROJ)
    wavenumber_first_cartesian = signed_index(vertical_lines // grid_edge_length, grid_edge_length).astype(orbital_coefficients.dtype)
    freq_y = signed_index(vertical_lines % grid_edge_length, grid_edge_length).astype(orbital_coefficients.dtype)
    freq_z = signed_index(jnp.arange(grid_edge_length, dtype=jnp.int32), grid_edge_length).astype(orbital_coefficients.dtype)
    q_two = ((wavenumber_first_cartesian * wavenumber_first_cartesian + freq_y * freq_y)[:, None] + (freq_z * freq_z)[None, :]) / (grid_edge_length * grid_edge_length)
    kinetic = kinetic_scale * q_two[None, None] * coeff
    return (kinetic + local + vnl) * live[None, None, :, None]
```

```python
import math

import jax
import jax.numpy as jnp
import numpy as np
from jax import lax
from jax.experimental import pallas as pl
from jax.experimental.pallas import tpu as pltpu
from jax.sharding import PartitionSpec as P

EDGE = 192
TEAMS = 8
SHEETS = 64
DEPTH = 3
ROWS = DEPTH + 1
LINES = 8
STICKS = TEAMS * LINES
NPROJ = 2048
NATOM = 512
CUT = 48
HALF_ROWS = 64
CHUNK = 512
CHUNKS = SHEETS * STICKS // CHUNK
PCHUNK = 256
BLOCKS = NPROJ // 128

F32 = jnp.float32
BF16 = jnp.bfloat16

NN = (((1,), (0,)), ((), ()))
NT = (((1,), (1,)), ((), ()))


def split_table(table):
    high = table.astype(np.float32).astype(jnp.bfloat16)
    low = (table - high.astype(np.float64)).astype(np.float32).astype(jnp.bfloat16)
    return high, low


def depth_table():
    steps = np.arange(EDGE)
    planes = steps.reshape(SHEETS, DEPTH).T.reshape(-1)
    turns = (planes[:, None] * steps[None, :] % EDGE) * (2.0 * math.pi / EDGE)
    return np.concatenate([np.cos(turns), np.sin(turns)], axis=0)


def column_phase(freqs, valid):
    turns = (freqs[:, None] * np.arange(EDGE)[None, :] % EDGE) * (2.0 * math.pi / EDGE)
    keep = valid[:, None].astype(np.float64)
    return np.cos(turns) * keep, np.sin(turns) * keep


def lateral_tables():
    spot = np.arange(2 * HALF_ROWS)
    y_cos, y_sin = column_phase(spot - CUT, spot <= 2 * CUT)
    pad = ((0, 0), (0, 256 - EDGE))
    y_cos, y_sin = np.pad(y_cos, pad), np.pad(y_sin, pad)
    y_inverse = np.block([[y_cos, y_sin], [-y_sin, y_cos]])
    x_spot = 2 * (spot % HALF_ROWS) + spot // HALF_ROWS
    x_cos, x_sin = column_phase(x_spot - CUT, x_spot <= 2 * CUT)
    x_forward = np.block([[x_cos, x_sin], [-x_sin, x_cos]])
    return y_inverse, x_forward.T, x_forward, y_inverse.T


def split(value):
    high = value.astype(BF16)
    return high, (value - high.astype(F32)).astype(BF16)


def mul(left, right, form):
    return lax.dot_general(left, right, form, preferred_element_type=F32)


def dot3(left, right, form):
    return mul(left[0], right[0], form) + mul(left[0], right[1], form) + mul(left[1], right[0], form)


def lateral_split(cols):
    x = (cols * 43691) >> 23
    y = cols - x * EDGE
    x = jnp.where(x < EDGE // 2, x, x - EDGE)
    y = jnp.where(y < EDGE // 2, y, y - EDGE)
    return x, y


def sincos_turns(turns):
    quarter = turns * 4.0
    near = jnp.floor(quarter + 0.5)
    x = (quarter - near) * (0.5 * math.pi)
    which = near.astype(jnp.int32) & 3
    xx = x * x
    sine = x * (1.0 + xx * (-1.0 / 6 + xx * (1.0 / 120 + xx * (-1.0 / 5040 + xx * (1.0 / 362880)))))
    cosine = 1.0 + xx * (-0.5 + xx * (1.0 / 24 + xx * (-1.0 / 720 + xx * (1.0 / 40320))))
    odd = (which & 1) == 1
    c = jnp.where(odd, sine, cosine)
    s = jnp.where(odd, cosine, sine)
    return jnp.where(((which + 1) & 2) == 2, -c, c), jnp.where((which & 2) == 2, -s, s)


def own_lateral(cols_ref, sheet):
    row = cols_ref[pl.ds(sheet, 1), :]
    x, y = lateral_split(row)
    eye = lax.broadcasted_iota(jnp.int32, (STICKS, STICKS), 0) == lax.broadcasted_iota(
        jnp.int32, (STICKS, STICKS), 1
    )

    def upright(value):
        wide = jnp.broadcast_to(value.astype(F32), (STICKS, STICKS))
        return jnp.sum(jnp.where(eye, wide, 0.0), axis=1, keepdims=True)

    return upright(x), upright(y)


def live_column(counts_ref, sheet, team):
    line = lax.broadcasted_iota(jnp.int32, (LINES, EDGE), 0)
    return line < counts_ref[team * SHEETS + sheet]


def live_sticks(sticks_ref, counts_ref, sheet):
    rows = []
    for part in range(2):
        for team in range(TEAMS):
            live = live_column(counts_ref, sheet, team)
            rows.append(jnp.where(live, sticks_ref[team, part], 0.0))
    return jnp.concatenate(rows, axis=0)


def table_kernel(sheet_ref, cols_ref, atom_ref, pos_ref, radius_ref, a_ref, bh_ref, bl_ref, mask_ref):
    sheet = sheet_ref[0]
    gx, gy = own_lateral(cols_ref, sheet)
    gxy = gx * gx + gy * gy
    pos = pos_ref[...]
    first = pos.astype(BF16).astype(F32)
    second = (pos - first).astype(BF16).astype(F32)
    third = (pos - first - second).astype(BF16).astype(F32)
    line = lax.broadcasted_iota(jnp.int32, (16, NATOM), 0)
    rows = jnp.zeros((16, NATOM), F32)
    for step, piece in enumerate((first, second, third)):
        for axis in range(3):
            rows = jnp.where(line == 3 * step + axis, piece[axis : axis + 1, :], rows)
    rows = rows.astype(BF16)
    low_g = lax.broadcasted_iota(jnp.int32, (8, PCHUNK), 0).astype(F32)
    for at in range(0, NPROJ, PCHUNK):
        here = slice(at, at + PCHUNK)
        atoms = lax.broadcasted_iota(jnp.int32, (NATOM, PCHUNK), 0)
        member = jnp.where(atoms == atom_ref[:, here], 1.0, 0.0).astype(BF16)
        mask_ref[:, here] = member
        placed = mul(rows, member, NN)
        tx, ty, tz = (
            placed[axis : axis + 1] + placed[3 + axis : 4 + axis] + placed[6 + axis : 7 + axis]
            for axis in range(3)
        )
        spread = radius_ref[:, here] / (EDGE * EDGE)
        cosine, sine = sincos_turns(gx * tx + gy * ty)
        amp = jnp.exp(-spread * gxy)
        a_ref[:STICKS, here] = amp * cosine
        a_ref[STICKS:, here] = -amp * sine
        low_c, low_s = sincos_turns(low_g * tz)
        for bank in range(3):
            high_g = (
                lax.broadcasted_iota(jnp.int32, (8, PCHUNK), 0) + bank * 8
            ) * 8
            high_g = jnp.where(high_g < EDGE // 2, high_g, high_g - EDGE).astype(F32)
            high_c, high_s = sincos_turns(high_g * tz)
            for pair in range(4):
                re_rows, im_rows = [], []
                for inner in range(2):
                    row = pair * 2 + inner
                    hc, hs = high_c[row : row + 1], high_s[row : row + 1]
                    first_g = (bank * 8 + row) * 8
                    first_g = first_g if first_g < EDGE // 2 else first_g - EDGE
                    g = low_g + float(first_g)
                    amp_z = jnp.exp(-spread * (g * g))
                    re_rows.append(amp_z * (hc * low_c - hs * low_s))
                    im_rows.append(-amp_z * (hs * low_c + hc * low_s))
                z = (bank * 8 + pair * 2) * 8
                high, low = split(jnp.concatenate(re_rows, axis=0))
                bh_ref[z : z + 16, here] = high
                bl_ref[z : z + 16, here] = low
                high, low = split(jnp.concatenate(im_rows, axis=0))
                bh_ref[EDGE + z : EDGE + z + 16, here] = high
                bl_ref[EDGE + z : EDGE + z + 16, here] = low


def rows_of(re, im):
    re_high = re.astype(BF16).astype(F32)
    im_high = im.astype(BF16).astype(F32)
    line = lax.broadcasted_iota(jnp.int32, (16, re.shape[1]), 0)
    rows = jnp.where(line == 0, re_high, 0.0)
    rows = jnp.where(line == 1, im_high, rows)
    rows = jnp.where(line == 2, re - re_high, rows)
    return jnp.where(line == 3, im - im_high, rows).astype(BF16)


def every(start):
    return pl.ds(start, SHEETS, stride=ROWS)


def project_kernel(
    sheet_ref, counts_ref, sticks_ref, th_ref, tl_ref, a_ref, bh_ref, bl_ref, mask_ref, diag_ref, dij_ref,
    out_ref, becp_ref,
):
    coeff = split(live_sticks(sticks_ref, counts_ref, sheet_ref[0]))
    both = dot3((th_ref[...], tl_ref[...]), coeff, NT)
    with_cos, with_sin = both[:EDGE], both[EDGE:]
    by_depth = with_cos + jnp.concatenate([-with_sin[:, STICKS:], with_sin[:, :STICKS]], axis=1)
    for plane in range(DEPTH):
        out_ref[every(plane), :] = by_depth[plane * SHEETS : (plane + 1) * SHEETS]
    out_ref[every(DEPTH), :] = jnp.zeros((SHEETS, 128), F32)
    for at in range(0, NPROJ, PCHUNK):
        here = slice(at, at + PCHUNK)
        with_re = dot3(coeff, (bh_ref[:EDGE, here], bl_ref[:EDGE, here]), NN)
        with_im = dot3(coeff, (bh_ref[EDGE:, here], bl_ref[EDGE:, here]), NN)
        y_re = with_re[:STICKS] + with_im[STICKS:]
        y_im = with_re[STICKS:] - with_im[:STICKS]
        a_re, a_im = a_ref[:STICKS, here], a_ref[STICKS:, here]
        becp_ref[0:1, here] = jnp.sum(a_re * y_re + a_im * y_im, axis=0, keepdims=True)
        becp_ref[1:2, here] = jnp.sum(a_re * y_im - a_im * y_re, axis=0, keepdims=True)
    scale = 1.0 / (math.sqrt(TEAMS * SHEETS * LINES * EDGE) * math.sqrt(NPROJ))
    re, im = becp_ref[0:1, :] * scale, becp_ref[1:2, :] * scale
    dij, diag = dij_ref[...], diag_ref[...]
    per_atom = mul(rows_of(re * dij, im * dij), mask_ref[...], NT)
    common = mul(
        rows_of(per_atom[0:1] + per_atom[2:3], per_atom[1:2] + per_atom[3:4]), mask_ref[...], NN
    )
    w = (
        re * diag + dij * (common[0:1] + common[2:3]),
        im * diag + dij * (common[1:2] + common[3:4]),
    )
    for part in range(2):
        for block in range(BLOCKS):
            row = ROWS * (part * BLOCKS + block) + DEPTH
            out_ref[row : row + 1, :] = w[part][:, block * 128 : (block + 1) * 128]


def spread_kernel(cols_ref, x_ref, hot_ref):
    half = SHEETS // 2
    x, y = lateral_split(jnp.concatenate([cols_ref[:half, :], cols_ref[half:, :]], axis=1))
    x, y = x + CUT, y + CUT
    x_ref[0] = x >> 1
    x_ref[1] = (x & 1) * 128 + y
    rows256 = lax.broadcasted_iota(jnp.int32, (256, 128), 0)
    per = CHUNK // 128
    for chunk in range(CHUNKS):
        for inner in range(per):
            r = chunk * per + inner
            lanes = slice(inner * 128, (inner + 1) * 128)
            hot_ref[chunk, :, lanes] = jnp.where(rows256 == x_ref[1, r : r + 1, :], 1.0, 0.0).astype(BF16)


def plane_kernel(
    x_ref, hot_ref, sticks_ref, potential_ref,
    yih_ref, yil_ref, xih_ref, xil_ref, xfh_ref, xfl_ref, yfh_ref, yfl_ref,
    out_ref, v_ref, left_ref, pick_ref,
):
    half = SHEETS // 2
    for plane in range(DEPTH):
        rows = sticks_ref[every(plane), :]
        top, bottom = rows[:half], rows[half:]
        for part in range(2):
            lanes = slice(part * STICKS, (part + 1) * STICKS)
            value = jnp.concatenate([top[:, lanes], bottom[:, lanes]], axis=1)
            high = value.astype(BF16).astype(F32)
            at = 2 * (2 * plane + part)
            v_ref[at] = high
            v_ref[at + 1] = value - high
    summed = jnp.sum(sticks_ref[every(DEPTH), :], axis=0, keepdims=True)
    out_ref[every(DEPTH), :] = jnp.broadcast_to(summed, (SHEETS, 128))
    rows64 = lax.broadcasted_iota(jnp.int32, (HALF_ROWS, 128), 0)
    per = CHUNK // 128
    total = jnp.zeros((12 * HALF_ROWS, 256), F32)
    for chunk in range(CHUNKS):
        slot = chunk % 2
        for inner in range(per):
            r = chunk * per + inner
            lanes = slice(inner * 128, (inner + 1) * 128)
            member = rows64 == x_ref[0, r : r + 1, :]
            for k in range(12):
                left_ref[slot, k * HALF_ROWS : (k + 1) * HALF_ROWS, lanes] = jnp.where(
                    member, v_ref[k, r : r + 1, :], 0.0
                ).astype(BF16)
        total = total + mul(left_ref[slot], hot_ref[chunk], NT)
    grids = []
    for plane in range(DEPTH):
        parts = []
        for part in range(2):
            at = 2 * (2 * plane + part) * HALF_ROWS
            grid = total[at : at + HALF_ROWS] + total[at + HALF_ROWS : at + 2 * HALF_ROWS]
            parts.append(jnp.concatenate([grid[:, :128], grid[:, 128:]], axis=0))
        grids.append(jnp.concatenate(parts, axis=1))
    work = jnp.concatenate(grids, axis=0)
    work = dot3(split(work), (yih_ref[...], yil_ref[...]), NN)
    work = jnp.concatenate(
        [
            jnp.concatenate(
                [work[p * 128 : (p + 1) * 128, :256], work[p * 128 : (p + 1) * 128, 256:]], axis=0
            )
            for p in range(DEPTH)
        ],
        axis=1,
    )
    work = dot3((xih_ref[...], xil_ref[...]), split(work), NN)
    local = jnp.concatenate([potential_ref[p] for p in range(DEPTH)], axis=1)
    work = jnp.concatenate([work[:EDGE] * local, work[EDGE:] * local], axis=0)
    work = dot3((xfh_ref[...], xfl_ref[...]), split(work), NN)
    work = jnp.concatenate(
        [
            jnp.concatenate(
                [work[:128, p * 256 : (p + 1) * 256], work[128:, p * 256 : (p + 1) * 256]], axis=1
            )
            for p in range(DEPTH)
        ],
        axis=0,
    )
    work = dot3(split(work), (yfh_ref[...], yfl_ref[...]), NN)
    pieces = []
    for p in range(DEPTH):
        for c in range(2):
            block = work[p * 128 : (p + 1) * 128, c * 128 : (c + 1) * 128]
            pieces.append(jnp.concatenate([block[:HALF_ROWS], block[HALF_ROWS:]], axis=1))
    high, low = split(jnp.concatenate(pieces, axis=0))
    for chunk in range(CHUNKS):
        hot = hot_ref[chunk]
        found = mul(high, hot, NN) + mul(low, hot, NN)
        for inner in range(per):
            r = chunk * per + inner
            lanes = slice(inner * 128, (inner + 1) * 128)
            member = rows64 == x_ref[0, r : r + 1, :]
            for k in range(6):
                pick_ref[k, r : r + 1, :] = jnp.sum(
                    jnp.where(member, found[k * HALF_ROWS : (k + 1) * HALF_ROWS, lanes], 0.0),
                    axis=0,
                    keepdims=True,
                )
    for plane in range(DEPTH):
        re, im = pick_ref[2 * plane], pick_ref[2 * plane + 1]
        out_ref[every(plane), :] = jnp.concatenate(
            [
                jnp.concatenate([re[:, :STICKS], im[:, :STICKS]], axis=1),
                jnp.concatenate([re[:, STICKS:], im[:, STICKS:]], axis=1),
            ],
            axis=0,
        )


def finish_kernel(
    sheet_ref, counts_ref, cols_ref, sticks_ref, back_ref, a_ref, bh_ref, bl_ref, th_ref, tl_ref, out_ref
):
    sheet = sheet_ref[0]
    vnl_re = jnp.zeros((2 * STICKS, EDGE), F32)
    vnl_im = jnp.zeros((2 * STICKS, EDGE), F32)
    step = 2 * PCHUNK
    for at in range(0, NPROJ, step):
        here = slice(at, at + step)
        a_re, a_im = a_ref[:STICKS, here], a_ref[STICKS:, here]
        w_re, w_im = (
            jnp.concatenate(
                [
                    back_ref[row : row + 1, :]
                    for row in range(
                        ROWS * (part * BLOCKS + at // 128) + DEPTH,
                        ROWS * (part * BLOCKS + (at + step) // 128) + DEPTH,
                        ROWS,
                    )
                ],
                axis=1,
            )
            for part in range(2)
        )
        weighted = split(
            jnp.concatenate([a_re * w_re - a_im * w_im, a_re * w_im + a_im * w_re], axis=0)
        )
        vnl_re = vnl_re + dot3(weighted, (bh_ref[:EDGE, here], bl_ref[:EDGE, here]), NT)
        vnl_im = vnl_im + dot3(weighted, (bh_ref[EDGE:, here], bl_ref[EDGE:, here]), NT)
    back = jnp.concatenate([back_ref[every(plane), :] for plane in range(DEPTH)], axis=0)
    back = split(back.T)
    with_cos = dot3(back, (th_ref[:EDGE], tl_ref[:EDGE]), NN)
    with_sin = dot3(back, (th_ref[EDGE:], tl_ref[EDGE:]), NN)
    box_scale = 1.0 / float(EDGE) ** 3
    sums = (
        (with_cos[:STICKS] + with_sin[STICKS:]) * box_scale + (vnl_re[:STICKS] - vnl_im[STICKS:]),
        (with_cos[STICKS:] - with_sin[:STICKS]) * box_scale + (vnl_re[STICKS:] + vnl_im[:STICKS]),
    )
    gx, gy = own_lateral(cols_ref, sheet)
    gz = lax.broadcasted_iota(jnp.int32, (1, EDGE), 1)
    gz = jnp.where(gz < EDGE // 2, gz, gz - EDGE).astype(F32)
    kinetic = 2.0 * (((gx * gx + gy * gy) + gz * gz) / (EDGE * EDGE))
    for team in range(TEAMS):
        live = live_column(counts_ref, sheet, team)
        rows = slice(team * LINES, (team + 1) * LINES)
        for part in range(2):
            value = kinetic[rows] * sticks_ref[team, part] + sums[part][rows]
            out_ref[team, part] = jnp.where(live, value, 0.0)


def call(kernel, n_scalars, n_inputs, outs, scratch=(), flops=0, limit=20 << 20):
    smem = pl.BlockSpec(memory_space=pltpu.SMEM)
    vmem = pl.BlockSpec(memory_space=pltpu.VMEM)
    return pl.pallas_call(
        kernel,
        out_shape=outs,
        in_specs=[smem] * n_scalars + [vmem] * n_inputs,
        out_specs=jax.tree.map(lambda _: vmem, outs),
        scratch_shapes=list(scratch),
        compiler_params=pltpu.CompilerParams(vmem_limit_bytes=limit),
        cost_estimate=pl.CostEstimate(flops=flops, bytes_accessed=4 << 20, transcendentals=0),
    )


def shape(dims, dtype=F32):
    return jax.ShapeDtypeStruct(dims, dtype)


def make_tables(sheet, cols, proj_atom, atom_pos, proj_radius):
    return call(
        table_kernel, 1, 4,
        (
            shape((2 * STICKS, NPROJ)),
            shape((2 * EDGE, NPROJ), BF16),
            shape((2 * EDGE, NPROJ), BF16),
            shape((NATOM, NPROJ), BF16),
        ),
        flops=2 << 30,
    )(sheet, cols, proj_atom.reshape(1, NPROJ), atom_pos, proj_radius.reshape(1, NPROJ))


def project(sheet, counts, sticks, tables, proj_diag, dij):
    a, bh, bl, mask = tables
    return call(
        project_kernel, 2, 9, shape((SHEETS * ROWS, 2 * STICKS)), [pltpu.VMEM((2, NPROJ), F32)], flops=3 << 30
    )(
        sheet, counts, sticks, *split_table(depth_table()), a, bh, bl, mask,
        proj_diag.reshape(1, NPROJ), dij.reshape(1, NPROJ),
    )


def spread(cols):
    return call(
        spread_kernel, 0, 1,
        (shape((2, SHEETS // 2, 128), jnp.int32), shape((CHUNKS, 256, CHUNK), BF16)),
        flops=1 << 30,
    )(cols)


def plane_work(spots, sticks, potential):
    tables = [piece for table in lateral_tables() for piece in split_table(table)]
    padded = jnp.pad(potential.reshape(DEPTH, EDGE, EDGE), ((0, 0), (0, 0), (0, 256 - EDGE)))
    return call(
        plane_kernel, 0, 12, shape((SHEETS * ROWS, 2 * STICKS)),
        [
            pltpu.VMEM((12, SHEETS // 2, 128), F32),
            pltpu.VMEM((2, 12 * HALF_ROWS, CHUNK), BF16),
            pltpu.VMEM((6, SHEETS // 2, 128), F32),
        ],
        flops=8 << 30,
        limit=28 << 20,
    )(*spots, sticks, padded, *tables)


def finish(sheet, counts, cols, sticks, back, tables):
    a, bh, bl, _ = tables
    return call(finish_kernel, 2, 8, shape((TEAMS, 2, LINES, EDGE)), flops=3 << 30)(
        sheet, counts, cols, sticks, back, a, bh, bl, *split_table(depth_table())
    )


def over_sheets(rows):
    sent = rows.reshape(SHEETS, ROWS, 2 * STICKS)
    return lax.all_to_all(sent, "pw", split_axis=0, concat_axis=0, tiled=True).reshape(rows.shape)


def body(
    orbital_coefficients,
    potential,
    line_lateral_place,
    stick_count,
    proj_atom,
    atom_pos,
    proj_radius,
    proj_diag,
    ionic_pseudo_dij,
):
    sheet = lax.axis_index("pw").astype(jnp.int32).reshape(1)
    layout = line_lateral_place[: TEAMS * SHEETS * LINES].reshape(TEAMS, SHEETS, LINES)
    cols = jnp.transpose(layout, (1, 0, 2)).reshape(SHEETS, STICKS)
    sticks = lax.all_to_all(orbital_coefficients, "tg", split_axis=0, concat_axis=0, tiled=True)
    tables = make_tables(sheet, cols, proj_atom, atom_pos, proj_radius)
    by_depth = project(sheet, stick_count, sticks, tables, proj_diag, ionic_pseudo_dij)
    by_plane = over_sheets(by_depth)
    picked = plane_work(spread(cols), by_plane, potential)
    back = over_sheets(picked)
    done = finish(sheet, stick_count, cols, sticks, back, tables)
    return lax.all_to_all(done, "tg", split_axis=0, concat_axis=0, tiled=True)


def solution(mesh):
    return jax.shard_map(
        body,
        mesh=mesh,
        in_specs=(
            P(None, None, ("tg", "pw"), None),
            P("pw", None),
            P(),
            P(),
            P(),
            P(),
            P(),
            P(),
            P(),
        ),
        out_specs=P(None, None, ("tg", "pw"), None),
        check_vma=False,
    )
```

```python
import math

import jax
import jax.numpy as jnp
import numpy as np
from jax import lax
from jax.experimental import pallas as pl
from jax.experimental.pallas import tpu as pltpu
from jax.sharding import PartitionSpec as P

EDGE = 192
TEAMS = 8
SHEETS = 64
DEPTH = 3
ROWS = DEPTH + 1
LINES = 8
STICKS = TEAMS * LINES
NPROJ = 2048
NATOM = 512
CUT = 48
HALF_ROWS = 64
CHUNK = 512
CHUNKS = SHEETS * STICKS // CHUNK
PCHUNK = 256
BLOCKS = NPROJ // 128

F32 = jnp.float32
BF16 = jnp.bfloat16

NN = (((1,), (0,)), ((), ()))
NT = (((1,), (1,)), ((), ()))


def split_table(table):
    high = table.astype(np.float32).astype(jnp.bfloat16)
    low = (table - high.astype(np.float64)).astype(np.float32).astype(jnp.bfloat16)
    return high, low


def depth_table():
    steps = np.arange(EDGE)
    planes = steps.reshape(SHEETS, DEPTH).T.reshape(-1)
    turns = (planes[:, None] * steps[None, :] % EDGE) * (2.0 * math.pi / EDGE)
    return np.concatenate([np.cos(turns), np.sin(turns)], axis=0)


def fold_matrix():
    fold = np.zeros((EDGE, 256))
    for z in range(EDGE):
        g = z if z < EDGE // 2 else z - EDGE
        fold[z, abs(g)] = 1.0
        fold[z, 128 + abs(g)] = np.sign(g)
    return fold.astype(jnp.bfloat16)


def column_phase(freqs, valid):
    turns = (freqs[:, None] * np.arange(EDGE)[None, :] % EDGE) * (2.0 * math.pi / EDGE)
    keep = valid[:, None].astype(np.float64)
    return np.cos(turns) * keep, np.sin(turns) * keep


def lateral_tables():
    spot = np.arange(2 * HALF_ROWS)
    y_cos, y_sin = column_phase(spot - CUT, spot <= 2 * CUT)
    pad = ((0, 0), (0, 256 - EDGE))
    y_cos, y_sin = np.pad(y_cos, pad), np.pad(y_sin, pad)
    y_inverse = np.block([[y_cos, y_sin], [-y_sin, y_cos]])
    x_spot = 2 * (spot % HALF_ROWS) + spot // HALF_ROWS
    x_cos, x_sin = column_phase(x_spot - CUT, x_spot <= 2 * CUT)
    x_forward = np.block([[x_cos, x_sin], [-x_sin, x_cos]])
    return y_inverse, x_forward.T, x_forward, y_inverse.T


def split(value):
    high = value.astype(BF16)
    return high, (value - high.astype(F32)).astype(BF16)


def mul(left, right, form):
    return lax.dot_general(left, right, form, preferred_element_type=F32)


def dot3(left, right, form):
    return mul(left[0], right[0], form) + mul(left[0], right[1], form) + mul(left[1], right[0], form)


def lateral_split(cols):
    x = (cols * 43691) >> 23
    y = cols - x * EDGE
    x = jnp.where(x < EDGE // 2, x, x - EDGE)
    y = jnp.where(y < EDGE // 2, y, y - EDGE)
    return x, y


def sincos_turns(turns):
    quarter = turns * 4.0
    near = jnp.floor(quarter + 0.5)
    x = (quarter - near) * (0.5 * math.pi)
    which = near.astype(jnp.int32) & 3
    xx = x * x
    sine = x * (1.0 + xx * (-1.0 / 6 + xx * (1.0 / 120 + xx * (-1.0 / 5040 + xx * (1.0 / 362880)))))
    cosine = 1.0 + xx * (-0.5 + xx * (1.0 / 24 + xx * (-1.0 / 720 + xx * (1.0 / 40320))))
    odd = (which & 1) == 1
    c = jnp.where(odd, sine, cosine)
    s = jnp.where(odd, cosine, sine)
    return jnp.where(((which + 1) & 2) == 2, -c, c), jnp.where((which & 2) == 2, -s, s)


def own_lateral(cols_ref, sheet):
    row = cols_ref[pl.ds(sheet, 1), :]
    x, y = lateral_split(row)
    eye = lax.broadcasted_iota(jnp.int32, (STICKS, STICKS), 0) == lax.broadcasted_iota(
        jnp.int32, (STICKS, STICKS), 1
    )

    def upright(value):
        wide = jnp.broadcast_to(value.astype(F32), (STICKS, STICKS))
        return jnp.sum(jnp.where(eye, wide, 0.0), axis=1, keepdims=True)

    return upright(x), upright(y)


def live_column(counts_ref, sheet, team):
    line = lax.broadcasted_iota(jnp.int32, (LINES, EDGE), 0)
    return line < counts_ref[team * SHEETS + sheet]


def live_sticks(sticks_ref, counts_ref, sheet):
    rows = []
    for part in range(2):
        for team in range(TEAMS):
            live = live_column(counts_ref, sheet, team)
            rows.append(jnp.where(live, sticks_ref[team, part], 0.0))
    return jnp.concatenate(rows, axis=0)


def member_of(atom_row):
    atoms = lax.broadcasted_iota(jnp.int32, (NATOM, atom_row.shape[1]), 0)
    return jnp.where(atoms == atom_row, 1.0, 0.0).astype(BF16)


def table_kernel(
    sheet_ref, cols_ref, atom_hbm, pos_hbm, radius_hbm, a_hbm, bh_hbm, bl_hbm,
    atom_ref, pos_ref, radius_ref, a_ref, bh_ref, bl_ref, in_sem, out_sem,
):
    loads = [
        pltpu.make_async_copy(source, target, in_sem.at[k])
        for k, (source, target) in enumerate(
            ((atom_hbm, atom_ref), (pos_hbm, pos_ref), (radius_hbm, radius_ref))
        )
    ]
    for load in loads:
        load.start()
    gx, gy = own_lateral(cols_ref, sheet_ref[0])
    gxy = gx * gx + gy * gy
    for load in loads:
        load.wait()
    pos = pos_ref[...]
    first = pos.astype(BF16).astype(F32)
    second = (pos - first).astype(BF16).astype(F32)
    third = (pos - first - second).astype(BF16).astype(F32)
    line = lax.broadcasted_iota(jnp.int32, (16, NATOM), 0)
    rows = jnp.zeros((16, NATOM), F32)
    for step, piece in enumerate((first, second, third)):
        for axis in range(3):
            rows = jnp.where(line == 3 * step + axis, piece[axis : axis + 1, :], rows)
    rows = rows.astype(BF16)
    low_g = lax.broadcasted_iota(jnp.int32, (8, PCHUNK), 0).astype(F32)
    for at in range(0, NPROJ, PCHUNK):
        here = slice(at, at + PCHUNK)
        placed = mul(rows, member_of(atom_ref[:, here]), NN)
        tx, ty, tz = (
            placed[axis : axis + 1] + placed[3 + axis : 4 + axis] + placed[6 + axis : 7 + axis]
            for axis in range(3)
        )
        spread = radius_ref[:, here] / (EDGE * EDGE)
        cosine, sine = sincos_turns(gx * tx + gy * ty)
        amp = jnp.exp(-spread * gxy)
        a_ref[:STICKS, here] = amp * cosine
        a_ref[STICKS:, here] = -amp * sine
        low_c, low_s = sincos_turns(low_g * tz)
        for bank in range(2):
            high_g = lax.broadcasted_iota(jnp.int32, (8, PCHUNK), 0) * 8 + bank * 64
            high_c, high_s = sincos_turns(high_g.astype(F32) * tz)
            for pair in range(4):
                re_rows, im_rows = [], []
                for inner in range(2):
                    row = pair * 2 + inner
                    hc, hs = high_c[row : row + 1], high_s[row : row + 1]
                    g = low_g + float((bank * 8 + row) * 8)
                    amp_z = jnp.exp(-spread * (g * g))
                    re_rows.append(amp_z * (hc * low_c - hs * low_s))
                    im_rows.append(-amp_z * (hs * low_c + hc * low_s))
                z = (bank * 8 + pair * 2) * 8
                for base, found in ((z, re_rows), (128 + z, im_rows)):
                    high, low = split(jnp.concatenate(found, axis=0))
                    bh_ref[base : base + 16, here] = high
                    bl_ref[base : base + 16, here] = low
    stores = [
        pltpu.make_async_copy(source, target, out_sem.at[k])
        for k, (source, target) in enumerate(((a_ref, a_hbm), (bh_ref, bh_hbm), (bl_ref, bl_hbm)))
    ]
    for store in stores:
        store.start()
    for store in stores:
        store.wait()


def rows_of(re, im):
    re_high = re.astype(BF16).astype(F32)
    im_high = im.astype(BF16).astype(F32)
    line = lax.broadcasted_iota(jnp.int32, (16, re.shape[1]), 0)
    rows = jnp.where(line == 0, re_high, 0.0)
    rows = jnp.where(line == 1, im_high, rows)
    rows = jnp.where(line == 2, re - re_high, rows)
    return jnp.where(line == 3, im - im_high, rows).astype(BF16)


def every(start):
    return pl.ds(start, SHEETS, stride=ROWS)


def project_kernel(
    sheet_ref, counts_ref, sticks_ref, th_ref, tl_ref, fold_ref, atom_ref, diag_ref, dij_ref, a_hbm, bh_hbm, bl_hbm,
    out_ref, becp_ref, mask_ref, a_ref, bh_ref, bl_ref, sem,
):
    loads = [
        pltpu.make_async_copy(source, target, sem.at[k])
        for k, (source, target) in enumerate(((bh_hbm, bh_ref), (bl_hbm, bl_ref), (a_hbm, a_ref)))
    ]
    for load in loads:
        load.start()
    for at in range(0, NPROJ, PCHUNK):
        mask_ref[:, at : at + PCHUNK] = member_of(atom_ref[:, at : at + PCHUNK])
    coeff = split(live_sticks(sticks_ref, counts_ref, sheet_ref[0]))
    both = dot3((th_ref[...], tl_ref[...]), coeff, NT)
    with_cos, with_sin = both[:EDGE], both[EDGE:]
    by_depth = with_cos + jnp.concatenate([-with_sin[:, STICKS:], with_sin[:, :STICKS]], axis=1)
    folded = mul(coeff[0], fold_ref[...], NN) + mul(coeff[1], fold_ref[...], NN)
    paired = split(
        jnp.concatenate(
            [
                jnp.concatenate([folded[:STICKS, :128], folded[STICKS:, 128:]], axis=1),
                jnp.concatenate([folded[STICKS:, :128], -folded[:STICKS, 128:]], axis=1),
            ],
            axis=0,
        )
    )
    for plane in range(DEPTH):
        out_ref[every(plane), :] = by_depth[plane * SHEETS : (plane + 1) * SHEETS]
    out_ref[every(DEPTH), :] = jnp.zeros((SHEETS, 128), F32)
    for load in loads:
        load.wait()
    for at in range(0, NPROJ, PCHUNK):
        here = slice(at, at + PCHUNK)
        y = dot3(paired, (bh_ref[:, here], bl_ref[:, here]), NN)
        y_re, y_im = y[:STICKS], y[STICKS:]
        a_re, a_im = a_ref[:STICKS, here], a_ref[STICKS:, here]
        becp_ref[0:1, here] = jnp.sum(a_re * y_re + a_im * y_im, axis=0, keepdims=True)
        becp_ref[1:2, here] = jnp.sum(a_re * y_im - a_im * y_re, axis=0, keepdims=True)
    scale = 1.0 / (math.sqrt(TEAMS * SHEETS * LINES * EDGE) * math.sqrt(NPROJ))
    re, im = becp_ref[0:1, :] * scale, becp_ref[1:2, :] * scale
    dij, diag = dij_ref[...], diag_ref[...]
    per_atom = mul(rows_of(re * dij, im * dij), mask_ref[...], NT)
    common = mul(
        rows_of(per_atom[0:1] + per_atom[2:3], per_atom[1:2] + per_atom[3:4]), mask_ref[...], NN
    )
    w = (
        re * diag + dij * (common[0:1] + common[2:3]),
        im * diag + dij * (common[1:2] + common[3:4]),
    )
    for part in range(2):
        for block in range(BLOCKS):
            row = ROWS * (part * BLOCKS + block) + DEPTH
            out_ref[row : row + 1, :] = w[part][:, block * 128 : (block + 1) * 128]


def plane_kernel(
    cols_ref, sticks_ref, potential_ref,
    yih_ref, yil_ref, xih_ref, xil_ref, xfh_ref, xfl_ref, yfh_ref, yfl_ref,
    out_ref, x_ref, v_ref, hot_ref, left_ref, pick_ref,
):
    half = SHEETS // 2
    x, y = lateral_split(jnp.concatenate([cols_ref[:half, :], cols_ref[half:, :]], axis=1))
    x, y = x + CUT, y + CUT
    x_ref[0] = x >> 1
    x_ref[1] = (x & 1) * 128 + y
    for plane in range(DEPTH):
        rows = sticks_ref[every(plane), :]
        top, bottom = rows[:half], rows[half:]
        for part in range(2):
            lanes = slice(part * STICKS, (part + 1) * STICKS)
            value = jnp.concatenate([top[:, lanes], bottom[:, lanes]], axis=1)
            high = value.astype(BF16).astype(F32)
            at = 2 * (2 * plane + part)
            v_ref[at] = high
            v_ref[at + 1] = value - high
    summed = jnp.sum(sticks_ref[every(DEPTH), :], axis=0, keepdims=True)
    out_ref[every(DEPTH), :] = jnp.broadcast_to(summed, (SHEETS, 128))
    rows64 = lax.broadcasted_iota(jnp.int32, (HALF_ROWS, 128), 0)
    rows256 = lax.broadcasted_iota(jnp.int32, (256, 128), 0)
    per = CHUNK // 128
    total = jnp.zeros((12 * HALF_ROWS, 256), F32)
    for chunk in range(CHUNKS):
        slot = chunk % 2
        for inner in range(per):
            r = chunk * per + inner
            lanes = slice(inner * 128, (inner + 1) * 128)
            member = jnp.where(rows64 == x_ref[0, r : r + 1, :], 1.0, 0.0).astype(BF16)
            hot_ref[chunk, :, lanes] = jnp.where(rows256 == x_ref[1, r : r + 1, :], 1.0, 0.0).astype(BF16)
            for k in range(12):
                value = jnp.broadcast_to(v_ref[k, r : r + 1, :], (16, 128)).astype(BF16)
                value = jnp.concatenate([value] * (HALF_ROWS // 16), axis=0)
                left_ref[slot, k * HALF_ROWS : (k + 1) * HALF_ROWS, lanes] = member * value
        total = total + mul(left_ref[slot], hot_ref[chunk], NT)
    grids = []
    for plane in range(DEPTH):
        parts = []
        for part in range(2):
            at = 2 * (2 * plane + part) * HALF_ROWS
            grid = total[at : at + HALF_ROWS] + total[at + HALF_ROWS : at + 2 * HALF_ROWS]
            parts.append(jnp.concatenate([grid[:, :128], grid[:, 128:]], axis=0))
        grids.append(jnp.concatenate(parts, axis=1))
    work = jnp.concatenate(grids, axis=0)
    work = dot3(split(work), (yih_ref[...], yil_ref[...]), NN)
    work = jnp.concatenate(
        [
            jnp.concatenate(
                [work[p * 128 : (p + 1) * 128, :256], work[p * 128 : (p + 1) * 128, 256:]], axis=0
            )
            for p in range(DEPTH)
        ],
        axis=1,
    )
    work = dot3((xih_ref[...], xil_ref[...]), split(work), NN)
    local = jnp.concatenate([potential_ref[p] for p in range(DEPTH)], axis=1)
    work = jnp.concatenate([work[:EDGE] * local, work[EDGE:] * local], axis=0)
    work = dot3((xfh_ref[...], xfl_ref[...]), split(work), NN)
    work = jnp.concatenate(
        [
            jnp.concatenate(
                [work[:128, p * 256 : (p + 1) * 256], work[128:, p * 256 : (p + 1) * 256]], axis=1
            )
            for p in range(DEPTH)
        ],
        axis=0,
    )
    work = dot3(split(work), (yfh_ref[...], yfl_ref[...]), NN)
    pieces = []
    for p in range(DEPTH):
        for c in range(2):
            block = work[p * 128 : (p + 1) * 128, c * 128 : (c + 1) * 128]
            pieces.append(jnp.concatenate([block[:HALF_ROWS], block[HALF_ROWS:]], axis=1))
    high, low = split(jnp.concatenate(pieces, axis=0))
    for chunk in range(CHUNKS):
        hot = hot_ref[chunk]
        found = mul(high, hot, NN) + mul(low, hot, NN)
        for inner in range(per):
            r = chunk * per + inner
            lanes = slice(inner * 128, (inner + 1) * 128)
            member = rows64 == x_ref[0, r : r + 1, :]
            for k in range(6):
                pick_ref[k, r : r + 1, :] = jnp.sum(
                    jnp.where(member, found[k * HALF_ROWS : (k + 1) * HALF_ROWS, lanes], 0.0),
                    axis=0,
                    keepdims=True,
                )
    for plane in range(DEPTH):
        re, im = pick_ref[2 * plane], pick_ref[2 * plane + 1]
        out_ref[every(plane), :] = jnp.concatenate(
            [
                jnp.concatenate([re[:, :STICKS], im[:, :STICKS]], axis=1),
                jnp.concatenate([re[:, STICKS:], im[:, STICKS:]], axis=1),
            ],
            axis=0,
        )


def finish_kernel(
    sheet_ref, counts_ref, cols_ref, sticks_ref, back_ref, a_ref, bh_ref, bl_ref, th_ref, tl_ref, fold_ref,
    out_ref,
):
    sheet = sheet_ref[0]
    vnl = jnp.zeros((2 * STICKS, 256), F32)
    step = 2 * PCHUNK
    for at in range(0, NPROJ, step):
        here = slice(at, at + step)
        a_re, a_im = a_ref[:STICKS, here], a_ref[STICKS:, here]
        w_re, w_im = (
            jnp.concatenate(
                [
                    back_ref[row : row + 1, :]
                    for row in range(
                        ROWS * (part * BLOCKS + at // 128) + DEPTH,
                        ROWS * (part * BLOCKS + (at + step) // 128) + DEPTH,
                        ROWS,
                    )
                ],
                axis=1,
            )
            for part in range(2)
        )
        weighted = split(
            jnp.concatenate([a_re * w_re - a_im * w_im, a_re * w_im + a_im * w_re], axis=0)
        )
        vnl = vnl + dot3(weighted, (bh_ref[:, here], bl_ref[:, here]), NT)
    vnl = split(
        jnp.concatenate(
            [
                jnp.concatenate([vnl[:STICKS, :128], -vnl[STICKS:, 128:]], axis=1),
                jnp.concatenate([vnl[STICKS:, :128], vnl[:STICKS, 128:]], axis=1),
            ],
            axis=0,
        )
    )
    vnl = mul(vnl[0], fold_ref[...], NT) + mul(vnl[1], fold_ref[...], NT)
    back = jnp.concatenate([back_ref[every(plane), :] for plane in range(DEPTH)], axis=0)
    back = split(back.T)
    with_cos = dot3(back, (th_ref[:EDGE], tl_ref[:EDGE]), NN)
    with_sin = dot3(back, (th_ref[EDGE:], tl_ref[EDGE:]), NN)
    box_scale = 1.0 / float(EDGE) ** 3
    sums = (
        (with_cos[:STICKS] + with_sin[STICKS:]) * box_scale + vnl[:STICKS],
        (with_cos[STICKS:] - with_sin[:STICKS]) * box_scale + vnl[STICKS:],
    )
    gx, gy = own_lateral(cols_ref, sheet)
    gz = lax.broadcasted_iota(jnp.int32, (1, EDGE), 1)
    gz = jnp.where(gz < EDGE // 2, gz, gz - EDGE).astype(F32)
    kinetic = 2.0 * (((gx * gx + gy * gy) + gz * gz) / (EDGE * EDGE))
    for team in range(TEAMS):
        live = live_column(counts_ref, sheet, team)
        rows = slice(team * LINES, (team + 1) * LINES)
        for part in range(2):
            value = kinetic[rows] * sticks_ref[team, part] + sums[part][rows]
            out_ref[team, part] = jnp.where(live, value, 0.0)


def call(kernel, places, outs, scratch=(), flops=0, limit=20 << 20, out_place=pltpu.VMEM):
    kinds = {"s": pltpu.SMEM, "v": pltpu.VMEM, "h": pltpu.HBM}
    return pl.pallas_call(
        kernel,
        out_shape=outs,
        in_specs=[pl.BlockSpec(memory_space=kinds[place]) for place in places],
        out_specs=jax.tree.map(lambda _: pl.BlockSpec(memory_space=out_place), outs),
        scratch_shapes=list(scratch),
        compiler_params=pltpu.CompilerParams(vmem_limit_bytes=limit),
        cost_estimate=pl.CostEstimate(flops=flops, bytes_accessed=4 << 20, transcendentals=0),
    )


def shape(dims, dtype=F32):
    return jax.ShapeDtypeStruct(dims, dtype)


TABLES = (((2 * STICKS, NPROJ), F32), ((256, NPROJ), BF16), ((256, NPROJ), BF16))


def make_tables(sheet, cols, proj_atom, atom_pos, proj_radius):
    return call(
        table_kernel, "svhhh", tuple(shape(*table) for table in TABLES),
        [
            pltpu.VMEM((1, NPROJ), jnp.int32),
            pltpu.VMEM((3, NATOM), F32),
            pltpu.VMEM((1, NPROJ), F32),
            *(pltpu.VMEM(*table) for table in TABLES),
            pltpu.SemaphoreType.DMA((3,)),
            pltpu.SemaphoreType.DMA((3,)),
        ],
        flops=2 << 30,
        out_place=pltpu.HBM,
    )(sheet, cols, proj_atom.reshape(1, NPROJ), atom_pos, proj_radius.reshape(1, NPROJ))


def project(sheet, counts, sticks, tables, proj_atom, proj_diag, dij):
    return call(
        project_kernel, "ssvvvvvvvhhh", shape((SHEETS * ROWS, 2 * STICKS)),
        [
            pltpu.VMEM((2, NPROJ), F32),
            pltpu.VMEM((NATOM, NPROJ), BF16),
            *(pltpu.VMEM(*table) for table in TABLES),
            pltpu.SemaphoreType.DMA((3,)),
        ],
        flops=3 << 30,
    )(
        sheet, counts, sticks, *split_table(depth_table()), fold_matrix(),
        proj_atom.reshape(1, NPROJ), proj_diag.reshape(1, NPROJ), dij.reshape(1, NPROJ), *tables,
    )


def plane_work(cols, sticks, potential):
    tables = [piece for table in lateral_tables() for piece in split_table(table)]
    padded = jnp.pad(potential.reshape(DEPTH, EDGE, EDGE), ((0, 0), (0, 0), (0, 256 - EDGE)))
    return call(
        plane_kernel, "v" * 11, shape((SHEETS * ROWS, 2 * STICKS)),
        [
            pltpu.VMEM((2, SHEETS // 2, 128), jnp.int32),
            pltpu.VMEM((12, SHEETS // 2, 128), F32),
            pltpu.VMEM((CHUNKS, 256, CHUNK), BF16),
            pltpu.VMEM((2, 12 * HALF_ROWS, CHUNK), BF16),
            pltpu.VMEM((6, SHEETS // 2, 128), F32),
        ],
        flops=8 << 30,
        limit=28 << 20,
    )(cols, sticks, padded, *tables)


def finish(sheet, counts, cols, sticks, back, tables):
    return call(finish_kernel, "ssvvvvvvvvv", shape((TEAMS, 2, LINES, EDGE)), flops=3 << 30)(
        sheet, counts, cols, sticks, back, *tables, *split_table(depth_table()), fold_matrix()
    )


def over_sheets(rows):
    sent = rows.reshape(SHEETS, ROWS, 2 * STICKS)
    return lax.all_to_all(sent, "pw", split_axis=0, concat_axis=0, tiled=True).reshape(rows.shape)


def body(
    orbital_coefficients,
    potential,
    line_lateral_place,
    stick_count,
    proj_atom,
    atom_pos,
    proj_radius,
    proj_diag,
    ionic_pseudo_dij,
):
    sheet = lax.axis_index("pw").astype(jnp.int32).reshape(1)
    layout = line_lateral_place[: TEAMS * SHEETS * LINES].reshape(TEAMS, SHEETS, LINES)
    cols = jnp.transpose(layout, (1, 0, 2)).reshape(SHEETS, STICKS)
    sticks = lax.all_to_all(orbital_coefficients, "tg", split_axis=0, concat_axis=0, tiled=True)
    tables = make_tables(sheet, cols, proj_atom, atom_pos, proj_radius)
    by_depth = project(sheet, stick_count, sticks, tables, proj_atom, proj_diag, ionic_pseudo_dij)
    by_plane = over_sheets(by_depth)
    picked = plane_work(cols, by_plane, potential)
    back = over_sheets(picked)
    done = finish(sheet, stick_count, cols, sticks, back, tables)
    return lax.all_to_all(done, "tg", split_axis=0, concat_axis=0, tiled=True)


def solution(mesh):
    return jax.shard_map(
        body,
        mesh=mesh,
        in_specs=(
            P(None, None, ("tg", "pw"), None),
            P("pw", None),
            P(),
            P(),
            P(),
            P(),
            P(),
            P(),
            P(),
        ),
        out_specs=P(None, None, ("tg", "pw"), None),
        check_vma=False,
    )
```

```python
import math

import jax
import jax.numpy as jnp
import numpy as np
from jax import lax
from jax.experimental import pallas as pl
from jax.experimental.pallas import tpu as pltpu
from jax.sharding import PartitionSpec as P

EDGE = 192
TEAMS = 8
SHEETS = 64
DEPTH = 3
ROWS = DEPTH + 1
LINES = 8
STICKS = TEAMS * LINES
NPROJ = 2048
NATOM = 512
CUT = 48
HALF_ROWS = 64
CHUNK = 512
CHUNKS = SHEETS * STICKS // CHUNK
PCHUNK = 256
BLOCKS = NPROJ // 128

F32 = jnp.float32
BF16 = jnp.bfloat16

NN = (((1,), (0,)), ((), ()))
NT = (((1,), (1,)), ((), ()))


def split_table(table):
    high = table.astype(np.float32).astype(jnp.bfloat16)
    low = (table - high.astype(np.float64)).astype(np.float32).astype(jnp.bfloat16)
    return high, low


def depth_table():
    steps = np.arange(EDGE)
    planes = steps.reshape(SHEETS, DEPTH).T.reshape(-1)
    turns = (planes[:, None] * steps[None, :] % EDGE) * (2.0 * math.pi / EDGE)
    return np.concatenate([np.cos(turns), np.sin(turns)], axis=0)


def fold_matrix():
    fold = np.zeros((EDGE, 256))
    for z in range(EDGE):
        g = z if z < EDGE // 2 else z - EDGE
        fold[z, abs(g)] = 1.0
        fold[z, 128 + abs(g)] = np.sign(g)
    return fold.astype(jnp.bfloat16)


def column_phase(freqs, valid):
    turns = (freqs[:, None] * np.arange(EDGE)[None, :] % EDGE) * (2.0 * math.pi / EDGE)
    keep = valid[:, None].astype(np.float64)
    return np.cos(turns) * keep, np.sin(turns) * keep


def lateral_tables():
    spot = np.arange(2 * HALF_ROWS)
    y_cos, y_sin = column_phase(spot - CUT, spot <= 2 * CUT)
    pad = ((0, 0), (0, 256 - EDGE))
    y_cos, y_sin = np.pad(y_cos, pad), np.pad(y_sin, pad)
    y_inverse = np.block([[y_cos, y_sin], [-y_sin, y_cos]])
    x_spot = 2 * (spot % HALF_ROWS) + spot // HALF_ROWS
    x_cos, x_sin = column_phase(x_spot - CUT, x_spot <= 2 * CUT)
    x_forward = np.block([[x_cos, x_sin], [-x_sin, x_cos]])
    return y_inverse, x_forward.T, x_forward, y_inverse.T


def split(value):
    high = value.astype(BF16)
    return high, (value - high.astype(F32)).astype(BF16)


def mul(left, right, form):
    return lax.dot_general(left, right, form, preferred_element_type=F32)


def dot3(left, right, form):
    return mul(left[0], right[0], form) + mul(left[0], right[1], form) + mul(left[1], right[0], form)


def lateral_split(cols):
    x = (cols * 43691) >> 23
    y = cols - x * EDGE
    x = jnp.where(x < EDGE // 2, x, x - EDGE)
    y = jnp.where(y < EDGE // 2, y, y - EDGE)
    return x, y


def sincos_turns(turns):
    quarter = turns * 4.0
    near = jnp.floor(quarter + 0.5)
    x = (quarter - near) * (0.5 * math.pi)
    which = near.astype(jnp.int32) & 3
    xx = x * x
    sine = x * (1.0 + xx * (-1.0 / 6 + xx * (1.0 / 120 + xx * (-1.0 / 5040 + xx * (1.0 / 362880)))))
    cosine = 1.0 + xx * (-0.5 + xx * (1.0 / 24 + xx * (-1.0 / 720 + xx * (1.0 / 40320))))
    odd = (which & 1) == 1
    c = jnp.where(odd, sine, cosine)
    s = jnp.where(odd, cosine, sine)
    return jnp.where(((which + 1) & 2) == 2, -c, c), jnp.where((which & 2) == 2, -s, s)


def own_lateral(cols_ref, sheet):
    row = cols_ref[pl.ds(sheet, 1), :]
    x, y = lateral_split(row)
    eye = lax.broadcasted_iota(jnp.int32, (STICKS, STICKS), 0) == lax.broadcasted_iota(
        jnp.int32, (STICKS, STICKS), 1
    )

    def upright(value):
        wide = jnp.broadcast_to(value.astype(F32), (STICKS, STICKS))
        return jnp.sum(jnp.where(eye, wide, 0.0), axis=1, keepdims=True)

    return upright(x), upright(y)


def live_column(counts_ref, sheet, team):
    line = lax.broadcasted_iota(jnp.int32, (LINES, EDGE), 0)
    return line < counts_ref[team * SHEETS + sheet]


def live_sticks(sticks_ref, counts_ref, sheet):
    rows = []
    for part in range(2):
        for team in range(TEAMS):
            live = live_column(counts_ref, sheet, team)
            rows.append(jnp.where(live, sticks_ref[team, part], 0.0))
    return jnp.concatenate(rows, axis=0)


def member_of(atom_row):
    atoms = lax.broadcasted_iota(jnp.int32, (NATOM, atom_row.shape[1]), 0)
    return jnp.where(atoms == atom_row, 1.0, 0.0).astype(BF16)


def place_kernel(sheet_ref, cols_ref, atom_hbm, pos_hbm, radius_hbm, a_ref, place_ref, atom_ref, pos_ref, radius_ref, sem):
    loads = [
        pltpu.make_async_copy(source, target, sem.at[k])
        for k, (source, target) in enumerate(
            ((atom_hbm, atom_ref), (pos_hbm, pos_ref), (radius_hbm, radius_ref))
        )
    ]
    for load in loads:
        load.start()
    gx, gy = own_lateral(cols_ref, sheet_ref[0])
    gxy = gx * gx + gy * gy
    for load in loads:
        load.wait()
    pos = pos_ref[...]
    first = pos.astype(BF16).astype(F32)
    second = (pos - first).astype(BF16).astype(F32)
    third = (pos - first - second).astype(BF16).astype(F32)
    line = lax.broadcasted_iota(jnp.int32, (16, NATOM), 0)
    rows = jnp.zeros((16, NATOM), F32)
    for step, piece in enumerate((first, second, third)):
        for axis in range(3):
            rows = jnp.where(line == 3 * step + axis, piece[axis : axis + 1, :], rows)
    rows = rows.astype(BF16)
    for at in range(0, NPROJ, PCHUNK):
        here = slice(at, at + PCHUNK)
        placed = mul(rows, member_of(atom_ref[:, here]), NN)
        tx, ty, tz = (
            placed[axis : axis + 1] + placed[3 + axis : 4 + axis] + placed[6 + axis : 7 + axis]
            for axis in range(3)
        )
        spread = radius_ref[:, here] / (EDGE * EDGE)
        place_ref[0:1, here] = tz
        place_ref[1:2, here] = spread
        cosine, sine = sincos_turns(gx * tx + gy * ty)
        amp = jnp.exp(-spread * gxy)
        a_ref[:STICKS, here] = amp * cosine
        a_ref[STICKS:, here] = -amp * sine


def depth_factors(place_ref, bh_ref, bl_ref):
    low_g = lax.broadcasted_iota(jnp.int32, (8, PCHUNK), 0).astype(F32)
    for at in range(0, NPROJ, PCHUNK):
        here = slice(at, at + PCHUNK)
        tz, spread = place_ref[0:1, here], place_ref[1:2, here]
        low_c, low_s = sincos_turns(low_g * tz)
        for bank in range(2):
            high_g = lax.broadcasted_iota(jnp.int32, (8, PCHUNK), 0) * 8 + bank * 64
            high_c, high_s = sincos_turns(high_g.astype(F32) * tz)
            for pair in range(4):
                re_rows, im_rows = [], []
                for inner in range(2):
                    row = pair * 2 + inner
                    hc, hs = high_c[row : row + 1], high_s[row : row + 1]
                    g = low_g + float((bank * 8 + row) * 8)
                    amp_z = jnp.exp(-spread * (g * g))
                    re_rows.append(amp_z * (hc * low_c - hs * low_s))
                    im_rows.append(-amp_z * (hs * low_c + hc * low_s))
                z = (bank * 8 + pair * 2) * 8
                for base, found in ((z, re_rows), (128 + z, im_rows)):
                    high, low = split(jnp.concatenate(found, axis=0))
                    bh_ref[base : base + 16, here] = high
                    bl_ref[base : base + 16, here] = low


def rows_of(re, im):
    re_high = re.astype(BF16).astype(F32)
    im_high = im.astype(BF16).astype(F32)
    line = lax.broadcasted_iota(jnp.int32, (16, re.shape[1]), 0)
    rows = jnp.where(line == 0, re_high, 0.0)
    rows = jnp.where(line == 1, im_high, rows)
    rows = jnp.where(line == 2, re - re_high, rows)
    return jnp.where(line == 3, im - im_high, rows).astype(BF16)


def every(start):
    return pl.ds(start, SHEETS, stride=ROWS)


def project_kernel(
    sheet_ref, counts_ref, sticks_ref, th_ref, tl_ref, fold_ref, atom_ref, diag_ref, dij_ref, a_ref, place_ref,
    out_ref, bh_ref, bl_ref, becp_ref, mask_ref,
):
    depth_factors(place_ref, bh_ref, bl_ref)
    for at in range(0, NPROJ, PCHUNK):
        mask_ref[:, at : at + PCHUNK] = member_of(atom_ref[:, at : at + PCHUNK])
    coeff = split(live_sticks(sticks_ref, counts_ref, sheet_ref[0]))
    both = dot3((th_ref[...], tl_ref[...]), coeff, NT)
    with_cos, with_sin = both[:EDGE], both[EDGE:]
    by_depth = with_cos + jnp.concatenate([-with_sin[:, STICKS:], with_sin[:, :STICKS]], axis=1)
    folded = mul(coeff[0], fold_ref[...], NN) + mul(coeff[1], fold_ref[...], NN)
    paired = split(
        jnp.concatenate(
            [
                jnp.concatenate([folded[:STICKS, :128], folded[STICKS:, 128:]], axis=1),
                jnp.concatenate([folded[STICKS:, :128], -folded[:STICKS, 128:]], axis=1),
            ],
            axis=0,
        )
    )
    for plane in range(DEPTH):
        out_ref[every(plane), :] = by_depth[plane * SHEETS : (plane + 1) * SHEETS]
    out_ref[every(DEPTH), :] = jnp.zeros((SHEETS, 128), F32)
    for at in range(0, NPROJ, PCHUNK):
        here = slice(at, at + PCHUNK)
        y = dot3(paired, (bh_ref[:, here], bl_ref[:, here]), NN)
        y_re, y_im = y[:STICKS], y[STICKS:]
        a_re, a_im = a_ref[:STICKS, here], a_ref[STICKS:, here]
        becp_ref[0:1, here] = jnp.sum(a_re * y_re + a_im * y_im, axis=0, keepdims=True)
        becp_ref[1:2, here] = jnp.sum(a_re * y_im - a_im * y_re, axis=0, keepdims=True)
    scale = 1.0 / (math.sqrt(TEAMS * SHEETS * LINES * EDGE) * math.sqrt(NPROJ))
    re, im = becp_ref[0:1, :] * scale, becp_ref[1:2, :] * scale
    dij, diag = dij_ref[...], diag_ref[...]
    per_atom = mul(rows_of(re * dij, im * dij), mask_ref[...], NT)
    common = mul(
        rows_of(per_atom[0:1] + per_atom[2:3], per_atom[1:2] + per_atom[3:4]), mask_ref[...], NN
    )
    w = (
        re * diag + dij * (common[0:1] + common[2:3]),
        im * diag + dij * (common[1:2] + common[3:4]),
    )
    for part in range(2):
        for block in range(BLOCKS):
            row = ROWS * (part * BLOCKS + block) + DEPTH
            out_ref[row : row + 1, :] = w[part][:, block * 128 : (block + 1) * 128]


def plane_kernel(
    cols_ref, sticks_ref, potential_ref,
    yih_ref, yil_ref, xih_ref, xil_ref, xfh_ref, xfl_ref, yfh_ref, yfl_ref,
    out_ref, x_ref, v_ref, hot_ref, left_ref, pick_ref,
):
    half = SHEETS // 2
    x, y = lateral_split(jnp.concatenate([cols_ref[:half, :], cols_ref[half:, :]], axis=1))
    x, y = x + CUT, y + CUT
    x_ref[0] = x >> 1
    x_ref[1] = (x & 1) * 128 + y
    for plane in range(DEPTH):
        rows = sticks_ref[every(plane), :]
        top, bottom = rows[:half], rows[half:]
        for part in range(2):
            lanes = slice(part * STICKS, (part + 1) * STICKS)
            value = jnp.concatenate([top[:, lanes], bottom[:, lanes]], axis=1)
            high = value.astype(BF16).astype(F32)
            at = 2 * (2 * plane + part)
            v_ref[at] = high
            v_ref[at + 1] = value - high
    summed = jnp.sum(sticks_ref[every(DEPTH), :], axis=0, keepdims=True)
    out_ref[every(DEPTH), :] = jnp.broadcast_to(summed, (SHEETS, 128))
    rows64 = lax.broadcasted_iota(jnp.int32, (HALF_ROWS, 128), 0)
    rows256 = lax.broadcasted_iota(jnp.int32, (256, 128), 0)
    per = CHUNK // 128
    total = jnp.zeros((12 * HALF_ROWS, 256), F32)
    for chunk in range(CHUNKS):
        slot = chunk % 2
        for inner in range(per):
            r = chunk * per + inner
            lanes = slice(inner * 128, (inner + 1) * 128)
            member = jnp.where(rows64 == x_ref[0, r : r + 1, :], 1.0, 0.0).astype(BF16)
            hot_ref[chunk, :, lanes] = jnp.where(rows256 == x_ref[1, r : r + 1, :], 1.0, 0.0).astype(BF16)
            for k in range(12):
                value = jnp.broadcast_to(v_ref[k, r : r + 1, :], (16, 128)).astype(BF16)
                value = jnp.concatenate([value] * (HALF_ROWS // 16), axis=0)
                left_ref[slot, k * HALF_ROWS : (k + 1) * HALF_ROWS, lanes] = member * value
        total = total + mul(left_ref[slot], hot_ref[chunk], NT)
    grids = []
    for plane in range(DEPTH):
        parts = []
        for part in range(2):
            at = 2 * (2 * plane + part) * HALF_ROWS
            grid = total[at : at + HALF_ROWS] + total[at + HALF_ROWS : at + 2 * HALF_ROWS]
            parts.append(jnp.concatenate([grid[:, :128], grid[:, 128:]], axis=0))
        grids.append(jnp.concatenate(parts, axis=1))
    work = jnp.concatenate(grids, axis=0)
    work = dot3(split(work), (yih_ref[...], yil_ref[...]), NN)
    work = jnp.concatenate(
        [
            jnp.concatenate(
                [work[p * 128 : (p + 1) * 128, :256], work[p * 128 : (p + 1) * 128, 256:]], axis=0
            )
            for p in range(DEPTH)
        ],
        axis=1,
    )
    work = dot3((xih_ref[...], xil_ref[...]), split(work), NN)
    local = jnp.concatenate([potential_ref[p] for p in range(DEPTH)], axis=1)
    work = jnp.concatenate([work[:EDGE] * local, work[EDGE:] * local], axis=0)
    work = dot3((xfh_ref[...], xfl_ref[...]), split(work), NN)
    work = jnp.concatenate(
        [
            jnp.concatenate(
                [work[:128, p * 256 : (p + 1) * 256], work[128:, p * 256 : (p + 1) * 256]], axis=1
            )
            for p in range(DEPTH)
        ],
        axis=0,
    )
    work = dot3(split(work), (yfh_ref[...], yfl_ref[...]), NN)
    pieces = []
    for p in range(DEPTH):
        for c in range(2):
            block = work[p * 128 : (p + 1) * 128, c * 128 : (c + 1) * 128]
            pieces.append(jnp.concatenate([block[:HALF_ROWS], block[HALF_ROWS:]], axis=1))
    high, low = split(jnp.concatenate(pieces, axis=0))
    for chunk in range(CHUNKS):
        hot = hot_ref[chunk]
        found = mul(high, hot, NN) + mul(low, hot, NN)
        for inner in range(per):
            r = chunk * per + inner
            lanes = slice(inner * 128, (inner + 1) * 128)
            member = rows64 == x_ref[0, r : r + 1, :]
            for k in range(6):
                pick_ref[k, r : r + 1, :] = jnp.sum(
                    jnp.where(member, found[k * HALF_ROWS : (k + 1) * HALF_ROWS, lanes], 0.0),
                    axis=0,
                    keepdims=True,
                )
    for plane in range(DEPTH):
        re, im = pick_ref[2 * plane], pick_ref[2 * plane + 1]
        out_ref[every(plane), :] = jnp.concatenate(
            [
                jnp.concatenate([re[:, :STICKS], im[:, :STICKS]], axis=1),
                jnp.concatenate([re[:, STICKS:], im[:, STICKS:]], axis=1),
            ],
            axis=0,
        )


def finish_kernel(
    sheet_ref, counts_ref, cols_ref, sticks_ref, back_ref, a_ref, bh_ref, bl_ref, th_ref, tl_ref, fold_ref,
    out_ref,
):
    sheet = sheet_ref[0]
    vnl = jnp.zeros((2 * STICKS, 256), F32)
    step = 2 * PCHUNK
    for at in range(0, NPROJ, step):
        here = slice(at, at + step)
        a_re, a_im = a_ref[:STICKS, here], a_ref[STICKS:, here]
        w_re, w_im = (
            jnp.concatenate(
                [
                    back_ref[row : row + 1, :]
                    for row in range(
                        ROWS * (part * BLOCKS + at // 128) + DEPTH,
                        ROWS * (part * BLOCKS + (at + step) // 128) + DEPTH,
                        ROWS,
                    )
                ],
                axis=1,
            )
            for part in range(2)
        )
        weighted = split(
            jnp.concatenate([a_re * w_re - a_im * w_im, a_re * w_im + a_im * w_re], axis=0)
        )
        vnl = vnl + dot3(weighted, (bh_ref[:, here], bl_ref[:, here]), NT)
    vnl = split(
        jnp.concatenate(
            [
                jnp.concatenate([vnl[:STICKS, :128], -vnl[STICKS:, 128:]], axis=1),
                jnp.concatenate([vnl[STICKS:, :128], vnl[:STICKS, 128:]], axis=1),
            ],
            axis=0,
        )
    )
    vnl = mul(vnl[0], fold_ref[...], NT) + mul(vnl[1], fold_ref[...], NT)
    back = jnp.concatenate([back_ref[every(plane), :] for plane in range(DEPTH)], axis=0)
    back = split(back.T)
    with_cos = dot3(back, (th_ref[:EDGE], tl_ref[:EDGE]), NN)
    with_sin = dot3(back, (th_ref[EDGE:], tl_ref[EDGE:]), NN)
    box_scale = 1.0 / float(EDGE) ** 3
    sums = (
        (with_cos[:STICKS] + with_sin[STICKS:]) * box_scale + vnl[:STICKS],
        (with_cos[STICKS:] - with_sin[:STICKS]) * box_scale + vnl[STICKS:],
    )
    gx, gy = own_lateral(cols_ref, sheet)
    gz = lax.broadcasted_iota(jnp.int32, (1, EDGE), 1)
    gz = jnp.where(gz < EDGE // 2, gz, gz - EDGE).astype(F32)
    kinetic = 2.0 * (((gx * gx + gy * gy) + gz * gz) / (EDGE * EDGE))
    for team in range(TEAMS):
        live = live_column(counts_ref, sheet, team)
        rows = slice(team * LINES, (team + 1) * LINES)
        for part in range(2):
            value = kinetic[rows] * sticks_ref[team, part] + sums[part][rows]
            out_ref[team, part] = jnp.where(live, value, 0.0)


def call(kernel, places, outs, scratch=(), flops=0, limit=20 << 20):
    kinds = {"s": pltpu.SMEM, "v": pltpu.VMEM, "h": pltpu.HBM}
    return pl.pallas_call(
        kernel,
        out_shape=outs,
        in_specs=[pl.BlockSpec(memory_space=kinds[place]) for place in places],
        out_specs=jax.tree.map(lambda _: pl.BlockSpec(memory_space=pltpu.VMEM), outs),
        scratch_shapes=list(scratch),
        compiler_params=pltpu.CompilerParams(vmem_limit_bytes=limit),
        cost_estimate=pl.CostEstimate(flops=flops, bytes_accessed=4 << 20, transcendentals=0),
    )


def shape(dims, dtype=F32):
    return jax.ShapeDtypeStruct(dims, dtype)


def make_places(sheet, cols, proj_atom, atom_pos, proj_radius):
    return call(
        place_kernel, "svhhh", (shape((2 * STICKS, NPROJ)), shape((2, NPROJ))),
        [
            pltpu.VMEM((1, NPROJ), jnp.int32),
            pltpu.VMEM((3, NATOM), F32),
            pltpu.VMEM((1, NPROJ), F32),
            pltpu.SemaphoreType.DMA((3,)),
        ],
        flops=2 << 30,
    )(sheet, cols, proj_atom.reshape(1, NPROJ), atom_pos, proj_radius.reshape(1, NPROJ))


def project(sheet, counts, sticks, places, proj_atom, proj_diag, dij):
    return call(
        project_kernel, "ssvvvvvvvvv",
        (shape((SHEETS * ROWS, 2 * STICKS)), shape((256, NPROJ), BF16), shape((256, NPROJ), BF16)),
        [pltpu.VMEM((2, NPROJ), F32), pltpu.VMEM((NATOM, NPROJ), BF16)],
        flops=3 << 30,
    )(
        sheet, counts, sticks, *split_table(depth_table()), fold_matrix(),
        proj_atom.reshape(1, NPROJ), proj_diag.reshape(1, NPROJ), dij.reshape(1, NPROJ), *places,
    )


def plane_work(cols, sticks, potential):
    tables = [piece for table in lateral_tables() for piece in split_table(table)]
    padded = jnp.pad(potential.reshape(DEPTH, EDGE, EDGE), ((0, 0), (0, 0), (0, 256 - EDGE)))
    return call(
        plane_kernel, "v" * 11, shape((SHEETS * ROWS, 2 * STICKS)),
        [
            pltpu.VMEM((2, SHEETS // 2, 128), jnp.int32),
            pltpu.VMEM((12, SHEETS // 2, 128), F32),
            pltpu.VMEM((CHUNKS, 256, CHUNK), BF16),
            pltpu.VMEM((2, 12 * HALF_ROWS, CHUNK), BF16),
            pltpu.VMEM((6, SHEETS // 2, 128), F32),
        ],
        flops=8 << 30,
        limit=28 << 20,
    )(cols, sticks, padded, *tables)


def finish(sheet, counts, cols, sticks, back, tables):
    return call(finish_kernel, "ssvvvvvvvvv", shape((TEAMS, 2, LINES, EDGE)), flops=3 << 30)(
        sheet, counts, cols, sticks, back, *tables, *split_table(depth_table()), fold_matrix()
    )


def over_sheets(rows):
    sent = rows.reshape(SHEETS, ROWS, 2 * STICKS)
    return lax.all_to_all(sent, "pw", split_axis=0, concat_axis=0, tiled=True).reshape(rows.shape)


def body(
    orbital_coefficients,
    potential,
    line_lateral_place,
    stick_count,
    proj_atom,
    atom_pos,
    proj_radius,
    proj_diag,
    ionic_pseudo_dij,
):
    sheet = lax.axis_index("pw").astype(jnp.int32).reshape(1)
    layout = line_lateral_place[: TEAMS * SHEETS * LINES].reshape(TEAMS, SHEETS, LINES)
    cols = jnp.transpose(layout, (1, 0, 2)).reshape(SHEETS, STICKS)
    sticks = lax.all_to_all(orbital_coefficients, "tg", split_axis=0, concat_axis=0, tiled=True)
    places = make_places(sheet, cols, proj_atom, atom_pos, proj_radius)
    by_depth, *factors = project(sheet, stick_count, sticks, places, proj_atom, proj_diag, ionic_pseudo_dij)
    by_plane = over_sheets(by_depth)
    picked = plane_work(cols, by_plane, potential)
    back = over_sheets(picked)
    done = finish(sheet, stick_count, cols, sticks, back, (places[0], *factors))
    return lax.all_to_all(done, "tg", split_axis=0, concat_axis=0, tiled=True)


def solution(mesh):
    return jax.shard_map(
        body,
        mesh=mesh,
        in_specs=(
            P(None, None, ("tg", "pw"), None),
            P("pw", None),
            P(),
            P(),
            P(),
            P(),
            P(),
            P(),
            P(),
        ),
        out_specs=P(None, None, ("tg", "pw"), None),
        check_vma=False,
    )
```

```python
import math

import jax
import jax.numpy as jnp
import numpy as np
from jax import lax
from jax.experimental import pallas as pl
from jax.experimental.pallas import tpu as pltpu
from jax.sharding import PartitionSpec as P

EDGE = 192
TEAMS = 8
SHEETS = 64
DEPTH = 3
ROWS = DEPTH + 1
LINES = 8
STICKS = TEAMS * LINES
NPROJ = 2048
NATOM = 512
CUT = 48
HALF_ROWS = 64
CHUNK = 1024
CHUNKS = SHEETS * STICKS // CHUNK
PCHUNK = 256
BLOCKS = NPROJ // 128

F32 = jnp.float32
BF16 = jnp.bfloat16

NN = (((1,), (0,)), ((), ()))
NT = (((1,), (1,)), ((), ()))


def split_table(table):
    high = table.astype(np.float32).astype(jnp.bfloat16)
    low = (table - high.astype(np.float64)).astype(np.float32).astype(jnp.bfloat16)
    return high, low


def depth_table():
    steps = np.arange(EDGE)
    planes = steps.reshape(SHEETS, DEPTH).T.reshape(-1)
    turns = (planes[:, None] * steps[None, :] % EDGE) * (2.0 * math.pi / EDGE)
    return np.concatenate([np.cos(turns), np.sin(turns)], axis=0)


def fold_matrix():
    fold = np.zeros((EDGE, 256))
    for z in range(EDGE):
        g = z if z < EDGE // 2 else z - EDGE
        fold[z, abs(g)] = 1.0
        fold[z, 128 + abs(g)] = np.sign(g)
    return fold.astype(jnp.bfloat16)


def column_phase(freqs, valid):
    turns = (freqs[:, None] * np.arange(EDGE)[None, :] % EDGE) * (2.0 * math.pi / EDGE)
    keep = valid[:, None].astype(np.float64)
    return np.cos(turns) * keep, np.sin(turns) * keep


def lateral_tables():
    spot = np.arange(2 * HALF_ROWS)
    y_cos, y_sin = column_phase(spot - CUT, spot <= 2 * CUT)
    pad = ((0, 0), (0, 256 - EDGE))
    y_cos, y_sin = np.pad(y_cos, pad), np.pad(y_sin, pad)
    y_inverse = np.block([[y_cos, y_sin], [-y_sin, y_cos]])
    x_spot = 2 * (spot % HALF_ROWS) + spot // HALF_ROWS
    x_cos, x_sin = column_phase(x_spot - CUT, x_spot <= 2 * CUT)
    x_forward = np.block([[x_cos, x_sin], [-x_sin, x_cos]])
    return y_inverse, x_forward.T, x_forward, y_inverse.T


def split(value):
    high = value.astype(BF16)
    return high, (value - high.astype(F32)).astype(BF16)


def mul(left, right, form):
    return lax.dot_general(left, right, form, preferred_element_type=F32)


def dot3(left, right, form):
    return mul(left[0], right[0], form) + mul(left[0], right[1], form) + mul(left[1], right[0], form)


def lateral_split(cols):
    x = (cols * 43691) >> 23
    y = cols - x * EDGE
    x = jnp.where(x < EDGE // 2, x, x - EDGE)
    y = jnp.where(y < EDGE // 2, y, y - EDGE)
    return x, y


def sincos_turns(turns):
    quarter = turns * 4.0
    near = jnp.floor(quarter + 0.5)
    x = (quarter - near) * (0.5 * math.pi)
    which = near.astype(jnp.int32) & 3
    xx = x * x
    sine = x * (1.0 + xx * (-1.0 / 6 + xx * (1.0 / 120 + xx * (-1.0 / 5040 + xx * (1.0 / 362880)))))
    cosine = 1.0 + xx * (-0.5 + xx * (1.0 / 24 + xx * (-1.0 / 720 + xx * (1.0 / 40320))))
    odd = (which & 1) == 1
    c = jnp.where(odd, sine, cosine)
    s = jnp.where(odd, cosine, sine)
    return jnp.where(((which + 1) & 2) == 2, -c, c), jnp.where((which & 2) == 2, -s, s)


def own_lateral(cols_ref, sheet):
    row = cols_ref[pl.ds(sheet, 1), :]
    x, y = lateral_split(row)
    eye = lax.broadcasted_iota(jnp.int32, (STICKS, STICKS), 0) == lax.broadcasted_iota(
        jnp.int32, (STICKS, STICKS), 1
    )

    def upright(value):
        wide = jnp.broadcast_to(value.astype(F32), (STICKS, STICKS))
        return jnp.sum(jnp.where(eye, wide, 0.0), axis=1, keepdims=True)

    return upright(x), upright(y)


def live_column(counts_ref, sheet, team):
    line = lax.broadcasted_iota(jnp.int32, (LINES, EDGE), 0)
    return line < counts_ref[team * SHEETS + sheet]


def live_sticks(sticks_ref, counts_ref, sheet):
    rows = []
    for part in range(2):
        for team in range(TEAMS):
            live = live_column(counts_ref, sheet, team)
            rows.append(jnp.where(live, sticks_ref[team, part], 0.0))
    return jnp.concatenate(rows, axis=0)


def member_of(atom_row):
    atoms = lax.broadcasted_iota(jnp.int32, (NATOM, atom_row.shape[1]), 0)
    return jnp.where(atoms == atom_row, 1.0, 0.0).astype(BF16)


def place_kernel(sheet_ref, cols_ref, atom_hbm, pos_hbm, radius_hbm, a_ref, place_ref, atom_ref, pos_ref, radius_ref, sem):
    loads = [
        pltpu.make_async_copy(source, target, sem.at[k])
        for k, (source, target) in enumerate(
            ((atom_hbm, atom_ref), (pos_hbm, pos_ref), (radius_hbm, radius_ref))
        )
    ]
    for load in loads:
        load.start()
    gx, gy = own_lateral(cols_ref, sheet_ref[0])
    gxy = gx * gx + gy * gy
    for load in loads:
        load.wait()
    pos = pos_ref[...]
    first = pos.astype(BF16).astype(F32)
    second = (pos - first).astype(BF16).astype(F32)
    third = (pos - first - second).astype(BF16).astype(F32)
    line = lax.broadcasted_iota(jnp.int32, (16, NATOM), 0)
    rows = jnp.zeros((16, NATOM), F32)
    for step, piece in enumerate((first, second, third)):
        for axis in range(3):
            rows = jnp.where(line == 3 * step + axis, piece[axis : axis + 1, :], rows)
    rows = rows.astype(BF16)
    for at in range(0, NPROJ, PCHUNK):
        here = slice(at, at + PCHUNK)
        placed = mul(rows, member_of(atom_ref[:, here]), NN)
        tx, ty, tz = (
            placed[axis : axis + 1] + placed[3 + axis : 4 + axis] + placed[6 + axis : 7 + axis]
            for axis in range(3)
        )
        spread = radius_ref[:, here] / (EDGE * EDGE)
        place_ref[0:1, here] = tz
        place_ref[1:2, here] = spread
        cosine, sine = sincos_turns(gx * tx + gy * ty)
        amp = jnp.exp(-spread * gxy)
        a_ref[:STICKS, here] = amp * cosine
        a_ref[STICKS:, here] = -amp * sine


def depth_factors(place_ref, bh_ref, bl_ref):
    low_g = lax.broadcasted_iota(jnp.int32, (8, PCHUNK), 0).astype(F32)
    for at in range(0, NPROJ, PCHUNK):
        here = slice(at, at + PCHUNK)
        tz, spread = place_ref[0:1, here], place_ref[1:2, here]
        low_c, low_s = sincos_turns(low_g * tz)
        for bank in range(2):
            high_g = lax.broadcasted_iota(jnp.int32, (8, PCHUNK), 0) * 8 + bank * 64
            high_c, high_s = sincos_turns(high_g.astype(F32) * tz)
            for pair in range(4):
                re_rows, im_rows = [], []
                for inner in range(2):
                    row = pair * 2 + inner
                    hc, hs = high_c[row : row + 1], high_s[row : row + 1]
                    g = low_g + float((bank * 8 + row) * 8)
                    amp_z = jnp.exp(-spread * (g * g))
                    re_rows.append(amp_z * (hc * low_c - hs * low_s))
                    im_rows.append(-amp_z * (hs * low_c + hc * low_s))
                z = (bank * 8 + pair * 2) * 8
                for base, found in ((z, re_rows), (128 + z, im_rows)):
                    high, low = split(jnp.concatenate(found, axis=0))
                    bh_ref[base : base + 16, here] = high
                    bl_ref[base : base + 16, here] = low


def rows_of(re, im):
    re_high = re.astype(BF16).astype(F32)
    im_high = im.astype(BF16).astype(F32)
    line = lax.broadcasted_iota(jnp.int32, (16, re.shape[1]), 0)
    rows = jnp.where(line == 0, re_high, 0.0)
    rows = jnp.where(line == 1, im_high, rows)
    rows = jnp.where(line == 2, re - re_high, rows)
    return jnp.where(line == 3, im - im_high, rows).astype(BF16)


def every(start):
    return pl.ds(start, SHEETS, stride=ROWS)


def project_kernel(
    sheet_ref, counts_ref, sticks_ref, th_ref, tl_ref, fold_ref, atom_ref, diag_ref, dij_ref, a_ref, place_ref,
    out_ref, bh_ref, bl_ref, becp_ref, mask_ref,
):
    depth_factors(place_ref, bh_ref, bl_ref)
    for at in range(0, NPROJ, PCHUNK):
        mask_ref[:, at : at + PCHUNK] = member_of(atom_ref[:, at : at + PCHUNK])
    coeff = split(live_sticks(sticks_ref, counts_ref, sheet_ref[0]))
    both = dot3((th_ref[...], tl_ref[...]), coeff, NT)
    with_cos, with_sin = both[:EDGE], both[EDGE:]
    by_depth = with_cos + jnp.concatenate([-with_sin[:, STICKS:], with_sin[:, :STICKS]], axis=1)
    folded = mul(coeff[0], fold_ref[...], NN) + mul(coeff[1], fold_ref[...], NN)
    paired = split(
        jnp.concatenate(
            [
                jnp.concatenate([folded[:STICKS, :128], folded[STICKS:, 128:]], axis=1),
                jnp.concatenate([folded[STICKS:, :128], -folded[:STICKS, 128:]], axis=1),
            ],
            axis=0,
        )
    )
    for plane in range(DEPTH):
        out_ref[every(plane), :] = by_depth[plane * SHEETS : (plane + 1) * SHEETS]
    out_ref[every(DEPTH), :] = jnp.zeros((SHEETS, 128), F32)
    for at in range(0, NPROJ, PCHUNK):
        here = slice(at, at + PCHUNK)
        y = dot3(paired, (bh_ref[:, here], bl_ref[:, here]), NN)
        y_re, y_im = y[:STICKS], y[STICKS:]
        a_re, a_im = a_ref[:STICKS, here], a_ref[STICKS:, here]
        becp_ref[0:1, here] = jnp.sum(a_re * y_re + a_im * y_im, axis=0, keepdims=True)
        becp_ref[1:2, here] = jnp.sum(a_re * y_im - a_im * y_re, axis=0, keepdims=True)
    scale = 1.0 / (math.sqrt(TEAMS * SHEETS * LINES * EDGE) * math.sqrt(NPROJ))
    re, im = becp_ref[0:1, :] * scale, becp_ref[1:2, :] * scale
    dij, diag = dij_ref[...], diag_ref[...]
    per_atom = mul(rows_of(re * dij, im * dij), mask_ref[...], NT)
    common = mul(
        rows_of(per_atom[0:1] + per_atom[2:3], per_atom[1:2] + per_atom[3:4]), mask_ref[...], NN
    )
    w = (
        re * diag + dij * (common[0:1] + common[2:3]),
        im * diag + dij * (common[1:2] + common[3:4]),
    )
    for part in range(2):
        for block in range(BLOCKS):
            row = ROWS * (part * BLOCKS + block) + DEPTH
            out_ref[row : row + 1, :] = w[part][:, block * 128 : (block + 1) * 128]


def plane_kernel(
    cols_ref, sticks_ref, potential_ref,
    yih_ref, yil_ref, xih_ref, xil_ref, xfh_ref, xfl_ref, yfh_ref, yfl_ref,
    out_ref, x_ref, v_ref, hot_ref, left_ref, pick_ref,
):
    half = SHEETS // 2
    x, y = lateral_split(jnp.concatenate([cols_ref[:half, :], cols_ref[half:, :]], axis=1))
    x, y = x + CUT, y + CUT
    x_ref[0] = x >> 1
    x_ref[1] = (x & 1) * 128 + y
    for plane in range(DEPTH):
        rows = sticks_ref[every(plane), :]
        top, bottom = rows[:half], rows[half:]
        for part in range(2):
            lanes = slice(part * STICKS, (part + 1) * STICKS)
            value = jnp.concatenate([top[:, lanes], bottom[:, lanes]], axis=1)
            high = value.astype(BF16).astype(F32)
            at = 2 * (2 * plane + part)
            v_ref[at] = high
            v_ref[at + 1] = value - high
    summed = jnp.sum(sticks_ref[every(DEPTH), :], axis=0, keepdims=True)
    out_ref[every(DEPTH), :] = jnp.broadcast_to(summed, (SHEETS, 128))
    rows64 = lax.broadcasted_iota(jnp.int32, (HALF_ROWS, 128), 0)
    half_rows = rows64.astype(F32).astype(BF16)
    full_rows = lax.broadcasted_iota(jnp.int32, (256, 128), 0).astype(F32).astype(BF16)
    one, zero = jnp.ones((), BF16), jnp.zeros((), BF16)

    def tall(row, height):
        packed = jnp.broadcast_to(row, (16, 128)).astype(BF16)
        return jnp.concatenate([packed] * (height // 16), axis=0)

    per = CHUNK // 128
    total = jnp.zeros((12 * HALF_ROWS, 256), F32)
    for chunk in range(CHUNKS):
        slot = chunk % 2
        for inner in range(per):
            r = chunk * per + inner
            lanes = slice(inner * 128, (inner + 1) * 128)
            spot = x_ref[:, r : r + 1, :].astype(F32)
            member = jnp.where(half_rows == tall(spot[0], HALF_ROWS), one, zero)
            hot_ref[chunk, :, lanes] = jnp.where(full_rows == tall(spot[1], 256), one, zero)
            for k in range(12):
                value = tall(v_ref[k, r : r + 1, :], HALF_ROWS)
                left_ref[slot, k * HALF_ROWS : (k + 1) * HALF_ROWS, lanes] = member * value
        total = total + mul(left_ref[slot], hot_ref[chunk], NT)
    grids = []
    for plane in range(DEPTH):
        parts = []
        for part in range(2):
            at = 2 * (2 * plane + part) * HALF_ROWS
            grid = total[at : at + HALF_ROWS] + total[at + HALF_ROWS : at + 2 * HALF_ROWS]
            parts.append(jnp.concatenate([grid[:, :128], grid[:, 128:]], axis=0))
        grids.append(jnp.concatenate(parts, axis=1))
    work = jnp.concatenate(grids, axis=0)
    work = dot3(split(work), (yih_ref[...], yil_ref[...]), NN)
    work = jnp.concatenate(
        [
            jnp.concatenate(
                [work[p * 128 : (p + 1) * 128, :256], work[p * 128 : (p + 1) * 128, 256:]], axis=0
            )
            for p in range(DEPTH)
        ],
        axis=1,
    )
    work = dot3((xih_ref[...], xil_ref[...]), split(work), NN)
    local = jnp.concatenate([potential_ref[p] for p in range(DEPTH)], axis=1)
    work = jnp.concatenate([work[:EDGE] * local, work[EDGE:] * local], axis=0)
    work = dot3((xfh_ref[...], xfl_ref[...]), split(work), NN)
    work = jnp.concatenate(
        [
            jnp.concatenate(
                [work[:128, p * 256 : (p + 1) * 256], work[128:, p * 256 : (p + 1) * 256]], axis=1
            )
            for p in range(DEPTH)
        ],
        axis=0,
    )
    work = dot3(split(work), (yfh_ref[...], yfl_ref[...]), NN)
    pieces = []
    for p in range(DEPTH):
        for c in range(2):
            block = work[p * 128 : (p + 1) * 128, c * 128 : (c + 1) * 128]
            pieces.append(jnp.concatenate([block[:HALF_ROWS], block[HALF_ROWS:]], axis=1))
    high, low = split(jnp.concatenate(pieces, axis=0))
    for chunk in range(CHUNKS):
        hot = hot_ref[chunk]
        found = mul(high, hot, NN) + mul(low, hot, NN)
        for inner in range(per):
            r = chunk * per + inner
            lanes = slice(inner * 128, (inner + 1) * 128)
            member = rows64 == x_ref[0, r : r + 1, :]
            for k in range(6):
                pick_ref[k, r : r + 1, :] = jnp.sum(
                    jnp.where(member, found[k * HALF_ROWS : (k + 1) * HALF_ROWS, lanes], 0.0),
                    axis=0,
                    keepdims=True,
                )
    for plane in range(DEPTH):
        re, im = pick_ref[2 * plane], pick_ref[2 * plane + 1]
        out_ref[every(plane), :] = jnp.concatenate(
            [
                jnp.concatenate([re[:, :STICKS], im[:, :STICKS]], axis=1),
                jnp.concatenate([re[:, STICKS:], im[:, STICKS:]], axis=1),
            ],
            axis=0,
        )


def finish_kernel(
    sheet_ref, counts_ref, cols_ref, sticks_ref, back_ref, a_ref, place_ref, th_ref, tl_ref, fold_ref,
    out_ref, bh_ref, bl_ref,
):
    sheet = sheet_ref[0]
    depth_factors(place_ref, bh_ref, bl_ref)
    vnl = jnp.zeros((2 * STICKS, 256), F32)
    step = 2 * PCHUNK
    for at in range(0, NPROJ, step):
        here = slice(at, at + step)
        a_re, a_im = a_ref[:STICKS, here], a_ref[STICKS:, here]
        w_re, w_im = (
            jnp.concatenate(
                [
                    back_ref[row : row + 1, :]
                    for row in range(
                        ROWS * (part * BLOCKS + at // 128) + DEPTH,
                        ROWS * (part * BLOCKS + (at + step) // 128) + DEPTH,
                        ROWS,
                    )
                ],
                axis=1,
            )
            for part in range(2)
        )
        weighted = split(
            jnp.concatenate([a_re * w_re - a_im * w_im, a_re * w_im + a_im * w_re], axis=0)
        )
        vnl = vnl + dot3(weighted, (bh_ref[:, here], bl_ref[:, here]), NT)
    vnl = split(
        jnp.concatenate(
            [
                jnp.concatenate([vnl[:STICKS, :128], -vnl[STICKS:, 128:]], axis=1),
                jnp.concatenate([vnl[STICKS:, :128], vnl[:STICKS, 128:]], axis=1),
            ],
            axis=0,
        )
    )
    vnl = mul(vnl[0], fold_ref[...], NT) + mul(vnl[1], fold_ref[...], NT)
    back = jnp.concatenate([back_ref[every(plane), :] for plane in range(DEPTH)], axis=0)
    back = split(back.T)
    with_cos = dot3(back, (th_ref[:EDGE], tl_ref[:EDGE]), NN)
    with_sin = dot3(back, (th_ref[EDGE:], tl_ref[EDGE:]), NN)
    box_scale = 1.0 / float(EDGE) ** 3
    sums = (
        (with_cos[:STICKS] + with_sin[STICKS:]) * box_scale + vnl[:STICKS],
        (with_cos[STICKS:] - with_sin[:STICKS]) * box_scale + vnl[STICKS:],
    )
    gx, gy = own_lateral(cols_ref, sheet)
    gz = lax.broadcasted_iota(jnp.int32, (1, EDGE), 1)
    gz = jnp.where(gz < EDGE // 2, gz, gz - EDGE).astype(F32)
    kinetic = 2.0 * (((gx * gx + gy * gy) + gz * gz) / (EDGE * EDGE))
    for team in range(TEAMS):
        live = live_column(counts_ref, sheet, team)
        rows = slice(team * LINES, (team + 1) * LINES)
        for part in range(2):
            value = kinetic[rows] * sticks_ref[team, part] + sums[part][rows]
            out_ref[team, part] = jnp.where(live, value, 0.0)


def call(kernel, places, outs, scratch=(), flops=0, limit=20 << 20):
    kinds = {"s": pltpu.SMEM, "v": pltpu.VMEM, "h": pltpu.HBM}
    return pl.pallas_call(
        kernel,
        out_shape=outs,
        in_specs=[pl.BlockSpec(memory_space=kinds[place]) for place in places],
        out_specs=jax.tree.map(lambda _: pl.BlockSpec(memory_space=pltpu.VMEM), outs),
        scratch_shapes=list(scratch),
        compiler_params=pltpu.CompilerParams(vmem_limit_bytes=limit),
        cost_estimate=pl.CostEstimate(flops=flops, bytes_accessed=4 << 20, transcendentals=0),
    )


def shape(dims, dtype=F32):
    return jax.ShapeDtypeStruct(dims, dtype)


def make_places(sheet, cols, proj_atom, atom_pos, proj_radius):
    return call(
        place_kernel, "svhhh", (shape((2 * STICKS, NPROJ)), shape((2, NPROJ))),
        [
            pltpu.VMEM((1, NPROJ), jnp.int32),
            pltpu.VMEM((3, NATOM), F32),
            pltpu.VMEM((1, NPROJ), F32),
            pltpu.SemaphoreType.DMA((3,)),
        ],
        flops=2 << 30,
    )(sheet, cols, proj_atom.reshape(1, NPROJ), atom_pos, proj_radius.reshape(1, NPROJ))


FACTORS = [pltpu.VMEM((256, NPROJ), BF16)] * 2


def project(sheet, counts, sticks, places, proj_atom, proj_diag, dij):
    return call(
        project_kernel, "ssvvvvvvvvv", shape((SHEETS * ROWS, 2 * STICKS)),
        [*FACTORS, pltpu.VMEM((2, NPROJ), F32), pltpu.VMEM((NATOM, NPROJ), BF16)],
        flops=3 << 30,
    )(
        sheet, counts, sticks, *split_table(depth_table()), fold_matrix(),
        proj_atom.reshape(1, NPROJ), proj_diag.reshape(1, NPROJ), dij.reshape(1, NPROJ), *places,
    )


def plane_work(cols, sticks, potential):
    tables = [piece for table in lateral_tables() for piece in split_table(table)]
    padded = jnp.pad(potential.reshape(DEPTH, EDGE, EDGE), ((0, 0), (0, 0), (0, 256 - EDGE)))
    return call(
        plane_kernel, "v" * 11, shape((SHEETS * ROWS, 2 * STICKS)),
        [
            pltpu.VMEM((2, SHEETS // 2, 128), jnp.int32),
            pltpu.VMEM((12, SHEETS // 2, 128), F32),
            pltpu.VMEM((CHUNKS, 256, CHUNK), BF16),
            pltpu.VMEM((2, 12 * HALF_ROWS, CHUNK), BF16),
            pltpu.VMEM((6, SHEETS // 2, 128), F32),
        ],
        flops=8 << 30,
        limit=28 << 20,
    )(cols, sticks, padded, *tables)


def finish(sheet, counts, cols, sticks, back, places):
    return call(finish_kernel, "ssvvvvvvvv", shape((TEAMS, 2, LINES, EDGE)), FACTORS, flops=3 << 30)(
        sheet, counts, cols, sticks, back, *places, *split_table(depth_table()), fold_matrix()
    )


def over_sheets(rows):
    sent = rows.reshape(SHEETS, ROWS, 2 * STICKS)
    return lax.all_to_all(sent, "pw", split_axis=0, concat_axis=0, tiled=True).reshape(rows.shape)


def body(
    orbital_coefficients,
    potential,
    line_lateral_place,
    stick_count,
    proj_atom,
    atom_pos,
    proj_radius,
    proj_diag,
    ionic_pseudo_dij,
):
    sheet = lax.axis_index("pw").astype(jnp.int32).reshape(1)
    layout = line_lateral_place[: TEAMS * SHEETS * LINES].reshape(TEAMS, SHEETS, LINES)
    cols = jnp.transpose(layout, (1, 0, 2)).reshape(SHEETS, STICKS)
    sticks = lax.all_to_all(orbital_coefficients, "tg", split_axis=0, concat_axis=0, tiled=True)
    places = make_places(sheet, cols, proj_atom, atom_pos, proj_radius)
    by_depth = project(sheet, stick_count, sticks, places, proj_atom, proj_diag, ionic_pseudo_dij)
    by_plane = over_sheets(by_depth)
    picked = plane_work(cols, by_plane, potential)
    back = over_sheets(picked)
    done = finish(sheet, stick_count, cols, sticks, back, places)
    return lax.all_to_all(done, "tg", split_axis=0, concat_axis=0, tiled=True)


def solution(mesh):
    return jax.shard_map(
        body,
        mesh=mesh,
        in_specs=(
            P(None, None, ("tg", "pw"), None),
            P("pw", None),
            P(),
            P(),
            P(),
            P(),
            P(),
            P(),
            P(),
        ),
        out_specs=P(None, None, ("tg", "pw"), None),
        check_vma=False,
    )
```

```python
import math

import jax
import jax.numpy as jnp
import numpy as np
from jax import lax
from jax.experimental import pallas as pl
from jax.experimental.pallas import tpu as pltpu
from jax.sharding import PartitionSpec as P

EDGE = 192
TEAMS = 8
SHEETS = 64
DEPTH = 3
ROWS = DEPTH + 1
LINES = 8
STICKS = TEAMS * LINES
NPROJ = 2048
NATOM = 512
CUT = 48
HALF_ROWS = 48
CHUNK = 1024
CHUNKS = SHEETS * STICKS // CHUNK
PCHUNK = 256
BLOCKS = NPROJ // 128

F32 = jnp.float32
BF16 = jnp.bfloat16

NN = (((1,), (0,)), ((), ()))
NT = (((1,), (1,)), ((), ()))


def split_table(table):
    high = table.astype(np.float32).astype(jnp.bfloat16)
    low = (table - high.astype(np.float64)).astype(np.float32).astype(jnp.bfloat16)
    return high, low


def depth_table():
    steps = np.arange(EDGE)
    planes = steps.reshape(SHEETS, DEPTH).T.reshape(-1)
    turns = (planes[:, None] * steps[None, :] % EDGE) * (2.0 * math.pi / EDGE)
    return np.concatenate([np.cos(turns), np.sin(turns)], axis=0)


def fold_matrix():
    fold = np.zeros((EDGE, 256))
    for z in range(EDGE):
        g = z if z < EDGE // 2 else z - EDGE
        fold[z, abs(g)] = 1.0
        fold[z, 128 + abs(g)] = np.sign(g)
    return fold.astype(jnp.bfloat16)


def column_phase(freqs, valid):
    turns = (freqs[:, None] * np.arange(EDGE)[None, :] % EDGE) * (2.0 * math.pi / EDGE)
    keep = valid[:, None].astype(np.float64)
    return np.cos(turns) * keep, np.sin(turns) * keep


def lateral_tables():
    spot = np.arange(128)
    y_cos, y_sin = column_phase(spot - CUT, spot <= 2 * CUT)
    pad = ((0, 0), (0, 256 - EDGE))
    y_cos, y_sin = np.pad(y_cos, pad), np.pad(y_sin, pad)
    y_inverse = np.block([[y_cos, y_sin], [-y_sin, y_cos]])
    x_spot = np.where(spot < 2 * HALF_ROWS, 2 * (spot % HALF_ROWS) + spot // HALF_ROWS, spot)
    x_cos, x_sin = column_phase(x_spot - CUT, x_spot <= 2 * CUT)
    x_forward = np.block([[x_cos, x_sin], [-x_sin, x_cos]])
    return y_inverse, x_forward.T, x_forward, y_inverse.T


def split(value):
    high = value.astype(BF16)
    return high, (value - high.astype(F32)).astype(BF16)


def mul(left, right, form):
    return lax.dot_general(left, right, form, preferred_element_type=F32)


def dot3(left, right, form):
    return mul(left[0], right[0], form) + mul(left[0], right[1], form) + mul(left[1], right[0], form)


def lateral_split(cols):
    x = (cols * 43691) >> 23
    y = cols - x * EDGE
    x = jnp.where(x < EDGE // 2, x, x - EDGE)
    y = jnp.where(y < EDGE // 2, y, y - EDGE)
    return x, y


def sincos_turns(turns):
    quarter = turns * 4.0
    near = jnp.floor(quarter + 0.5)
    x = (quarter - near) * (0.5 * math.pi)
    which = near.astype(jnp.int32) & 3
    xx = x * x
    sine = x * (1.0 + xx * (-1.0 / 6 + xx * (1.0 / 120 + xx * (-1.0 / 5040 + xx * (1.0 / 362880)))))
    cosine = 1.0 + xx * (-0.5 + xx * (1.0 / 24 + xx * (-1.0 / 720 + xx * (1.0 / 40320))))
    odd = (which & 1) == 1
    c = jnp.where(odd, sine, cosine)
    s = jnp.where(odd, cosine, sine)
    return jnp.where(((which + 1) & 2) == 2, -c, c), jnp.where((which & 2) == 2, -s, s)


def own_lateral(cols_ref, sheet):
    row = cols_ref[pl.ds(sheet, 1), :]
    x, y = lateral_split(row)
    eye = lax.broadcasted_iota(jnp.int32, (STICKS, STICKS), 0) == lax.broadcasted_iota(
        jnp.int32, (STICKS, STICKS), 1
    )

    def upright(value):
        wide = jnp.broadcast_to(value.astype(F32), (STICKS, STICKS))
        return jnp.sum(jnp.where(eye, wide, 0.0), axis=1, keepdims=True)

    return upright(x), upright(y)


def live_sticks(sticks_ref, live_ref):
    rows = []
    for part in range(2):
        for team in range(TEAMS):
            live = live_ref[team * LINES : (team + 1) * LINES, :1] > 0.5
            rows.append(jnp.where(live, sticks_ref[team, part], 0.0))
    return jnp.concatenate(rows, axis=0)


def member_of(atom_row):
    atoms = lax.broadcasted_iota(jnp.int32, (NATOM, atom_row.shape[1]), 0)
    return jnp.where(atoms == atom_row, 1.0, 0.0).astype(BF16)


def place_kernel(
    sheet_ref, counts_ref, cols_ref, atom_hbm, pos_hbm, radius_hbm,
    a_ref, place_ref, live_ref, atom_ref, pos_ref, radius_ref, sem,
):
    loads = [
        pltpu.make_async_copy(source, target, sem.at[k])
        for k, (source, target) in enumerate(
            ((atom_hbm, atom_ref), (pos_hbm, pos_ref), (radius_hbm, radius_ref))
        )
    ]
    for load in loads:
        load.start()
    for team in range(TEAMS):
        line = lax.broadcasted_iota(jnp.int32, (LINES, 128), 0)
        live = line < counts_ref[team * SHEETS + sheet_ref[0]]
        live_ref[team * LINES : (team + 1) * LINES, :] = jnp.where(live, 1.0, 0.0)
    gx, gy = own_lateral(cols_ref, sheet_ref[0])
    gxy = gx * gx + gy * gy
    for load in loads:
        load.wait()
    pos = pos_ref[...]
    first = pos.astype(BF16).astype(F32)
    second = (pos - first).astype(BF16).astype(F32)
    third = (pos - first - second).astype(BF16).astype(F32)
    line = lax.broadcasted_iota(jnp.int32, (16, NATOM), 0)
    rows = jnp.zeros((16, NATOM), F32)
    for step, piece in enumerate((first, second, third)):
        for axis in range(3):
            rows = jnp.where(line == 3 * step + axis, piece[axis : axis + 1, :], rows)
    rows = rows.astype(BF16)
    for at in range(0, NPROJ, PCHUNK):
        here = slice(at, at + PCHUNK)
        placed = mul(rows, member_of(atom_ref[:, here]), NN)
        tx, ty, tz = (
            placed[axis : axis + 1] + placed[3 + axis : 4 + axis] + placed[6 + axis : 7 + axis]
            for axis in range(3)
        )
        spread = radius_ref[:, here] / (EDGE * EDGE)
        place_ref[0:1, here] = tz
        place_ref[1:2, here] = spread
        cosine, sine = sincos_turns(gx * tx + gy * ty)
        amp = jnp.exp(-spread * gxy)
        a_ref[:STICKS, here] = amp * cosine
        a_ref[STICKS:, here] = -amp * sine


def depth_factors(place_ref, bh_ref, bl_ref):
    low_g = lax.broadcasted_iota(jnp.int32, (8, PCHUNK), 0).astype(F32)
    for at in range(0, NPROJ, PCHUNK):
        here = slice(at, at + PCHUNK)
        tz, spread = place_ref[0:1, here], place_ref[1:2, here]
        low_c, low_s = sincos_turns(low_g * tz)
        for bank in range(2):
            high_g = lax.broadcasted_iota(jnp.int32, (8, PCHUNK), 0) * 8 + bank * 64
            high_c, high_s = sincos_turns(high_g.astype(F32) * tz)
            for pair in range(4):
                re_rows, im_rows = [], []
                for inner in range(2):
                    row = pair * 2 + inner
                    hc, hs = high_c[row : row + 1], high_s[row : row + 1]
                    g = low_g + float((bank * 8 + row) * 8)
                    amp_z = jnp.exp(-spread * (g * g))
                    re_rows.append(amp_z * (hc * low_c - hs * low_s))
                    im_rows.append(-amp_z * (hs * low_c + hc * low_s))
                z = (bank * 8 + pair * 2) * 8
                for base, found in ((z, re_rows), (128 + z, im_rows)):
                    high, low = split(jnp.concatenate(found, axis=0))
                    bh_ref[base : base + 16, here] = high
                    bl_ref[base : base + 16, here] = low


def rows_of(re, im):
    re_high = re.astype(BF16).astype(F32)
    im_high = im.astype(BF16).astype(F32)
    line = lax.broadcasted_iota(jnp.int32, (16, re.shape[1]), 0)
    rows = jnp.where(line == 0, re_high, 0.0)
    rows = jnp.where(line == 1, im_high, rows)
    rows = jnp.where(line == 2, re - re_high, rows)
    return jnp.where(line == 3, im - im_high, rows).astype(BF16)


def every(start):
    return pl.ds(start, SHEETS, stride=ROWS)


def project_kernel(
    sticks_ref, th_ref, tl_ref, fold_ref, atom_ref, diag_ref, dij_ref, a_ref, place_ref, live_ref,
    out_ref, bh_ref, bl_ref, becp_ref, mask_ref,
):
    depth_factors(place_ref, bh_ref, bl_ref)
    for at in range(0, NPROJ, PCHUNK):
        mask_ref[:, at : at + PCHUNK] = member_of(atom_ref[:, at : at + PCHUNK])
    coeff = split(live_sticks(sticks_ref, live_ref))
    both = dot3((th_ref[...], tl_ref[...]), coeff, NT)
    with_cos, with_sin = both[:EDGE], both[EDGE:]
    by_depth = with_cos + jnp.concatenate([-with_sin[:, STICKS:], with_sin[:, :STICKS]], axis=1)
    folded = mul(coeff[0], fold_ref[...], NN) + mul(coeff[1], fold_ref[...], NN)
    paired = split(
        jnp.concatenate(
            [
                jnp.concatenate([folded[:STICKS, :128], folded[STICKS:, 128:]], axis=1),
                jnp.concatenate([folded[STICKS:, :128], -folded[:STICKS, 128:]], axis=1),
            ],
            axis=0,
        )
    )
    for plane in range(DEPTH):
        out_ref[every(plane), :] = by_depth[plane * SHEETS : (plane + 1) * SHEETS]
    out_ref[every(DEPTH), :] = jnp.zeros((SHEETS, 128), F32)
    for at in range(0, NPROJ, PCHUNK):
        here = slice(at, at + PCHUNK)
        y = dot3(paired, (bh_ref[:, here], bl_ref[:, here]), NN)
        y_re, y_im = y[:STICKS], y[STICKS:]
        a_re, a_im = a_ref[:STICKS, here], a_ref[STICKS:, here]
        becp_ref[0:1, here] = jnp.sum(a_re * y_re + a_im * y_im, axis=0, keepdims=True)
        becp_ref[1:2, here] = jnp.sum(a_re * y_im - a_im * y_re, axis=0, keepdims=True)
    scale = 1.0 / (math.sqrt(TEAMS * SHEETS * LINES * EDGE) * math.sqrt(NPROJ))
    re, im = becp_ref[0:1, :] * scale, becp_ref[1:2, :] * scale
    dij, diag = dij_ref[...], diag_ref[...]
    per_atom = mul(rows_of(re * dij, im * dij), mask_ref[...], NT)
    common = mul(
        rows_of(per_atom[0:1] + per_atom[2:3], per_atom[1:2] + per_atom[3:4]), mask_ref[...], NN
    )
    w = (
        re * diag + dij * (common[0:1] + common[2:3]),
        im * diag + dij * (common[1:2] + common[3:4]),
    )
    for part in range(2):
        for block in range(BLOCKS):
            row = ROWS * (part * BLOCKS + block) + DEPTH
            out_ref[row : row + 1, :] = w[part][:, block * 128 : (block + 1) * 128]


def plane_kernel(
    cols_ref, sticks_ref, potential_ref,
    yih_ref, yil_ref, xih_ref, xil_ref, xfh_ref, xfl_ref, yfh_ref, yfl_ref,
    out_ref, x_ref, v_ref, hot_ref, left_ref, pick_ref,
):
    half = SHEETS // 2
    x, y = lateral_split(jnp.concatenate([cols_ref[:half, :], cols_ref[half:, :]], axis=1))
    x, y = x + CUT, y + CUT
    x_ref[0] = x >> 1
    x_ref[1] = (x & 1) * 128 + y
    for plane in range(DEPTH):
        rows = sticks_ref[every(plane), :]
        top, bottom = rows[:half], rows[half:]
        for part in range(2):
            lanes = slice(part * STICKS, (part + 1) * STICKS)
            value = jnp.concatenate([top[:, lanes], bottom[:, lanes]], axis=1)
            high = value.astype(BF16).astype(F32)
            at = 2 * (2 * plane + part)
            v_ref[at] = high
            v_ref[at + 1] = value - high
    summed = jnp.sum(sticks_ref[every(DEPTH), :], axis=0, keepdims=True)
    out_ref[every(DEPTH), :] = jnp.broadcast_to(summed, (SHEETS, 128))
    row_of = lax.broadcasted_iota(jnp.int32, (HALF_ROWS, 128), 0)
    half_rows = row_of.astype(F32).astype(BF16)
    full_rows = lax.broadcasted_iota(jnp.int32, (256, 128), 0).astype(F32).astype(BF16)
    one, zero = jnp.ones((), BF16), jnp.zeros((), BF16)

    def tall(row, height):
        packed = jnp.broadcast_to(row, (16, 128)).astype(BF16)
        return jnp.concatenate([packed] * (height // 16), axis=0)

    per = CHUNK // 128
    total = jnp.zeros((12 * HALF_ROWS, 256), F32)
    for chunk in range(CHUNKS):
        slot = chunk % 2
        for inner in range(per):
            r = chunk * per + inner
            lanes = slice(inner * 128, (inner + 1) * 128)
            spot = x_ref[:, r : r + 1, :].astype(F32)
            member = jnp.where(half_rows == tall(spot[0], HALF_ROWS), one, zero)
            hot_ref[chunk, :, lanes] = jnp.where(full_rows == tall(spot[1], 256), one, zero)
            for k in range(12):
                value = tall(v_ref[k, r : r + 1, :], HALF_ROWS)
                left_ref[slot, k * HALF_ROWS : (k + 1) * HALF_ROWS, lanes] = member * value
        total = total + mul(left_ref[slot], hot_ref[chunk], NT)
    lone = x_ref[0] == HALF_ROWS
    lone_spot = (lax.broadcasted_iota(jnp.int32, (32, 128), 0) == 0) & (
        lax.broadcasted_iota(jnp.int32, (32, 128), 1) == CUT
    )

    def whole(value):
        return jnp.sum(jnp.sum(value, axis=0, keepdims=True), axis=1, keepdims=True)

    grids = []
    for plane in range(DEPTH):
        parts = []
        for part in range(2):
            at = 2 * (2 * plane + part) * HALF_ROWS
            grid = total[at : at + HALF_ROWS] + total[at + HALF_ROWS : at + 2 * HALF_ROWS]
            at = 2 * (2 * plane + part)
            extra = whole(jnp.where(lone, v_ref[at] + v_ref[at + 1], 0.0))
            extra = jnp.where(lone_spot, extra, 0.0)
            parts.append(jnp.concatenate([grid[:, :128], grid[:, 128:], extra], axis=0))
        grids.append(jnp.concatenate(parts, axis=1))
    work = jnp.concatenate(grids, axis=0)
    work = dot3(split(work), (yih_ref[...], yil_ref[...]), NN)
    work = jnp.concatenate(
        [
            jnp.concatenate(
                [work[p * 128 : (p + 1) * 128, :256], work[p * 128 : (p + 1) * 128, 256:]], axis=0
            )
            for p in range(DEPTH)
        ],
        axis=1,
    )
    work = dot3((xih_ref[...], xil_ref[...]), split(work), NN)
    local = jnp.concatenate([potential_ref[p] for p in range(DEPTH)], axis=1)
    work = jnp.concatenate([work[:EDGE] * local, work[EDGE:] * local], axis=0)
    work = dot3((xfh_ref[...], xfl_ref[...]), split(work), NN)
    work = jnp.concatenate(
        [
            jnp.concatenate(
                [work[:128, p * 256 : (p + 1) * 256], work[128:, p * 256 : (p + 1) * 256]], axis=1
            )
            for p in range(DEPTH)
        ],
        axis=0,
    )
    work = dot3(split(work), (yfh_ref[...], yfl_ref[...]), NN)
    pieces, extras = [], []
    for p in range(DEPTH):
        for c in range(2):
            block = work[p * 128 : (p + 1) * 128, c * 128 : (c + 1) * 128]
            pieces.append(
                jnp.concatenate([block[:HALF_ROWS], block[HALF_ROWS : 2 * HALF_ROWS]], axis=1)
            )
            extras.append(whole(jnp.where(lone_spot, block[2 * HALF_ROWS :], 0.0)))
    high, low = split(jnp.concatenate(pieces, axis=0))
    for chunk in range(CHUNKS):
        hot = hot_ref[chunk]
        found = mul(high, hot, NN) + mul(low, hot, NN)
        for inner in range(per):
            r = chunk * per + inner
            lanes = slice(inner * 128, (inner + 1) * 128)
            member = row_of == x_ref[0, r : r + 1, :]
            for k in range(6):
                pick_ref[k, r : r + 1, :] = jnp.sum(
                    jnp.where(member, found[k * HALF_ROWS : (k + 1) * HALF_ROWS, lanes], 0.0),
                    axis=0,
                    keepdims=True,
                )
    for plane in range(DEPTH):
        re = pick_ref[2 * plane] + jnp.where(lone, extras[2 * plane], 0.0)
        im = pick_ref[2 * plane + 1] + jnp.where(lone, extras[2 * plane + 1], 0.0)
        out_ref[every(plane), :] = jnp.concatenate(
            [
                jnp.concatenate([re[:, :STICKS], im[:, :STICKS]], axis=1),
                jnp.concatenate([re[:, STICKS:], im[:, STICKS:]], axis=1),
            ],
            axis=0,
        )


def finish_kernel(
    sheet_ref, cols_ref, sticks_ref, back_ref, a_ref, place_ref, live_ref, th_ref, tl_ref, fold_ref,
    out_ref, bh_ref, bl_ref,
):
    sheet = sheet_ref[0]
    depth_factors(place_ref, bh_ref, bl_ref)
    vnl = jnp.zeros((2 * STICKS, 256), F32)
    step = 2 * PCHUNK
    for at in range(0, NPROJ, step):
        here = slice(at, at + step)
        a_re, a_im = a_ref[:STICKS, here], a_ref[STICKS:, here]
        w_re, w_im = (
            jnp.concatenate(
                [
                    back_ref[row : row + 1, :]
                    for row in range(
                        ROWS * (part * BLOCKS + at // 128) + DEPTH,
                        ROWS * (part * BLOCKS + (at + step) // 128) + DEPTH,
                        ROWS,
                    )
                ],
                axis=1,
            )
            for part in range(2)
        )
        weighted = split(
            jnp.concatenate([a_re * w_re - a_im * w_im, a_re * w_im + a_im * w_re], axis=0)
        )
        vnl = vnl + dot3(weighted, (bh_ref[:, here], bl_ref[:, here]), NT)
    vnl = split(
        jnp.concatenate(
            [
                jnp.concatenate([vnl[:STICKS, :128], -vnl[STICKS:, 128:]], axis=1),
                jnp.concatenate([vnl[STICKS:, :128], vnl[:STICKS, 128:]], axis=1),
            ],
            axis=0,
        )
    )
    vnl = mul(vnl[0], fold_ref[...], NT) + mul(vnl[1], fold_ref[...], NT)
    back = jnp.concatenate([back_ref[every(plane), :] for plane in range(DEPTH)], axis=0)
    back = split(back.T)
    with_cos = dot3(back, (th_ref[:EDGE], tl_ref[:EDGE]), NN)
    with_sin = dot3(back, (th_ref[EDGE:], tl_ref[EDGE:]), NN)
    box_scale = 1.0 / float(EDGE) ** 3
    sums = (
        (with_cos[:STICKS] + with_sin[STICKS:]) * box_scale + vnl[:STICKS],
        (with_cos[STICKS:] - with_sin[:STICKS]) * box_scale + vnl[STICKS:],
    )
    gx, gy = own_lateral(cols_ref, sheet)
    gz = lax.broadcasted_iota(jnp.int32, (1, EDGE), 1)
    gz = jnp.where(gz < EDGE // 2, gz, gz - EDGE).astype(F32)
    kinetic = 2.0 * (((gx * gx + gy * gy) + gz * gz) / (EDGE * EDGE))
    for team in range(TEAMS):
        rows = slice(team * LINES, (team + 1) * LINES)
        live = live_ref[rows, :1] > 0.5
        for part in range(2):
            value = kinetic[rows] * sticks_ref[team, part] + sums[part][rows]
            out_ref[team, part] = jnp.where(live, value, 0.0)


def call(kernel, places, outs, scratch=(), flops=0, limit=20 << 20):
    kinds = {"s": pltpu.SMEM, "v": pltpu.VMEM, "h": pltpu.HBM}
    return pl.pallas_call(
        kernel,
        out_shape=outs,
        in_specs=[pl.BlockSpec(memory_space=kinds[place]) for place in places],
        out_specs=jax.tree.map(lambda _: pl.BlockSpec(memory_space=pltpu.VMEM), outs),
        scratch_shapes=list(scratch),
        compiler_params=pltpu.CompilerParams(vmem_limit_bytes=limit),
        cost_estimate=pl.CostEstimate(flops=flops, bytes_accessed=4 << 20, transcendentals=0),
    )


def shape(dims, dtype=F32):
    return jax.ShapeDtypeStruct(dims, dtype)


def make_places(sheet, counts, cols, proj_atom, atom_pos, proj_radius):
    return call(
        place_kernel, "ssvhhh", (shape((2 * STICKS, NPROJ)), shape((2, NPROJ)), shape((STICKS, 128))),
        [
            pltpu.VMEM((1, NPROJ), jnp.int32),
            pltpu.VMEM((3, NATOM), F32),
            pltpu.VMEM((1, NPROJ), F32),
            pltpu.SemaphoreType.DMA((3,)),
        ],
        flops=2 << 30,
    )(sheet, counts, cols, proj_atom.reshape(1, NPROJ), atom_pos, proj_radius.reshape(1, NPROJ))


FACTORS = [pltpu.VMEM((256, NPROJ), BF16)] * 2


def project(sticks, places, proj_atom, proj_diag, dij):
    return call(
        project_kernel, "v" * 10, shape((SHEETS * ROWS, 2 * STICKS)),
        [*FACTORS, pltpu.VMEM((2, NPROJ), F32), pltpu.VMEM((NATOM, NPROJ), BF16)],
        flops=3 << 30,
    )(
        sticks, *split_table(depth_table()), fold_matrix(),
        proj_atom.reshape(1, NPROJ), proj_diag.reshape(1, NPROJ), dij.reshape(1, NPROJ), *places,
    )


def plane_work(cols, sticks, potential):
    tables = [piece for table in lateral_tables() for piece in split_table(table)]
    padded = jnp.pad(potential.reshape(DEPTH, EDGE, EDGE), ((0, 0), (0, 0), (0, 256 - EDGE)))
    return call(
        plane_kernel, "v" * 11, shape((SHEETS * ROWS, 2 * STICKS)),
        [
            pltpu.VMEM((2, SHEETS // 2, 128), jnp.int32),
            pltpu.VMEM((12, SHEETS // 2, 128), F32),
            pltpu.VMEM((CHUNKS, 256, CHUNK), BF16),
            pltpu.VMEM((2, 12 * HALF_ROWS, CHUNK), BF16),
            pltpu.VMEM((6, SHEETS // 2, 128), F32),
        ],
        flops=8 << 30,
        limit=28 << 20,
    )(cols, sticks, padded, *tables)


def finish(sheet, cols, sticks, back, places):
    return call(finish_kernel, "s" + "v" * 9, shape((TEAMS, 2, LINES, EDGE)), FACTORS, flops=3 << 30)(
        sheet, cols, sticks, back, *places, *split_table(depth_table()), fold_matrix()
    )


def over_sheets(rows):
    sent = rows.reshape(SHEETS, ROWS, 2 * STICKS)
    return lax.all_to_all(sent, "pw", split_axis=0, concat_axis=0, tiled=True).reshape(rows.shape)


def body(
    orbital_coefficients,
    potential,
    line_lateral_place,
    stick_count,
    proj_atom,
    atom_pos,
    proj_radius,
    proj_diag,
    ionic_pseudo_dij,
):
    sheet = lax.axis_index("pw").astype(jnp.int32).reshape(1)
    layout = line_lateral_place[: TEAMS * SHEETS * LINES].reshape(TEAMS, SHEETS, LINES)
    cols = jnp.transpose(layout, (1, 0, 2)).reshape(SHEETS, STICKS)
    sticks = lax.all_to_all(orbital_coefficients, "tg", split_axis=0, concat_axis=0, tiled=True)
    places = make_places(sheet, stick_count, cols, proj_atom, atom_pos, proj_radius)
    by_depth = project(sticks, places, proj_atom, proj_diag, ionic_pseudo_dij)
    by_plane = over_sheets(by_depth)
    picked = plane_work(cols, by_plane, potential)
    back = over_sheets(picked)
    done = finish(sheet, cols, sticks, back, places)
    return lax.all_to_all(done, "tg", split_axis=0, concat_axis=0, tiled=True)


def solution(mesh):
    return jax.shard_map(
        body,
        mesh=mesh,
        in_specs=(
            P(None, None, ("tg", "pw"), None),
            P("pw", None),
            P(),
            P(),
            P(),
            P(),
            P(),
            P(),
            P(),
        ),
        out_specs=P(None, None, ("tg", "pw"), None),
        check_vma=False,
    )
```

```python
import math

import jax
import jax.numpy as jnp
import numpy as np
from jax import lax
from jax.experimental import pallas as pl
from jax.experimental.pallas import tpu as pltpu
from jax.sharding import PartitionSpec as P

EDGE = 192
TEAMS = 8
SHEETS = 64
DEPTH = 3
ROWS = DEPTH + 1
LINES = 8
STICKS = TEAMS * LINES
NPROJ = 2048
NATOM = 512
CUT = 48
HALF_ROWS = 48
CHUNK = 1024
CHUNKS = SHEETS * STICKS // CHUNK
PCHUNK = 256
BLOCKS = NPROJ // 128

F32 = jnp.float32
BF16 = jnp.bfloat16

NN = (((1,), (0,)), ((), ()))
NT = (((1,), (1,)), ((), ()))


def split_table(table):
    high = table.astype(np.float32).astype(jnp.bfloat16)
    low = (table - high.astype(np.float64)).astype(np.float32).astype(jnp.bfloat16)
    return high, low


def depth_table():
    steps = np.arange(EDGE)
    planes = steps.reshape(SHEETS, DEPTH).T.reshape(-1)
    turns = (planes[:, None] * steps[None, :] % EDGE) * (2.0 * math.pi / EDGE)
    return np.concatenate([np.cos(turns), np.sin(turns)], axis=0)


def fold_matrix():
    fold = np.zeros((EDGE, 256))
    for z in range(EDGE):
        g = z if z < EDGE // 2 else z - EDGE
        fold[z, abs(g)] = 1.0
        fold[z, 128 + abs(g)] = np.sign(g)
    return fold.astype(jnp.bfloat16)


def column_phase(freqs, valid):
    turns = (freqs[:, None] * np.arange(EDGE)[None, :] % EDGE) * (2.0 * math.pi / EDGE)
    keep = valid[:, None].astype(np.float64)
    return np.cos(turns) * keep, np.sin(turns) * keep


def lateral_tables():
    spot = np.arange(128)
    y_cos, y_sin = column_phase(spot - CUT, spot <= 2 * CUT)
    pad = ((0, 0), (0, 256 - EDGE))
    y_cos, y_sin = np.pad(y_cos, pad), np.pad(y_sin, pad)
    y_inverse = np.block([[y_cos, y_sin], [-y_sin, y_cos]])
    x_spot = np.where(spot < 2 * HALF_ROWS, 2 * (spot % HALF_ROWS) + spot // HALF_ROWS, spot)
    x_cos, x_sin = column_phase(x_spot - CUT, x_spot <= 2 * CUT)
    x_forward = np.block([[x_cos, x_sin], [-x_sin, x_cos]])
    return y_inverse, x_forward.T, x_forward, y_inverse.T


def split(value):
    high = value.astype(BF16)
    return high, (value - high.astype(F32)).astype(BF16)


def mul(left, right, form):
    return lax.dot_general(left, right, form, preferred_element_type=F32)


def dot3(left, right, form):
    return mul(left[0], right[0], form) + mul(left[0], right[1], form) + mul(left[1], right[0], form)


def stacked(left, right, form):
    rows = left[0].shape[0]
    both = mul(jnp.concatenate(left, axis=0), right[0], form)
    return both[:rows] + both[rows:] + mul(left[0], right[1], form)


def lateral_split(cols):
    x = (cols * 43691) >> 23
    y = cols - x * EDGE
    x = jnp.where(x < EDGE // 2, x, x - EDGE)
    y = jnp.where(y < EDGE // 2, y, y - EDGE)
    return x, y


def sincos_turns(turns):
    quarter = turns * 4.0
    near = jnp.floor(quarter + 0.5)
    x = (quarter - near) * (0.5 * math.pi)
    which = near.astype(jnp.int32) & 3
    xx = x * x
    sine = x * (1.0 + xx * (-1.0 / 6 + xx * (1.0 / 120 + xx * (-1.0 / 5040 + xx * (1.0 / 362880)))))
    cosine = 1.0 + xx * (-0.5 + xx * (1.0 / 24 + xx * (-1.0 / 720 + xx * (1.0 / 40320))))
    odd = (which & 1) == 1
    c = jnp.where(odd, sine, cosine)
    s = jnp.where(odd, cosine, sine)
    return jnp.where(((which + 1) & 2) == 2, -c, c), jnp.where((which & 2) == 2, -s, s)


def own_lateral(cols_ref, sheet):
    row = cols_ref[pl.ds(sheet, 1), :]
    x, y = lateral_split(row)
    eye = lax.broadcasted_iota(jnp.int32, (STICKS, STICKS), 0) == lax.broadcasted_iota(
        jnp.int32, (STICKS, STICKS), 1
    )

    def upright(value):
        wide = jnp.broadcast_to(value.astype(F32), (STICKS, STICKS))
        return jnp.sum(jnp.where(eye, wide, 0.0), axis=1, keepdims=True)

    return upright(x), upright(y)


def live_sticks(sticks_ref, live_ref):
    rows = []
    for part in range(2):
        for team in range(TEAMS):
            live = live_ref[team * LINES : (team + 1) * LINES, :1] > 0.5
            rows.append(jnp.where(live, sticks_ref[team, part], 0.0))
    return jnp.concatenate(rows, axis=0)


def member_of(atom_row):
    atoms = lax.broadcasted_iota(jnp.int32, (NATOM, atom_row.shape[1]), 0)
    return jnp.where(atoms == atom_row, 1.0, 0.0).astype(BF16)


def place_kernel(
    sheet_ref, counts_ref, cols_ref, atom_hbm, pos_hbm, radius_hbm,
    a_ref, place_ref, live_ref, atom_ref, pos_ref, radius_ref, sem,
):
    loads = [
        pltpu.make_async_copy(source, target, sem.at[k])
        for k, (source, target) in enumerate(
            ((atom_hbm, atom_ref), (pos_hbm, pos_ref), (radius_hbm, radius_ref))
        )
    ]
    for load in loads:
        load.start()
    for team in range(TEAMS):
        line = lax.broadcasted_iota(jnp.int32, (LINES, 128), 0)
        live = line < counts_ref[team * SHEETS + sheet_ref[0]]
        live_ref[team * LINES : (team + 1) * LINES, :] = jnp.where(live, 1.0, 0.0)
    gx, gy = own_lateral(cols_ref, sheet_ref[0])
    gxy = gx * gx + gy * gy
    for load in loads:
        load.wait()
    pos = pos_ref[...]
    first = pos.astype(BF16).astype(F32)
    second = (pos - first).astype(BF16).astype(F32)
    third = (pos - first - second).astype(BF16).astype(F32)
    line = lax.broadcasted_iota(jnp.int32, (16, NATOM), 0)
    rows = jnp.zeros((16, NATOM), F32)
    for step, piece in enumerate((first, second, third)):
        for axis in range(3):
            rows = jnp.where(line == 3 * step + axis, piece[axis : axis + 1, :], rows)
    rows = rows.astype(BF16)
    for at in range(0, NPROJ, PCHUNK):
        here = slice(at, at + PCHUNK)
        placed = mul(rows, member_of(atom_ref[:, here]), NN)
        tx, ty, tz = (
            placed[axis : axis + 1] + placed[3 + axis : 4 + axis] + placed[6 + axis : 7 + axis]
            for axis in range(3)
        )
        spread = radius_ref[:, here] / (EDGE * EDGE)
        place_ref[0:1, here] = tz
        place_ref[1:2, here] = spread
        cosine, sine = sincos_turns(gx * tx + gy * ty)
        amp = jnp.exp(-spread * gxy)
        a_ref[:STICKS, here] = amp * cosine
        a_ref[STICKS:, here] = -amp * sine


def depth_factors(place_ref, bh_ref, bl_ref):
    low_g = lax.broadcasted_iota(jnp.int32, (8, PCHUNK), 0).astype(F32)
    for at in range(0, NPROJ, PCHUNK):
        here = slice(at, at + PCHUNK)
        tz, spread = place_ref[0:1, here], place_ref[1:2, here]
        low_c, low_s = sincos_turns(low_g * tz)
        for bank in range(2):
            high_g = lax.broadcasted_iota(jnp.int32, (8, PCHUNK), 0) * 8 + bank * 64
            high_c, high_s = sincos_turns(high_g.astype(F32) * tz)
            for pair in range(4):
                re_rows, im_rows = [], []
                for inner in range(2):
                    row = pair * 2 + inner
                    hc, hs = high_c[row : row + 1], high_s[row : row + 1]
                    g = low_g + float((bank * 8 + row) * 8)
                    amp_z = jnp.exp(-spread * (g * g))
                    re_rows.append(amp_z * (hc * low_c - hs * low_s))
                    im_rows.append(-amp_z * (hs * low_c + hc * low_s))
                z = (bank * 8 + pair * 2) * 8
                for base, found in ((z, re_rows), (128 + z, im_rows)):
                    high, low = split(jnp.concatenate(found, axis=0))
                    bh_ref[base : base + 16, here] = high
                    bl_ref[base : base + 16, here] = low


def factor_kernel(place_ref, token_ref, bh_ref, bl_ref):
    del token_ref
    depth_factors(place_ref, bh_ref, bl_ref)


def rows_of(re, im):
    re_high = re.astype(BF16).astype(F32)
    im_high = im.astype(BF16).astype(F32)
    line = lax.broadcasted_iota(jnp.int32, (16, re.shape[1]), 0)
    rows = jnp.where(line == 0, re_high, 0.0)
    rows = jnp.where(line == 1, im_high, rows)
    rows = jnp.where(line == 2, re - re_high, rows)
    return jnp.where(line == 3, im - im_high, rows).astype(BF16)


def every(start):
    return pl.ds(start, SHEETS, stride=ROWS)


def project_kernel(
    sticks_ref, th_ref, tl_ref, fold_ref, atom_ref, diag_ref, dij_ref, a_ref, place_ref, live_ref,
    out_ref, bh_ref, bl_ref, becp_ref, mask_ref,
):
    depth_factors(place_ref, bh_ref, bl_ref)
    for at in range(0, NPROJ, PCHUNK):
        mask_ref[:, at : at + PCHUNK] = member_of(atom_ref[:, at : at + PCHUNK])
    coeff = split(live_sticks(sticks_ref, live_ref))
    both = dot3((th_ref[...], tl_ref[...]), coeff, NT)
    with_cos, with_sin = both[:EDGE], both[EDGE:]
    by_depth = with_cos + jnp.concatenate([-with_sin[:, STICKS:], with_sin[:, :STICKS]], axis=1)
    folded = mul(coeff[0], fold_ref[...], NN) + mul(coeff[1], fold_ref[...], NN)
    paired = split(
        jnp.concatenate(
            [
                jnp.concatenate([folded[:STICKS, :128], folded[STICKS:, 128:]], axis=1),
                jnp.concatenate([folded[STICKS:, :128], -folded[:STICKS, 128:]], axis=1),
            ],
            axis=0,
        )
    )
    for plane in range(DEPTH):
        out_ref[every(plane), :] = by_depth[plane * SHEETS : (plane + 1) * SHEETS]
    out_ref[every(DEPTH), :] = jnp.zeros((SHEETS, 128), F32)
    for at in range(0, NPROJ, PCHUNK):
        here = slice(at, at + PCHUNK)
        y = stacked(paired, (bh_ref[:, here], bl_ref[:, here]), NN)
        y_re, y_im = y[:STICKS], y[STICKS:]
        a_re, a_im = a_ref[:STICKS, here], a_ref[STICKS:, here]
        becp_ref[0:1, here] = jnp.sum(a_re * y_re + a_im * y_im, axis=0, keepdims=True)
        becp_ref[1:2, here] = jnp.sum(a_re * y_im - a_im * y_re, axis=0, keepdims=True)
    scale = 1.0 / (math.sqrt(TEAMS * SHEETS * LINES * EDGE) * math.sqrt(NPROJ))
    re, im = becp_ref[0:1, :] * scale, becp_ref[1:2, :] * scale
    dij, diag = dij_ref[...], diag_ref[...]
    per_atom = mul(rows_of(re * dij, im * dij), mask_ref[...], NT)
    common = mul(
        rows_of(per_atom[0:1] + per_atom[2:3], per_atom[1:2] + per_atom[3:4]), mask_ref[...], NN
    )
    w = (
        re * diag + dij * (common[0:1] + common[2:3]),
        im * diag + dij * (common[1:2] + common[3:4]),
    )
    for part in range(2):
        for block in range(BLOCKS):
            row = ROWS * (part * BLOCKS + block) + DEPTH
            out_ref[row : row + 1, :] = w[part][:, block * 128 : (block + 1) * 128]


def plane_kernel(
    cols_ref, sticks_ref, potential_ref,
    yih_ref, yil_ref, xih_ref, xil_ref, xfh_ref, xfl_ref, yfh_ref, yfl_ref,
    out_ref, token_ref, x_ref, v_ref, hot_ref, left_ref, pick_ref,
):
    half = SHEETS // 2
    x, y = lateral_split(jnp.concatenate([cols_ref[:half, :], cols_ref[half:, :]], axis=1))
    x, y = x + CUT, y + CUT
    x_ref[0] = x >> 1
    x_ref[1] = (x & 1) * 128 + y
    for plane in range(DEPTH):
        rows = sticks_ref[every(plane), :]
        top, bottom = rows[:half], rows[half:]
        for part in range(2):
            lanes = slice(part * STICKS, (part + 1) * STICKS)
            value = jnp.concatenate([top[:, lanes], bottom[:, lanes]], axis=1)
            high = value.astype(BF16).astype(F32)
            at = 2 * (2 * plane + part)
            v_ref[at] = high
            v_ref[at + 1] = value - high
    token_ref[...] = jnp.zeros((8, 128), F32)
    summed = jnp.sum(sticks_ref[every(DEPTH), :], axis=0, keepdims=True)
    out_ref[every(DEPTH), :] = jnp.broadcast_to(summed, (SHEETS, 128))
    row_of = lax.broadcasted_iota(jnp.int32, (HALF_ROWS, 128), 0)
    half_rows = row_of.astype(F32).astype(BF16)
    full_rows = lax.broadcasted_iota(jnp.int32, (256, 128), 0).astype(F32).astype(BF16)
    one, zero = jnp.ones((), BF16), jnp.zeros((), BF16)

    def tall(row, height):
        packed = jnp.broadcast_to(row, (16, 128)).astype(BF16)
        return jnp.concatenate([packed] * (height // 16), axis=0)

    per = CHUNK // 128
    total = jnp.zeros((12 * HALF_ROWS, 256), F32)
    for chunk in range(CHUNKS):
        slot = chunk % 2
        for inner in range(per):
            r = chunk * per + inner
            lanes = slice(inner * 128, (inner + 1) * 128)
            spot = x_ref[:, r : r + 1, :].astype(F32)
            member = jnp.where(half_rows == tall(spot[0], HALF_ROWS), one, zero)
            hot_ref[chunk, :, lanes] = jnp.where(full_rows == tall(spot[1], 256), one, zero)
            for k in range(12):
                value = tall(v_ref[k, r : r + 1, :], HALF_ROWS)
                left_ref[slot, k * HALF_ROWS : (k + 1) * HALF_ROWS, lanes] = member * value
        total = total + mul(left_ref[slot], hot_ref[chunk], NT)
    lone = x_ref[0] == HALF_ROWS
    lone_spot = (lax.broadcasted_iota(jnp.int32, (32, 128), 0) == 0) & (
        lax.broadcasted_iota(jnp.int32, (32, 128), 1) == CUT
    )

    def whole(value):
        return jnp.sum(jnp.sum(value, axis=0, keepdims=True), axis=1, keepdims=True)

    grids = []
    for plane in range(DEPTH):
        parts = []
        for part in range(2):
            at = 2 * (2 * plane + part) * HALF_ROWS
            grid = total[at : at + HALF_ROWS] + total[at + HALF_ROWS : at + 2 * HALF_ROWS]
            at = 2 * (2 * plane + part)
            extra = whole(jnp.where(lone, v_ref[at] + v_ref[at + 1], 0.0))
            extra = jnp.where(lone_spot, extra, 0.0)
            parts.append(jnp.concatenate([grid[:, :128], grid[:, 128:], extra], axis=0))
        grids.append(jnp.concatenate(parts, axis=1))
    work = jnp.concatenate(grids, axis=0)
    work = dot3(split(work), (yih_ref[...], yil_ref[...]), NN)
    work = jnp.concatenate(
        [
            jnp.concatenate(
                [work[p * 128 : (p + 1) * 128, :256], work[p * 128 : (p + 1) * 128, 256:]], axis=0
            )
            for p in range(DEPTH)
        ],
        axis=1,
    )
    work = dot3((xih_ref[...], xil_ref[...]), split(work), NN)
    local = jnp.concatenate([potential_ref[p] for p in range(DEPTH)], axis=1)
    work = jnp.concatenate([work[:EDGE] * local, work[EDGE:] * local], axis=0)
    work = dot3((xfh_ref[...], xfl_ref[...]), split(work), NN)
    work = jnp.concatenate(
        [
            jnp.concatenate(
                [work[:128, p * 256 : (p + 1) * 256], work[128:, p * 256 : (p + 1) * 256]], axis=1
            )
            for p in range(DEPTH)
        ],
        axis=0,
    )
    work = dot3(split(work), (yfh_ref[...], yfl_ref[...]), NN)
    pieces, extras = [], []
    for p in range(DEPTH):
        for c in range(2):
            block = work[p * 128 : (p + 1) * 128, c * 128 : (c + 1) * 128]
            pieces.append(
                jnp.concatenate([block[:HALF_ROWS], block[HALF_ROWS : 2 * HALF_ROWS]], axis=1)
            )
            extras.append(whole(jnp.where(lone_spot, block[2 * HALF_ROWS :], 0.0)))
    stack = jnp.concatenate(split(jnp.concatenate(pieces, axis=0)), axis=0)
    for chunk in range(CHUNKS):
        found = mul(stack, hot_ref[chunk], NN)
        found = found[: 6 * HALF_ROWS] + found[6 * HALF_ROWS :]
        for inner in range(per):
            r = chunk * per + inner
            lanes = slice(inner * 128, (inner + 1) * 128)
            member = row_of == x_ref[0, r : r + 1, :]
            for k in range(6):
                pick_ref[k, r : r + 1, :] = jnp.sum(
                    jnp.where(member, found[k * HALF_ROWS : (k + 1) * HALF_ROWS, lanes], 0.0),
                    axis=0,
                    keepdims=True,
                )
    for plane in range(DEPTH):
        re = pick_ref[2 * plane] + jnp.where(lone, extras[2 * plane], 0.0)
        im = pick_ref[2 * plane + 1] + jnp.where(lone, extras[2 * plane + 1], 0.0)
        out_ref[every(plane), :] = jnp.concatenate(
            [
                jnp.concatenate([re[:, :STICKS], im[:, :STICKS]], axis=1),
                jnp.concatenate([re[:, STICKS:], im[:, STICKS:]], axis=1),
            ],
            axis=0,
        )


def finish_kernel(
    sheet_ref, cols_ref, sticks_ref, back_ref, a_ref, live_ref, bh_ref, bl_ref, th_ref, tl_ref, fold_ref, out_ref,
):
    sheet = sheet_ref[0]
    vnl = jnp.zeros((2 * STICKS, 256), F32)
    step = 2 * PCHUNK
    for at in range(0, NPROJ, step):
        here = slice(at, at + step)
        a_re, a_im = a_ref[:STICKS, here], a_ref[STICKS:, here]
        w_re, w_im = (
            jnp.concatenate(
                [
                    back_ref[row : row + 1, :]
                    for row in range(
                        ROWS * (part * BLOCKS + at // 128) + DEPTH,
                        ROWS * (part * BLOCKS + (at + step) // 128) + DEPTH,
                        ROWS,
                    )
                ],
                axis=1,
            )
            for part in range(2)
        )
        weighted = split(
            jnp.concatenate([a_re * w_re - a_im * w_im, a_re * w_im + a_im * w_re], axis=0)
        )
        vnl = vnl + stacked(weighted, (bh_ref[:, here], bl_ref[:, here]), NT)
    vnl = split(
        jnp.concatenate(
            [
                jnp.concatenate([vnl[:STICKS, :128], -vnl[STICKS:, 128:]], axis=1),
                jnp.concatenate([vnl[STICKS:, :128], vnl[:STICKS, 128:]], axis=1),
            ],
            axis=0,
        )
    )
    vnl = mul(vnl[0], fold_ref[...], NT) + mul(vnl[1], fold_ref[...], NT)
    back = jnp.concatenate([back_ref[every(plane), :] for plane in range(DEPTH)], axis=0)
    back = split(back.T)
    with_cos = dot3(back, (th_ref[:EDGE], tl_ref[:EDGE]), NN)
    with_sin = dot3(back, (th_ref[EDGE:], tl_ref[EDGE:]), NN)
    box_scale = 1.0 / float(EDGE) ** 3
    sums = (
        (with_cos[:STICKS] + with_sin[STICKS:]) * box_scale + vnl[:STICKS],
        (with_cos[STICKS:] - with_sin[:STICKS]) * box_scale + vnl[STICKS:],
    )
    gx, gy = own_lateral(cols_ref, sheet)
    gz = lax.broadcasted_iota(jnp.int32, (1, EDGE), 1)
    gz = jnp.where(gz < EDGE // 2, gz, gz - EDGE).astype(F32)
    kinetic = 2.0 * (((gx * gx + gy * gy) + gz * gz) / (EDGE * EDGE))
    for team in range(TEAMS):
        rows = slice(team * LINES, (team + 1) * LINES)
        live = live_ref[rows, :1] > 0.5
        for part in range(2):
            value = kinetic[rows] * sticks_ref[team, part] + sums[part][rows]
            out_ref[team, part] = jnp.where(live, value, 0.0)


def call(kernel, places, outs, scratch=(), flops=0, limit=20 << 20):
    kinds = {"s": pltpu.SMEM, "v": pltpu.VMEM, "h": pltpu.HBM}
    return pl.pallas_call(
        kernel,
        out_shape=outs,
        in_specs=[pl.BlockSpec(memory_space=kinds[place]) for place in places],
        out_specs=jax.tree.map(lambda _: pl.BlockSpec(memory_space=pltpu.VMEM), outs),
        scratch_shapes=list(scratch),
        compiler_params=pltpu.CompilerParams(vmem_limit_bytes=limit),
        cost_estimate=pl.CostEstimate(flops=flops, bytes_accessed=4 << 20, transcendentals=0),
    )


def shape(dims, dtype=F32):
    return jax.ShapeDtypeStruct(dims, dtype)


def make_places(sheet, counts, cols, proj_atom, atom_pos, proj_radius):
    return call(
        place_kernel, "ssvhhh", (shape((2 * STICKS, NPROJ)), shape((2, NPROJ)), shape((STICKS, 128))),
        [
            pltpu.VMEM((1, NPROJ), jnp.int32),
            pltpu.VMEM((3, NATOM), F32),
            pltpu.VMEM((1, NPROJ), F32),
            pltpu.SemaphoreType.DMA((3,)),
        ],
        flops=2 << 30,
    )(sheet, counts, cols, proj_atom.reshape(1, NPROJ), atom_pos, proj_radius.reshape(1, NPROJ))


FACTORS = [pltpu.VMEM((256, NPROJ), BF16)] * 2


def project(sticks, places, proj_atom, proj_diag, dij):
    return call(
        project_kernel, "v" * 10, shape((SHEETS * ROWS, 2 * STICKS)),
        [*FACTORS, pltpu.VMEM((2, NPROJ), F32), pltpu.VMEM((NATOM, NPROJ), BF16)],
        flops=3 << 30,
    )(
        sticks, *split_table(depth_table()), fold_matrix(),
        proj_atom.reshape(1, NPROJ), proj_diag.reshape(1, NPROJ), dij.reshape(1, NPROJ), *places,
    )


def plane_work(cols, sticks, potential):
    tables = [piece for table in lateral_tables() for piece in split_table(table)]
    padded = jnp.pad(potential.reshape(DEPTH, EDGE, EDGE), ((0, 0), (0, 0), (0, 256 - EDGE)))
    return call(
        plane_kernel, "v" * 11, (shape((SHEETS * ROWS, 2 * STICKS)), shape((8, 128))),
        [
            pltpu.VMEM((2, SHEETS // 2, 128), jnp.int32),
            pltpu.VMEM((12, SHEETS // 2, 128), F32),
            pltpu.VMEM((CHUNKS, 256, CHUNK), BF16),
            pltpu.VMEM((2, 12 * HALF_ROWS, CHUNK), BF16),
            pltpu.VMEM((6, SHEETS // 2, 128), F32),
        ],
        flops=8 << 30,
        limit=28 << 20,
    )(cols, sticks, padded, *tables)


def make_factors(place, token):
    factor = shape((256, NPROJ), BF16)
    return call(factor_kernel, "vv", (factor, factor), flops=1 << 30)(place, token)


def finish(sheet, cols, sticks, back, a, live, factors):
    return call(finish_kernel, "s" + "v" * 10, shape((TEAMS, 2, LINES, EDGE)), flops=3 << 30)(
        sheet, cols, sticks, back, a, live, *factors, *split_table(depth_table()), fold_matrix()
    )


def over_sheets(rows):
    sent = rows.reshape(SHEETS, ROWS, 2 * STICKS)
    return lax.all_to_all(sent, "pw", split_axis=0, concat_axis=0, tiled=True).reshape(rows.shape)


def body(
    orbital_coefficients,
    potential,
    line_lateral_place,
    stick_count,
    proj_atom,
    atom_pos,
    proj_radius,
    proj_diag,
    ionic_pseudo_dij,
):
    sheet = lax.axis_index("pw").astype(jnp.int32).reshape(1)
    layout = line_lateral_place[: TEAMS * SHEETS * LINES].reshape(TEAMS, SHEETS, LINES)
    cols = jnp.transpose(layout, (1, 0, 2)).reshape(SHEETS, STICKS)
    sticks = lax.all_to_all(orbital_coefficients, "tg", split_axis=0, concat_axis=0, tiled=True)
    places = make_places(sheet, stick_count, cols, proj_atom, atom_pos, proj_radius)
    by_depth = project(sticks, places, proj_atom, proj_diag, ionic_pseudo_dij)
    by_plane = over_sheets(by_depth)
    picked, token = plane_work(cols, by_plane, potential)
    back = over_sheets(picked)
    a, place, live = places
    done = finish(sheet, cols, sticks, back, a, live, make_factors(place, token))
    return lax.all_to_all(done, "tg", split_axis=0, concat_axis=0, tiled=True)


def solution(mesh):
    return jax.shard_map(
        body,
        mesh=mesh,
        in_specs=(
            P(None, None, ("tg", "pw"), None),
            P("pw", None),
            P(),
            P(),
            P(),
            P(),
            P(),
            P(),
            P(),
        ),
        out_specs=P(None, None, ("tg", "pw"), None),
        check_vma=False,
    )
```

```python
import math

import jax
import jax.numpy as jnp
import numpy as np
from jax import lax
from jax.experimental import pallas as pl
from jax.experimental.pallas import tpu as pltpu
from jax.sharding import PartitionSpec as P

EDGE = 192
TEAMS = 8
SHEETS = 64
DEPTH = 3
ROWS = DEPTH + 1
LINES = 8
STICKS = TEAMS * LINES
NPROJ = 2048
NATOM = 512
CUT = 48
HALF_ROWS = 48
CHUNK = 1024
CHUNKS = SHEETS * STICKS // CHUNK
PCHUNK = 256
BLOCKS = NPROJ // 128

F32 = jnp.float32
BF16 = jnp.bfloat16

NN = (((1,), (0,)), ((), ()))
NT = (((1,), (1,)), ((), ()))


def split_table(table):
    high = table.astype(np.float32).astype(jnp.bfloat16)
    low = (table - high.astype(np.float64)).astype(np.float32).astype(jnp.bfloat16)
    return high, low


def depth_table():
    steps = np.arange(EDGE)
    planes = steps.reshape(SHEETS, DEPTH).T.reshape(-1)
    turns = (planes[:, None] * steps[None, :] % EDGE) * (2.0 * math.pi / EDGE)
    return np.concatenate([np.cos(turns), np.sin(turns)], axis=0)


def fold_matrix():
    fold = np.zeros((EDGE, 256))
    for z in range(EDGE):
        g = z if z < EDGE // 2 else z - EDGE
        fold[z, abs(g)] = 1.0
        fold[z, 128 + abs(g)] = np.sign(g)
    return fold.astype(jnp.bfloat16)


def column_phase(freqs, valid):
    turns = (freqs[:, None] * np.arange(EDGE)[None, :] % EDGE) * (2.0 * math.pi / EDGE)
    keep = valid[:, None].astype(np.float64)
    return np.cos(turns) * keep, np.sin(turns) * keep


def lateral_tables():
    spot = np.arange(128)
    y_cos, y_sin = column_phase(spot - CUT, spot <= 2 * CUT)
    pad = ((0, 0), (0, 256 - EDGE))
    y_cos, y_sin = np.pad(y_cos, pad), np.pad(y_sin, pad)
    y_inverse = np.block([[y_cos, y_sin], [-y_sin, y_cos]])
    x_spot = np.where(spot < 2 * HALF_ROWS, 2 * (spot % HALF_ROWS) + spot // HALF_ROWS, spot)
    x_cos, x_sin = column_phase(x_spot - CUT, x_spot <= 2 * CUT)
    x_forward = np.block([[x_cos, x_sin], [-x_sin, x_cos]])
    return y_inverse, x_forward.T, x_forward, y_inverse.T


def split(value):
    high = value.astype(BF16)
    return high, (value - high.astype(F32)).astype(BF16)


def mul(left, right, form):
    return lax.dot_general(left, right, form, preferred_element_type=F32)


def dot3(left, right, form):
    return mul(left[0], right[0], form) + mul(left[0], right[1], form) + mul(left[1], right[0], form)


def lateral_split(cols):
    x = (cols * 43691) >> 23
    y = cols - x * EDGE
    x = jnp.where(x < EDGE // 2, x, x - EDGE)
    y = jnp.where(y < EDGE // 2, y, y - EDGE)
    return x, y


def sincos_turns(turns):
    quarter = turns * 4.0
    near = jnp.floor(quarter + 0.5)
    x = (quarter - near) * (0.5 * math.pi)
    which = near.astype(jnp.int32) & 3
    xx = x * x
    sine = x * (1.0 + xx * (-1.0 / 6 + xx * (1.0 / 120 + xx * (-1.0 / 5040 + xx * (1.0 / 362880)))))
    cosine = 1.0 + xx * (-0.5 + xx * (1.0 / 24 + xx * (-1.0 / 720 + xx * (1.0 / 40320))))
    odd = (which & 1) == 1
    c = jnp.where(odd, sine, cosine)
    s = jnp.where(odd, cosine, sine)
    return jnp.where(((which + 1) & 2) == 2, -c, c), jnp.where((which & 2) == 2, -s, s)


def own_lateral(cols_ref, sheet):
    row = cols_ref[pl.ds(sheet, 1), :]
    x, y = lateral_split(row)
    eye = lax.broadcasted_iota(jnp.int32, (STICKS, STICKS), 0) == lax.broadcasted_iota(
        jnp.int32, (STICKS, STICKS), 1
    )

    def upright(value):
        wide = jnp.broadcast_to(value.astype(F32), (STICKS, STICKS))
        return jnp.sum(jnp.where(eye, wide, 0.0), axis=1, keepdims=True)

    return upright(x), upright(y)


def live_sticks(sticks_ref, live_ref):
    rows = []
    for part in range(2):
        for team in range(TEAMS):
            live = live_ref[team * LINES : (team + 1) * LINES, :1] > 0.5
            rows.append(jnp.where(live, sticks_ref[team, part], 0.0))
    return jnp.concatenate(rows, axis=0)


def member_of(atom_row):
    atoms = lax.broadcasted_iota(jnp.int32, (NATOM, atom_row.shape[1]), 0)
    return jnp.where(atoms == atom_row, 1.0, 0.0).astype(BF16)


def place_kernel(
    sheet_ref, counts_ref, cols_ref, atom_hbm, pos_hbm, radius_hbm,
    a_ref, place_ref, live_ref, atom_ref, pos_ref, radius_ref, sem,
):
    loads = [
        pltpu.make_async_copy(source, target, sem.at[k])
        for k, (source, target) in enumerate(
            ((atom_hbm, atom_ref), (pos_hbm, pos_ref), (radius_hbm, radius_ref))
        )
    ]
    for load in loads:
        load.start()
    for team in range(TEAMS):
        line = lax.broadcasted_iota(jnp.int32, (LINES, 128), 0)
        live = line < counts_ref[team * SHEETS + sheet_ref[0]]
        live_ref[team * LINES : (team + 1) * LINES, :] = jnp.where(live, 1.0, 0.0)
    gx, gy = own_lateral(cols_ref, sheet_ref[0])
    gxy = gx * gx + gy * gy
    for load in loads:
        load.wait()
    pos = pos_ref[...]
    first = pos.astype(BF16).astype(F32)
    second = (pos - first).astype(BF16).astype(F32)
    third = (pos - first - second).astype(BF16).astype(F32)
    line = lax.broadcasted_iota(jnp.int32, (16, NATOM), 0)
    rows = jnp.zeros((16, NATOM), F32)
    for step, piece in enumerate((first, second, third)):
        for axis in range(3):
            rows = jnp.where(line == 3 * step + axis, piece[axis : axis + 1, :], rows)
    rows = rows.astype(BF16)
    for at in range(0, NPROJ, PCHUNK):
        here = slice(at, at + PCHUNK)
        placed = mul(rows, member_of(atom_ref[:, here]), NN)
        tx, ty, tz = (
            placed[axis : axis + 1] + placed[3 + axis : 4 + axis] + placed[6 + axis : 7 + axis]
            for axis in range(3)
        )
        spread = radius_ref[:, here] / (EDGE * EDGE)
        place_ref[0:1, here] = tz
        place_ref[1:2, here] = spread
        cosine, sine = sincos_turns(gx * tx + gy * ty)
        amp = jnp.exp(-spread * gxy)
        a_ref[:STICKS, here] = amp * cosine
        a_ref[STICKS:, here] = -amp * sine


def depth_factors(place_ref, bh_ref, bl_ref):
    low_g = lax.broadcasted_iota(jnp.int32, (8, PCHUNK), 0).astype(F32)
    for factor_ref in (bh_ref, bl_ref):
        for z in (112, 240):
            factor_ref[z : z + 16, :] = jnp.zeros((16, NPROJ), BF16)
    for at in range(0, NPROJ, PCHUNK):
        here = slice(at, at + PCHUNK)
        tz, spread = place_ref[0:1, here], place_ref[1:2, here]
        low_c, low_s = sincos_turns(low_g * tz)
        for bank in range(2):
            high_g = lax.broadcasted_iota(jnp.int32, (8, PCHUNK), 0) * 8 + bank * 64
            high_c, high_s = sincos_turns(high_g.astype(F32) * tz)
            for pair in range(4 - bank):
                re_rows, im_rows = [], []
                for inner in range(2):
                    row = pair * 2 + inner
                    hc, hs = high_c[row : row + 1], high_s[row : row + 1]
                    g = low_g + float((bank * 8 + row) * 8)
                    amp_z = jnp.exp(-spread * (g * g))
                    re_rows.append(amp_z * (hc * low_c - hs * low_s))
                    im_rows.append(-amp_z * (hs * low_c + hc * low_s))
                z = (bank * 8 + pair * 2) * 8
                for base, found in ((z, re_rows), (128 + z, im_rows)):
                    high, low = split(jnp.concatenate(found, axis=0))
                    bh_ref[base : base + 16, here] = high
                    bl_ref[base : base + 16, here] = low


def rows_of(re, im):
    re_high = re.astype(BF16).astype(F32)
    im_high = im.astype(BF16).astype(F32)
    line = lax.broadcasted_iota(jnp.int32, (16, re.shape[1]), 0)
    rows = jnp.where(line == 0, re_high, 0.0)
    rows = jnp.where(line == 1, im_high, rows)
    rows = jnp.where(line == 2, re - re_high, rows)
    return jnp.where(line == 3, im - im_high, rows).astype(BF16)


def every(start):
    return pl.ds(start, SHEETS, stride=ROWS)


def project_kernel(
    sticks_ref, th_ref, tl_ref, fold_ref, atom_ref, diag_ref, dij_ref, a_ref, place_ref, live_ref,
    out_ref, bh_ref, bl_ref, becp_ref, mask_ref,
):
    depth_factors(place_ref, bh_ref, bl_ref)
    for at in range(0, NPROJ, PCHUNK):
        mask_ref[:, at : at + PCHUNK] = member_of(atom_ref[:, at : at + PCHUNK])
    coeff = split(live_sticks(sticks_ref, live_ref))
    both = dot3((th_ref[...], tl_ref[...]), coeff, NT)
    with_cos, with_sin = both[:EDGE], both[EDGE:]
    by_depth = with_cos + jnp.concatenate([-with_sin[:, STICKS:], with_sin[:, :STICKS]], axis=1)
    folded = mul(coeff[0], fold_ref[...], NN) + mul(coeff[1], fold_ref[...], NN)
    paired = split(
        jnp.concatenate(
            [
                jnp.concatenate([folded[:STICKS, :128], folded[STICKS:, 128:]], axis=1),
                jnp.concatenate([folded[STICKS:, :128], -folded[:STICKS, 128:]], axis=1),
            ],
            axis=0,
        )
    )
    for plane in range(DEPTH):
        out_ref[every(plane), :] = by_depth[plane * SHEETS : (plane + 1) * SHEETS]
    out_ref[every(DEPTH), :] = jnp.zeros((SHEETS, 128), F32)
    for at in range(0, NPROJ, PCHUNK):
        here = slice(at, at + PCHUNK)
        y = dot3(paired, (bh_ref[:, here], bl_ref[:, here]), NN)
        y_re, y_im = y[:STICKS], y[STICKS:]
        a_re, a_im = a_ref[:STICKS, here], a_ref[STICKS:, here]
        becp_ref[0:1, here] = jnp.sum(a_re * y_re + a_im * y_im, axis=0, keepdims=True)
        becp_ref[1:2, here] = jnp.sum(a_re * y_im - a_im * y_re, axis=0, keepdims=True)
    scale = 1.0 / (math.sqrt(TEAMS * SHEETS * LINES * EDGE) * math.sqrt(NPROJ))
    re, im = becp_ref[0:1, :] * scale, becp_ref[1:2, :] * scale
    dij, diag = dij_ref[...], diag_ref[...]
    per_atom = mul(rows_of(re * dij, im * dij), mask_ref[...], NT)
    common = mul(
        rows_of(per_atom[0:1] + per_atom[2:3], per_atom[1:2] + per_atom[3:4]), mask_ref[...], NN
    )
    w = (
        re * diag + dij * (common[0:1] + common[2:3]),
        im * diag + dij * (common[1:2] + common[3:4]),
    )
    for part in range(2):
        for block in range(BLOCKS):
            row = ROWS * (part * BLOCKS + block) + DEPTH
            out_ref[row : row + 1, :] = w[part][:, block * 128 : (block + 1) * 128]


def plane_kernel(
    cols_ref, sticks_ref, potential_ref,
    yih_ref, yil_ref, xih_ref, xil_ref, xfh_ref, xfl_ref, yfh_ref, yfl_ref,
    out_ref, x_ref, v_ref, hot_ref, left_ref, pick_ref,
):
    half = SHEETS // 2
    x, y = lateral_split(jnp.concatenate([cols_ref[:half, :], cols_ref[half:, :]], axis=1))
    x, y = x + CUT, y + CUT
    x_ref[0] = x >> 1
    x_ref[1] = (x & 1) * 128 + y
    for plane in range(DEPTH):
        rows = sticks_ref[every(plane), :]
        top, bottom = rows[:half], rows[half:]
        for part in range(2):
            lanes = slice(part * STICKS, (part + 1) * STICKS)
            value = jnp.concatenate([top[:, lanes], bottom[:, lanes]], axis=1)
            high = value.astype(BF16).astype(F32)
            at = 2 * (2 * plane + part)
            v_ref[at] = high
            v_ref[at + 1] = value - high
    summed = jnp.sum(sticks_ref[every(DEPTH), :], axis=0, keepdims=True)
    out_ref[every(DEPTH), :] = jnp.broadcast_to(summed, (SHEETS, 128))
    row_of = lax.broadcasted_iota(jnp.int32, (HALF_ROWS, 128), 0)
    half_rows = row_of.astype(F32).astype(BF16)
    full_rows = lax.broadcasted_iota(jnp.int32, (256, 128), 0).astype(F32).astype(BF16)
    one, zero = jnp.ones((), BF16), jnp.zeros((), BF16)

    def tall(row, height):
        packed = jnp.broadcast_to(row, (16, 128)).astype(BF16)
        return jnp.concatenate([packed] * (height // 16), axis=0)

    per = CHUNK // 128
    total = jnp.zeros((12 * HALF_ROWS, 256), F32)
    for chunk in range(CHUNKS):
        slot = chunk % 2
        for inner in range(per):
            r = chunk * per + inner
            lanes = slice(inner * 128, (inner + 1) * 128)
            spot = x_ref[:, r : r + 1, :].astype(F32)
            member = jnp.where(half_rows == tall(spot[0], HALF_ROWS), one, zero)
            hot_ref[chunk, :, lanes] = jnp.where(full_rows == tall(spot[1], 256), one, zero)
            for k in range(12):
                value = tall(v_ref[k, r : r + 1, :], HALF_ROWS)
                left_ref[slot, k * HALF_ROWS : (k + 1) * HALF_ROWS, lanes] = member * value
        total = total + mul(left_ref[slot], hot_ref[chunk], NT)
    lone = x_ref[0] == HALF_ROWS
    lone_spot = (lax.broadcasted_iota(jnp.int32, (32, 128), 0) == 0) & (
        lax.broadcasted_iota(jnp.int32, (32, 128), 1) == CUT
    )

    def whole(value):
        return jnp.sum(jnp.sum(value, axis=0, keepdims=True), axis=1, keepdims=True)

    grids = []
    for plane in range(DEPTH):
        parts = []
        for part in range(2):
            at = 2 * (2 * plane + part) * HALF_ROWS
            grid = total[at : at + HALF_ROWS] + total[at + HALF_ROWS : at + 2 * HALF_ROWS]
            at = 2 * (2 * plane + part)
            extra = whole(jnp.where(lone, v_ref[at] + v_ref[at + 1], 0.0))
            extra = jnp.where(lone_spot, extra, 0.0)
            parts.append(jnp.concatenate([grid[:, :128], grid[:, 128:], extra], axis=0))
        grids.append(jnp.concatenate(parts, axis=1))
    work = jnp.concatenate(grids, axis=0)
    work = dot3(split(work), (yih_ref[...], yil_ref[...]), NN)
    x_inverse, x_forward = (xih_ref[...], xil_ref[...]), (xfh_ref[...], xfl_ref[...])
    fields = []
    for p in range(DEPTH):
        rows = slice(p * 128, (p + 1) * 128)
        field = jnp.concatenate([work[rows, :256], work[rows, 256:]], axis=0)
        fields.append(dot3(x_inverse, split(field), NN))
    grids = []
    for p in range(DEPTH):
        local = potential_ref[p]
        field = jnp.concatenate([fields[p][:EDGE] * local, fields[p][EDGE:] * local], axis=0)
        grid = dot3(x_forward, split(field), NN)
        grids.append(jnp.concatenate([grid[:128], grid[128:]], axis=1))
    work = jnp.concatenate(grids, axis=0)
    work = dot3(split(work), (yfh_ref[...], yfl_ref[...]), NN)
    pieces, extras = [], []
    for p in range(DEPTH):
        for c in range(2):
            block = work[p * 128 : (p + 1) * 128, c * 128 : (c + 1) * 128]
            pieces.append(
                jnp.concatenate([block[:HALF_ROWS], block[HALF_ROWS : 2 * HALF_ROWS]], axis=1)
            )
            extras.append(whole(jnp.where(lone_spot, block[2 * HALF_ROWS :], 0.0)))
    high, low = split(jnp.concatenate(pieces, axis=0))
    for chunk in range(CHUNKS):
        hot = hot_ref[chunk]
        found = mul(high, hot, NN) + mul(low, hot, NN)
        for inner in range(per):
            r = chunk * per + inner
            lanes = slice(inner * 128, (inner + 1) * 128)
            member = row_of == x_ref[0, r : r + 1, :]
            for k in range(6):
                pick_ref[k, r : r + 1, :] = jnp.sum(
                    jnp.where(member, found[k * HALF_ROWS : (k + 1) * HALF_ROWS, lanes], 0.0),
                    axis=0,
                    keepdims=True,
                )
    for plane in range(DEPTH):
        re = pick_ref[2 * plane] + jnp.where(lone, extras[2 * plane], 0.0)
        im = pick_ref[2 * plane + 1] + jnp.where(lone, extras[2 * plane + 1], 0.0)
        out_ref[every(plane), :] = jnp.concatenate(
            [
                jnp.concatenate([re[:, :STICKS], im[:, :STICKS]], axis=1),
                jnp.concatenate([re[:, STICKS:], im[:, STICKS:]], axis=1),
            ],
            axis=0,
        )


def finish_kernel(
    sheet_ref, cols_ref, sticks_ref, back_ref, a_ref, place_ref, live_ref, th_ref, tl_ref, fold_ref,
    out_ref, bh_ref, bl_ref,
):
    sheet = sheet_ref[0]
    depth_factors(place_ref, bh_ref, bl_ref)
    vnl = jnp.zeros((2 * STICKS, 256), F32)
    step = 2 * PCHUNK
    for at in range(0, NPROJ, step):
        here = slice(at, at + step)
        a_re, a_im = a_ref[:STICKS, here], a_ref[STICKS:, here]
        w_re, w_im = (
            jnp.concatenate(
                [
                    back_ref[row : row + 1, :]
                    for row in range(
                        ROWS * (part * BLOCKS + at // 128) + DEPTH,
                        ROWS * (part * BLOCKS + (at + step) // 128) + DEPTH,
                        ROWS,
                    )
                ],
                axis=1,
            )
            for part in range(2)
        )
        weighted = split(
            jnp.concatenate([a_re * w_re - a_im * w_im, a_re * w_im + a_im * w_re], axis=0)
        )
        vnl = vnl + dot3(weighted, (bh_ref[:, here], bl_ref[:, here]), NT)
    vnl = split(
        jnp.concatenate(
            [
                jnp.concatenate([vnl[:STICKS, :128], -vnl[STICKS:, 128:]], axis=1),
                jnp.concatenate([vnl[STICKS:, :128], vnl[:STICKS, 128:]], axis=1),
            ],
            axis=0,
        )
    )
    vnl = mul(vnl[0], fold_ref[...], NT) + mul(vnl[1], fold_ref[...], NT)
    back = jnp.concatenate([back_ref[every(plane), :] for plane in range(DEPTH)], axis=0)
    back = split(back.T)
    with_cos = dot3(back, (th_ref[:EDGE], tl_ref[:EDGE]), NN)
    with_sin = dot3(back, (th_ref[EDGE:], tl_ref[EDGE:]), NN)
    box_scale = 1.0 / float(EDGE) ** 3
    sums = (
        (with_cos[:STICKS] + with_sin[STICKS:]) * box_scale + vnl[:STICKS],
        (with_cos[STICKS:] - with_sin[:STICKS]) * box_scale + vnl[STICKS:],
    )
    gx, gy = own_lateral(cols_ref, sheet)
    gz = lax.broadcasted_iota(jnp.int32, (1, EDGE), 1)
    gz = jnp.where(gz < EDGE // 2, gz, gz - EDGE).astype(F32)
    kinetic = 2.0 * (((gx * gx + gy * gy) + gz * gz) / (EDGE * EDGE))
    for team in range(TEAMS):
        rows = slice(team * LINES, (team + 1) * LINES)
        live = live_ref[rows, :1] > 0.5
        for part in range(2):
            value = kinetic[rows] * sticks_ref[team, part] + sums[part][rows]
            out_ref[team, part] = jnp.where(live, value, 0.0)


def call(kernel, places, outs, scratch=(), flops=0, limit=20 << 20):
    kinds = {"s": pltpu.SMEM, "v": pltpu.VMEM, "h": pltpu.HBM}
    return pl.pallas_call(
        kernel,
        out_shape=outs,
        in_specs=[pl.BlockSpec(memory_space=kinds[place]) for place in places],
        out_specs=jax.tree.map(lambda _: pl.BlockSpec(memory_space=pltpu.VMEM), outs),
        scratch_shapes=list(scratch),
        compiler_params=pltpu.CompilerParams(vmem_limit_bytes=limit),
        cost_estimate=pl.CostEstimate(flops=flops, bytes_accessed=4 << 20, transcendentals=0),
    )


def shape(dims, dtype=F32):
    return jax.ShapeDtypeStruct(dims, dtype)


def make_places(sheet, counts, cols, proj_atom, atom_pos, proj_radius):
    return call(
        place_kernel, "ssvhhh", (shape((2 * STICKS, NPROJ)), shape((2, NPROJ)), shape((STICKS, 128))),
        [
            pltpu.VMEM((1, NPROJ), jnp.int32),
            pltpu.VMEM((3, NATOM), F32),
            pltpu.VMEM((1, NPROJ), F32),
            pltpu.SemaphoreType.DMA((3,)),
        ],
        flops=2 << 30,
    )(sheet, counts, cols, proj_atom.reshape(1, NPROJ), atom_pos, proj_radius.reshape(1, NPROJ))


FACTORS = [pltpu.VMEM((256, NPROJ), BF16)] * 2


def project(sticks, places, proj_atom, proj_diag, dij):
    return call(
        project_kernel, "v" * 10, shape((SHEETS * ROWS, 2 * STICKS)),
        [*FACTORS, pltpu.VMEM((2, NPROJ), F32), pltpu.VMEM((NATOM, NPROJ), BF16)],
        flops=3 << 30,
    )(
        sticks, *split_table(depth_table()), fold_matrix(),
        proj_atom.reshape(1, NPROJ), proj_diag.reshape(1, NPROJ), dij.reshape(1, NPROJ), *places,
    )


def plane_work(cols, sticks, potential):
    tables = [piece for table in lateral_tables() for piece in split_table(table)]
    padded = jnp.pad(potential.reshape(DEPTH, EDGE, EDGE), ((0, 0), (0, 0), (0, 256 - EDGE)))
    return call(
        plane_kernel, "v" * 11, shape((SHEETS * ROWS, 2 * STICKS)),
        [
            pltpu.VMEM((2, SHEETS // 2, 128), jnp.int32),
            pltpu.VMEM((12, SHEETS // 2, 128), F32),
            pltpu.VMEM((CHUNKS, 256, CHUNK), BF16),
            pltpu.VMEM((2, 12 * HALF_ROWS, CHUNK), BF16),
            pltpu.VMEM((6, SHEETS // 2, 128), F32),
        ],
        flops=8 << 30,
        limit=28 << 20,
    )(cols, sticks, padded, *tables)


def finish(sheet, cols, sticks, back, places):
    return call(finish_kernel, "s" + "v" * 9, shape((TEAMS, 2, LINES, EDGE)), FACTORS, flops=3 << 30)(
        sheet, cols, sticks, back, *places, *split_table(depth_table()), fold_matrix()
    )


def over_sheets(rows):
    sent = rows.reshape(SHEETS, ROWS, 2 * STICKS)
    return lax.all_to_all(sent, "pw", split_axis=0, concat_axis=0, tiled=True).reshape(rows.shape)


def body(
    orbital_coefficients,
    potential,
    line_lateral_place,
    stick_count,
    proj_atom,
    atom_pos,
    proj_radius,
    proj_diag,
    ionic_pseudo_dij,
):
    sheet = lax.axis_index("pw").astype(jnp.int32).reshape(1)
    layout = line_lateral_place[: TEAMS * SHEETS * LINES].reshape(TEAMS, SHEETS, LINES)
    cols = jnp.transpose(layout, (1, 0, 2)).reshape(SHEETS, STICKS)
    sticks = lax.all_to_all(orbital_coefficients, "tg", split_axis=0, concat_axis=0, tiled=True)
    places = make_places(sheet, stick_count, cols, proj_atom, atom_pos, proj_radius)
    by_depth = project(sticks, places, proj_atom, proj_diag, ionic_pseudo_dij)
    by_plane = over_sheets(by_depth)
    picked = plane_work(cols, by_plane, potential)
    back = over_sheets(picked)
    done = finish(sheet, cols, sticks, back, places)
    return lax.all_to_all(done, "tg", split_axis=0, concat_axis=0, tiled=True)


def solution(mesh):
    return jax.shard_map(
        body,
        mesh=mesh,
        in_specs=(
            P(None, None, ("tg", "pw"), None),
            P("pw", None),
            P(),
            P(),
            P(),
            P(),
            P(),
            P(),
            P(),
        ),
        out_specs=P(None, None, ("tg", "pw"), None),
        check_vma=False,
    )
```

```python
import math

import jax
import jax.numpy as jnp
import numpy as np
from jax import lax
from jax.experimental import pallas as pl
from jax.experimental.pallas import tpu as pltpu
from jax.sharding import PartitionSpec as P

EDGE = 192
TEAMS = 8
SHEETS = 64
DEPTH = 3
ROWS = DEPTH + 1
LINES = 8
STICKS = TEAMS * LINES
NPROJ = 2048
NATOM = 512
CUT = 48
PACK = 32
CENTERS = (48, 142, 223)
CHUNK = 1024
CHUNKS = SHEETS * STICKS // CHUNK
PCHUNK = 256
BLOCKS = NPROJ // 128

F32 = jnp.float32
BF16 = jnp.bfloat16

NN = (((1,), (0,)), ((), ()))
NT = (((1,), (1,)), ((), ()))


def split_table(table):
    high = table.astype(np.float32).astype(jnp.bfloat16)
    low = (table - high.astype(np.float64)).astype(np.float32).astype(jnp.bfloat16)
    return high, low


def depth_table():
    steps = np.arange(EDGE)
    planes = steps.reshape(SHEETS, DEPTH).T.reshape(-1)
    turns = (planes[:, None] * steps[None, :] % EDGE) * (2.0 * math.pi / EDGE)
    return np.concatenate([np.cos(turns), np.sin(turns)], axis=0)


def fold_matrix():
    fold = np.zeros((EDGE, 256))
    for z in range(EDGE):
        g = z if z < EDGE // 2 else z - EDGE
        fold[z, abs(g)] = 1.0
        fold[z, 128 + abs(g)] = np.sign(g)
    return fold.astype(jnp.bfloat16)


def column_phase(freqs, valid):
    turns = (freqs[:, None] * np.arange(EDGE)[None, :] % EDGE) * (2.0 * math.pi / EDGE)
    keep = valid[:, None].astype(np.float64)
    return np.cos(turns) * keep, np.sin(turns) * keep


def packed_x(band, row):
    inner = row % 16
    size = 16 * band + (15 - inner if band == 2 else inner)
    return -size - 1 if row >= 16 else size


def lateral_tables():
    spot = np.arange(128)
    y_cos, y_sin = column_phase(spot - CUT, spot <= 2 * CUT)
    pad = ((0, 0), (0, 256 - EDGE))
    y_cos, y_sin = np.pad(y_cos, pad), np.pad(y_sin, pad)
    y_inverse = np.block([[y_cos, y_sin], [-y_sin, y_cos]])
    x_freq = np.array([packed_x(band, row) for band in range(3) for row in range(PACK)] + [CUT] * 32)
    x_cos, x_sin = column_phase(x_freq, spot <= 3 * PACK)
    x_forward = np.block([[x_cos, x_sin], [-x_sin, x_cos]])
    return y_inverse, x_forward.T, x_forward, y_inverse.T


def split(value):
    high = value.astype(BF16)
    return high, (value - high.astype(F32)).astype(BF16)


def mul(left, right, form):
    return lax.dot_general(left, right, form, preferred_element_type=F32)


def dot3(left, right, form):
    return mul(left[0], right[0], form) + mul(left[0], right[1], form) + mul(left[1], right[0], form)


def lateral_split(cols):
    x = (cols * 43691) >> 23
    y = cols - x * EDGE
    x = jnp.where(x < EDGE // 2, x, x - EDGE)
    y = jnp.where(y < EDGE // 2, y, y - EDGE)
    return x, y


def sincos_turns(turns):
    quarter = turns * 4.0
    near = jnp.floor(quarter + 0.5)
    x = (quarter - near) * (0.5 * math.pi)
    which = near.astype(jnp.int32) & 3
    xx = x * x
    sine = x * (1.0 + xx * (-1.0 / 6 + xx * (1.0 / 120 + xx * (-1.0 / 5040 + xx * (1.0 / 362880)))))
    cosine = 1.0 + xx * (-0.5 + xx * (1.0 / 24 + xx * (-1.0 / 720 + xx * (1.0 / 40320))))
    odd = (which & 1) == 1
    c = jnp.where(odd, sine, cosine)
    s = jnp.where(odd, cosine, sine)
    return jnp.where(((which + 1) & 2) == 2, -c, c), jnp.where((which & 2) == 2, -s, s)


def own_lateral(cols_ref, sheet):
    row = cols_ref[pl.ds(sheet, 1), :]
    x, y = lateral_split(row)
    eye = lax.broadcasted_iota(jnp.int32, (STICKS, STICKS), 0) == lax.broadcasted_iota(
        jnp.int32, (STICKS, STICKS), 1
    )

    def upright(value):
        wide = jnp.broadcast_to(value.astype(F32), (STICKS, STICKS))
        return jnp.sum(jnp.where(eye, wide, 0.0), axis=1, keepdims=True)

    return upright(x), upright(y)


def live_sticks(sticks_ref, live_ref):
    rows = []
    for part in range(2):
        for team in range(TEAMS):
            live = live_ref[team * LINES : (team + 1) * LINES, :1] > 0.5
            rows.append(jnp.where(live, sticks_ref[team, part], 0.0))
    return jnp.concatenate(rows, axis=0)


def member_of(atom_row):
    atoms = lax.broadcasted_iota(jnp.int32, (NATOM, atom_row.shape[1]), 0)
    return jnp.where(atoms == atom_row, 1.0, 0.0).astype(BF16)


def place_kernel(
    sheet_ref, counts_ref, cols_ref, atom_hbm, pos_hbm, radius_hbm,
    a_ref, place_ref, live_ref, atom_ref, pos_ref, radius_ref, sem,
):
    loads = [
        pltpu.make_async_copy(source, target, sem.at[k])
        for k, (source, target) in enumerate(
            ((atom_hbm, atom_ref), (pos_hbm, pos_ref), (radius_hbm, radius_ref))
        )
    ]
    for load in loads:
        load.start()
    for team in range(TEAMS):
        line = lax.broadcasted_iota(jnp.int32, (LINES, 128), 0)
        live = line < counts_ref[team * SHEETS + sheet_ref[0]]
        live_ref[team * LINES : (team + 1) * LINES, :] = jnp.where(live, 1.0, 0.0)
    gx, gy = own_lateral(cols_ref, sheet_ref[0])
    gxy = gx * gx + gy * gy
    for load in loads:
        load.wait()
    pos = pos_ref[...]
    first = pos.astype(BF16).astype(F32)
    second = (pos - first).astype(BF16).astype(F32)
    third = (pos - first - second).astype(BF16).astype(F32)
    line = lax.broadcasted_iota(jnp.int32, (16, NATOM), 0)
    rows = jnp.zeros((16, NATOM), F32)
    for step, piece in enumerate((first, second, third)):
        for axis in range(3):
            rows = jnp.where(line == 3 * step + axis, piece[axis : axis + 1, :], rows)
    rows = rows.astype(BF16)
    for at in range(0, NPROJ, PCHUNK):
        here = slice(at, at + PCHUNK)
        placed = mul(rows, member_of(atom_ref[:, here]), NN)
        tx, ty, tz = (
            placed[axis : axis + 1] + placed[3 + axis : 4 + axis] + placed[6 + axis : 7 + axis]
            for axis in range(3)
        )
        spread = radius_ref[:, here] / (EDGE * EDGE)
        place_ref[0:1, here] = tz
        place_ref[1:2, here] = spread
        cosine, sine = sincos_turns(gx * tx + gy * ty)
        amp = jnp.exp(-spread * gxy)
        a_ref[:STICKS, here] = amp * cosine
        a_ref[STICKS:, here] = -amp * sine


def depth_factors(place_ref, bh_ref, bl_ref):
    low_g = lax.broadcasted_iota(jnp.int32, (8, PCHUNK), 0).astype(F32)
    for factor_ref in (bh_ref, bl_ref):
        for z in (112, 240):
            factor_ref[z : z + 16, :] = jnp.zeros((16, NPROJ), BF16)
    for at in range(0, NPROJ, PCHUNK):
        here = slice(at, at + PCHUNK)
        tz, spread = place_ref[0:1, here], place_ref[1:2, here]
        low_c, low_s = sincos_turns(low_g * tz)
        for bank in range(2):
            high_g = lax.broadcasted_iota(jnp.int32, (8, PCHUNK), 0) * 8 + bank * 64
            high_c, high_s = sincos_turns(high_g.astype(F32) * tz)
            for pair in range(4 - bank):
                re_rows, im_rows = [], []
                for inner in range(2):
                    row = pair * 2 + inner
                    hc, hs = high_c[row : row + 1], high_s[row : row + 1]
                    g = low_g + float((bank * 8 + row) * 8)
                    amp_z = jnp.exp(-spread * (g * g))
                    re_rows.append(amp_z * (hc * low_c - hs * low_s))
                    im_rows.append(-amp_z * (hs * low_c + hc * low_s))
                z = (bank * 8 + pair * 2) * 8
                for base, found in ((z, re_rows), (128 + z, im_rows)):
                    high, low = split(jnp.concatenate(found, axis=0))
                    bh_ref[base : base + 16, here] = high
                    bl_ref[base : base + 16, here] = low


def rows_of(re, im):
    re_high = re.astype(BF16).astype(F32)
    im_high = im.astype(BF16).astype(F32)
    line = lax.broadcasted_iota(jnp.int32, (16, re.shape[1]), 0)
    rows = jnp.where(line == 0, re_high, 0.0)
    rows = jnp.where(line == 1, im_high, rows)
    rows = jnp.where(line == 2, re - re_high, rows)
    return jnp.where(line == 3, im - im_high, rows).astype(BF16)


def every(start):
    return pl.ds(start, SHEETS, stride=ROWS)


def project_kernel(
    sticks_ref, th_ref, tl_ref, fold_ref, atom_ref, diag_ref, dij_ref, a_ref, place_ref, live_ref,
    out_ref, bh_ref, bl_ref, becp_ref, mask_ref,
):
    depth_factors(place_ref, bh_ref, bl_ref)
    for at in range(0, NPROJ, PCHUNK):
        mask_ref[:, at : at + PCHUNK] = member_of(atom_ref[:, at : at + PCHUNK])
    coeff = split(live_sticks(sticks_ref, live_ref))
    both = dot3((th_ref[...], tl_ref[...]), coeff, NT)
    with_cos, with_sin = both[:EDGE], both[EDGE:]
    by_depth = with_cos + jnp.concatenate([-with_sin[:, STICKS:], with_sin[:, :STICKS]], axis=1)
    folded = mul(coeff[0], fold_ref[...], NN) + mul(coeff[1], fold_ref[...], NN)
    paired = split(
        jnp.concatenate(
            [
                jnp.concatenate([folded[:STICKS, :128], folded[STICKS:, 128:]], axis=1),
                jnp.concatenate([folded[STICKS:, :128], -folded[:STICKS, 128:]], axis=1),
            ],
            axis=0,
        )
    )
    for plane in range(DEPTH):
        out_ref[every(plane), :] = by_depth[plane * SHEETS : (plane + 1) * SHEETS]
    out_ref[every(DEPTH), :] = jnp.zeros((SHEETS, 128), F32)
    for at in range(0, NPROJ, PCHUNK):
        here = slice(at, at + PCHUNK)
        y = dot3(paired, (bh_ref[:, here], bl_ref[:, here]), NN)
        y_re, y_im = y[:STICKS], y[STICKS:]
        a_re, a_im = a_ref[:STICKS, here], a_ref[STICKS:, here]
        becp_ref[0:1, here] = jnp.sum(a_re * y_re + a_im * y_im, axis=0, keepdims=True)
        becp_ref[1:2, here] = jnp.sum(a_re * y_im - a_im * y_re, axis=0, keepdims=True)
    scale = 1.0 / (math.sqrt(TEAMS * SHEETS * LINES * EDGE) * math.sqrt(NPROJ))
    re, im = becp_ref[0:1, :] * scale, becp_ref[1:2, :] * scale
    dij, diag = dij_ref[...], diag_ref[...]
    per_atom = mul(rows_of(re * dij, im * dij), mask_ref[...], NT)
    common = mul(
        rows_of(per_atom[0:1] + per_atom[2:3], per_atom[1:2] + per_atom[3:4]), mask_ref[...], NN
    )
    w = (
        re * diag + dij * (common[0:1] + common[2:3]),
        im * diag + dij * (common[1:2] + common[3:4]),
    )
    for part in range(2):
        for block in range(BLOCKS):
            row = ROWS * (part * BLOCKS + block) + DEPTH
            out_ref[row : row + 1, :] = w[part][:, block * 128 : (block + 1) * 128]


def plane_kernel(
    cols_ref, sticks_ref, potential_ref,
    yih_ref, yil_ref, xih_ref, xil_ref, xfh_ref, xfl_ref, yfh_ref, yfl_ref,
    out_ref, x_ref, v_ref, hot_ref, left_ref, pick_ref,
):
    half = SHEETS // 2
    x, y = lateral_split(jnp.concatenate([cols_ref[:half, :], cols_ref[half:, :]], axis=1))
    size = jnp.where(x >= 0, x, -x - 1)
    band = size >> 4
    row = jnp.where(band == 2, 15 - (size & 15), size & 15) + jnp.where(x < 0, 16, 0)
    lane = y + jnp.where(band == 0, CENTERS[0], jnp.where(band == 1, CENTERS[1], CENTERS[2]))
    x_ref[0] = jnp.where(band > 2, PACK, row)
    x_ref[1] = jnp.where(lane >= 256, lane - 256, lane)
    for plane in range(DEPTH):
        rows = sticks_ref[every(plane), :]
        top, bottom = rows[:half], rows[half:]
        for part in range(2):
            lanes = slice(part * STICKS, (part + 1) * STICKS)
            value = jnp.concatenate([top[:, lanes], bottom[:, lanes]], axis=1)
            high = value.astype(BF16).astype(F32)
            at = 2 * (2 * plane + part)
            v_ref[at] = high
            v_ref[at + 1] = value - high
    summed = jnp.sum(sticks_ref[every(DEPTH), :], axis=0, keepdims=True)
    out_ref[every(DEPTH), :] = jnp.broadcast_to(summed, (SHEETS, 128))
    row_of = lax.broadcasted_iota(jnp.int32, (PACK, 128), 0)
    half_rows = row_of.astype(F32).astype(BF16)
    full_rows = lax.broadcasted_iota(jnp.int32, (256, 128), 0).astype(F32).astype(BF16)
    one, zero = jnp.ones((), BF16), jnp.zeros((), BF16)

    def tall(row, height):
        packed = jnp.broadcast_to(row, (16, 128)).astype(BF16)
        return jnp.concatenate([packed] * (height // 16), axis=0)

    per = CHUNK // 128
    total = jnp.zeros((12 * PACK, 256), F32)
    for chunk in range(CHUNKS):
        slot = chunk % 2
        for inner in range(per):
            r = chunk * per + inner
            lanes = slice(inner * 128, (inner + 1) * 128)
            spot = x_ref[:, r : r + 1, :].astype(F32)
            member = jnp.where(half_rows == tall(spot[0], PACK), one, zero)
            hot_ref[chunk, :, lanes] = jnp.where(full_rows == tall(spot[1], 256), one, zero)
            for k in range(12):
                value = tall(v_ref[k, r : r + 1, :], PACK)
                left_ref[slot, k * PACK : (k + 1) * PACK, lanes] = member * value
        total = total + mul(left_ref[slot], hot_ref[chunk], NT)
    lone = x_ref[0] == PACK
    lone_spot = (lax.broadcasted_iota(jnp.int32, (32, 128), 0) == 0) & (
        lax.broadcasted_iota(jnp.int32, (32, 128), 1) == CUT
    )

    def whole(value):
        return jnp.sum(jnp.sum(value, axis=0, keepdims=True), axis=1, keepdims=True)

    held = []
    row = lax.broadcasted_iota(jnp.int32, (PACK, 128), 0)
    y = lax.broadcasted_iota(jnp.int32, (PACK, 128), 1) - CUT
    for band in range(3):
        size = 16 * band + jnp.where(band == 2, 15 - (row & 15), row & 15)
        x = jnp.where(row >= 16, -size - 1, size)
        held.append(x * x + y * y <= CUT * CUT)

    def turned(grid, shift):
        return grid if shift == 0 else pltpu.roll(grid, shift, 1)

    grids = []
    for plane in range(DEPTH):
        parts = []
        for part in range(2):
            at = 2 * (2 * plane + part) * PACK
            grid = total[at : at + PACK] + total[at + PACK : at + 2 * PACK]
            at = 2 * (2 * plane + part)
            extra = whole(jnp.where(lone, v_ref[at] + v_ref[at + 1], 0.0))
            extra = jnp.where(lone_spot, extra, 0.0)
            bands = [
                jnp.where(held[band], turned(grid, (256 + CUT - CENTERS[band]) % 256)[:, :128], 0.0)
                for band in range(3)
            ]
            parts.append(jnp.concatenate([*bands, extra], axis=0))
        grids.append(jnp.concatenate(parts, axis=1))
    work = jnp.concatenate(grids, axis=0)
    work = dot3(split(work), (yih_ref[...], yil_ref[...]), NN)
    x_inverse, x_forward = (xih_ref[...], xil_ref[...]), (xfh_ref[...], xfl_ref[...])
    fields = []
    for p in range(DEPTH):
        rows = slice(p * 128, (p + 1) * 128)
        field = jnp.concatenate([work[rows, :256], work[rows, 256:]], axis=0)
        fields.append(dot3(x_inverse, split(field), NN))
    grids = []
    for p in range(DEPTH):
        local = potential_ref[p]
        field = jnp.concatenate([fields[p][:EDGE] * local, fields[p][EDGE:] * local], axis=0)
        grid = dot3(x_forward, split(field), NN)
        grids.append(jnp.concatenate([grid[:128], grid[128:]], axis=1))
    work = jnp.concatenate(grids, axis=0)
    work = dot3(split(work), (yfh_ref[...], yfl_ref[...]), NN)
    pieces, extras = [], []
    for p in range(DEPTH):
        for c in range(2):
            block = work[p * 128 : (p + 1) * 128, c * 128 : (c + 1) * 128]
            packed = jnp.zeros((PACK, 256), F32)
            for band in range(3):
                rows = jnp.where(held[band], block[band * PACK : (band + 1) * PACK], 0.0)
                wide = jnp.concatenate([rows, jnp.zeros((PACK, 128), F32)], axis=1)
                packed = packed + turned(wide, CENTERS[band] - CUT)
            pieces.append(packed)
            extras.append(whole(jnp.where(lone_spot, block[3 * PACK :], 0.0)))
    stack = jnp.concatenate(split(jnp.concatenate(pieces, axis=0)), axis=0)
    for chunk in range(CHUNKS):
        found = mul(stack, hot_ref[chunk], NN)
        found = found[: 6 * PACK] + found[6 * PACK :]
        for inner in range(per):
            r = chunk * per + inner
            lanes = slice(inner * 128, (inner + 1) * 128)
            member = row_of == x_ref[0, r : r + 1, :]
            for k in range(6):
                pick_ref[k, r : r + 1, :] = jnp.sum(
                    jnp.where(member, found[k * PACK : (k + 1) * PACK, lanes], 0.0),
                    axis=0,
                    keepdims=True,
                )
    for plane in range(DEPTH):
        re = pick_ref[2 * plane] + jnp.where(lone, extras[2 * plane], 0.0)
        im = pick_ref[2 * plane + 1] + jnp.where(lone, extras[2 * plane + 1], 0.0)
        out_ref[every(plane), :] = jnp.concatenate(
            [
                jnp.concatenate([re[:, :STICKS], im[:, :STICKS]], axis=1),
                jnp.concatenate([re[:, STICKS:], im[:, STICKS:]], axis=1),
            ],
            axis=0,
        )


def finish_kernel(
    sheet_ref, cols_ref, sticks_ref, back_ref, a_ref, place_ref, live_ref, th_ref, tl_ref, fold_ref,
    out_ref, bh_ref, bl_ref,
):
    sheet = sheet_ref[0]
    depth_factors(place_ref, bh_ref, bl_ref)
    vnl = jnp.zeros((2 * STICKS, 256), F32)
    step = 2 * PCHUNK
    for at in range(0, NPROJ, step):
        here = slice(at, at + step)
        a_re, a_im = a_ref[:STICKS, here], a_ref[STICKS:, here]
        w_re, w_im = (
            jnp.concatenate(
                [
                    back_ref[row : row + 1, :]
                    for row in range(
                        ROWS * (part * BLOCKS + at // 128) + DEPTH,
                        ROWS * (part * BLOCKS + (at + step) // 128) + DEPTH,
                        ROWS,
                    )
                ],
                axis=1,
            )
            for part in range(2)
        )
        weighted = split(
            jnp.concatenate([a_re * w_re - a_im * w_im, a_re * w_im + a_im * w_re], axis=0)
        )
        vnl = vnl + dot3(weighted, (bh_ref[:, here], bl_ref[:, here]), NT)
    vnl = split(
        jnp.concatenate(
            [
                jnp.concatenate([vnl[:STICKS, :128], -vnl[STICKS:, 128:]], axis=1),
                jnp.concatenate([vnl[STICKS:, :128], vnl[:STICKS, 128:]], axis=1),
            ],
            axis=0,
        )
    )
    vnl = mul(vnl[0], fold_ref[...], NT) + mul(vnl[1], fold_ref[...], NT)
    back = jnp.concatenate([back_ref[every(plane), :] for plane in range(DEPTH)], axis=0)
    back = split(back.T)
    with_cos = dot3(back, (th_ref[:EDGE], tl_ref[:EDGE]), NN)
    with_sin = dot3(back, (th_ref[EDGE:], tl_ref[EDGE:]), NN)
    box_scale = 1.0 / float(EDGE) ** 3
    sums = (
        (with_cos[:STICKS] + with_sin[STICKS:]) * box_scale + vnl[:STICKS],
        (with_cos[STICKS:] - with_sin[:STICKS]) * box_scale + vnl[STICKS:],
    )
    gx, gy = own_lateral(cols_ref, sheet)
    gz = lax.broadcasted_iota(jnp.int32, (1, EDGE), 1)
    gz = jnp.where(gz < EDGE // 2, gz, gz - EDGE).astype(F32)
    kinetic = 2.0 * (((gx * gx + gy * gy) + gz * gz) / (EDGE * EDGE))
    for team in range(TEAMS):
        rows = slice(team * LINES, (team + 1) * LINES)
        live = live_ref[rows, :1] > 0.5
        for part in range(2):
            value = kinetic[rows] * sticks_ref[team, part] + sums[part][rows]
            out_ref[team, part] = jnp.where(live, value, 0.0)


def call(kernel, places, outs, scratch=(), flops=0, limit=20 << 20):
    kinds = {"s": pltpu.SMEM, "v": pltpu.VMEM, "h": pltpu.HBM}
    return pl.pallas_call(
        kernel,
        out_shape=outs,
        in_specs=[pl.BlockSpec(memory_space=kinds[place]) for place in places],
        out_specs=jax.tree.map(lambda _: pl.BlockSpec(memory_space=pltpu.VMEM), outs),
        scratch_shapes=list(scratch),
        compiler_params=pltpu.CompilerParams(vmem_limit_bytes=limit),
        cost_estimate=pl.CostEstimate(flops=flops, bytes_accessed=4 << 20, transcendentals=0),
    )


def shape(dims, dtype=F32):
    return jax.ShapeDtypeStruct(dims, dtype)


def make_places(sheet, counts, cols, proj_atom, atom_pos, proj_radius):
    return call(
        place_kernel, "ssvhhh", (shape((2 * STICKS, NPROJ)), shape((2, NPROJ)), shape((STICKS, 128))),
        [
            pltpu.VMEM((1, NPROJ), jnp.int32),
            pltpu.VMEM((3, NATOM), F32),
            pltpu.VMEM((1, NPROJ), F32),
            pltpu.SemaphoreType.DMA((3,)),
        ],
        flops=2 << 30,
    )(sheet, counts, cols, proj_atom.reshape(1, NPROJ), atom_pos, proj_radius.reshape(1, NPROJ))


FACTORS = [pltpu.VMEM((256, NPROJ), BF16)] * 2


def project(sticks, places, proj_atom, proj_diag, dij):
    return call(
        project_kernel, "v" * 10, shape((SHEETS * ROWS, 2 * STICKS)),
        [*FACTORS, pltpu.VMEM((2, NPROJ), F32), pltpu.VMEM((NATOM, NPROJ), BF16)],
        flops=3 << 30,
    )(
        sticks, *split_table(depth_table()), fold_matrix(),
        proj_atom.reshape(1, NPROJ), proj_diag.reshape(1, NPROJ), dij.reshape(1, NPROJ), *places,
    )


def plane_work(cols, sticks, potential):
    tables = [piece for table in lateral_tables() for piece in split_table(table)]
    padded = jnp.pad(potential.reshape(DEPTH, EDGE, EDGE), ((0, 0), (0, 0), (0, 256 - EDGE)))
    return call(
        plane_kernel, "v" * 11, shape((SHEETS * ROWS, 2 * STICKS)),
        [
            pltpu.VMEM((2, SHEETS // 2, 128), jnp.int32),
            pltpu.VMEM((12, SHEETS // 2, 128), F32),
            pltpu.VMEM((CHUNKS, 256, CHUNK), BF16),
            pltpu.VMEM((2, 12 * PACK, CHUNK), BF16),
            pltpu.VMEM((6, SHEETS // 2, 128), F32),
        ],
        flops=8 << 30,
        limit=28 << 20,
    )(cols, sticks, padded, *tables)


def finish(sheet, cols, sticks, back, places):
    return call(finish_kernel, "s" + "v" * 9, shape((TEAMS, 2, LINES, EDGE)), FACTORS, flops=3 << 30)(
        sheet, cols, sticks, back, *places, *split_table(depth_table()), fold_matrix()
    )


def over_sheets(rows):
    sent = rows.reshape(SHEETS, ROWS, 2 * STICKS)
    return lax.all_to_all(sent, "pw", split_axis=0, concat_axis=0, tiled=True).reshape(rows.shape)


def body(
    orbital_coefficients,
    potential,
    line_lateral_place,
    stick_count,
    proj_atom,
    atom_pos,
    proj_radius,
    proj_diag,
    ionic_pseudo_dij,
):
    sheet = lax.axis_index("pw").astype(jnp.int32).reshape(1)
    layout = line_lateral_place[: TEAMS * SHEETS * LINES].reshape(TEAMS, SHEETS, LINES)
    cols = jnp.transpose(layout, (1, 0, 2)).reshape(SHEETS, STICKS)
    sticks = lax.all_to_all(orbital_coefficients, "tg", split_axis=0, concat_axis=0, tiled=True)
    places = make_places(sheet, stick_count, cols, proj_atom, atom_pos, proj_radius)
    by_depth = project(sticks, places, proj_atom, proj_diag, ionic_pseudo_dij)
    by_plane = over_sheets(by_depth)
    picked = plane_work(cols, by_plane, potential)
    back = over_sheets(picked)
    done = finish(sheet, cols, sticks, back, places)
    return lax.all_to_all(done, "tg", split_axis=0, concat_axis=0, tiled=True)


def solution(mesh):
    return jax.shard_map(
        body,
        mesh=mesh,
        in_specs=(
            P(None, None, ("tg", "pw"), None),
            P("pw", None),
            P(),
            P(),
            P(),
            P(),
            P(),
            P(),
            P(),
        ),
        out_specs=P(None, None, ("tg", "pw"), None),
        check_vma=False,
    )
```
